512 devices in a mesh: blk: 128 (over x, y_lo, z), rep: 4 (over y_hi, core).
Axes of the slice: x: 4, y: 8 (y_hi: 2, y_lo: 4; y = y_hi * 4 + y_lo), z: 8, core: 2. Of those that a mesh axis runs over, the one named last changes fastest.
Arguments:
- positions: float32 [3, 262144], P(None, ('blk', 'rep')), may hold values from -6 to 6
- normal_flow: float32 [3, 262144], P(None, ('blk', 'rep')), may hold values from -6 to 6
- send_owner: int32 [262144], P(('blk', 'rep')), may hold values from 0 to 127, as said below
- send_slot: int32 [262144], P(('blk', 'rep')), may hold values from 0 to 9, as said below
- recv_index: int32 [655360], P(('blk', 'rep')), may hold values from -1 to 1279, as said below
- loop_pos: int32 [655360], P(('blk', 'rep')), may hold values from 0 to 1279, as said below
- loop_len: int32 [655360], P(('blk', 'rep')), may hold values from 1 to 1280, as said below
Outputs:
- velocity: float32 [3, 262144], P(None, ('blk', 'rep'))
The draws below stay inside these ranges and needn't reach their ends.
Inputs may be any that keep to these rules, and one draw needn't show every extreme that they name: `send_slot`: A filament's points all lie on devices with one rep index, and its owner device has that rep index. No two points of one device share an owner and slot; at most 10 points go from one device to one owner, and some pair reaches it. `send_owner`: owner blk indices. `recv_index`: for each owner device, entry b * 10 + s is the owner-local column of the point arriving from the device of blk index b in slot s, or -1 where no point arrives; every point has its entry and no column is named twice. One owner holds up to 1280 points, and some owner holds that many. `loop_pos`: the owner-local points of one filament are consecutive columns of one device in filament order; unused columns have order 0. Some filament has 1280 points. `loop_len`: every filament has 16 or more points and at most 1280, a count reached by some filament; unused owner-local columns have 1.
All inputs are finite; a program needn't handle non-finite values.
Results may differ from the reference program's by a relative error of at most 0.0003.
Values sent between devices are 32-bit elements; how exact they have to be, the bound alone decides.
A program may use at most 64 MiB of HBM per device.

```python
import jax
import jax.numpy as jnp
from jax import lax

PT_DEV = 512
STOPS = 8
POINTS = 262144
CAP = 10
OWN_CAP = 1280
N_BLK = 128
N_REP = 4
DEVICES = 512


def filament_row(row_key):
    row_points = N_BLK * PT_DEV
    pattern = jnp.tile(jnp.array([1, 2, 3, 10], jnp.int32), N_BLK // 4)
    loads = PT_DEV * jax.random.permutation(jax.random.fold_in(row_key, 1), pattern) // 4
    span_end = jnp.cumsum(loads).astype(jnp.int32)
    span_start = span_end - loads
    canonical = jnp.arange(row_points, dtype=jnp.int32)
    owner_of = jnp.searchsorted(span_end, canonical, side='right').astype(jnp.int32)
    local_index = canonical - span_start[owner_of]
    unit_count = row_points // 16
    unit_index = jnp.arange(unit_count, dtype=jnp.int32)
    biggest_owner = jnp.argmax(loads).astype(jnp.int32)
    random_cut = (jax.random.randint(jax.random.fold_in(row_key, 2), (unit_count,), 0, 4) == 0) & (owner_of[::16] != biggest_owner)
    cut_here = random_cut | (local_index[::16] == 0)
    first_unit = lax.cummax(jnp.where(cut_here, unit_index, 0))
    next_cut = lax.cummin(jnp.where(cut_here, unit_index, unit_count), reverse=True)
    next_unit = jnp.concatenate([next_cut[1:], jnp.array([unit_count], jnp.int32)])
    point_unit = canonical // 16
    position_in_loop = canonical - 16 * first_unit[point_unit]
    loop_length = 16 * (next_unit[point_unit] - first_unit[point_unit])
    scramble = jax.random.permutation(jax.random.fold_in(row_key, 3), row_points).astype(jnp.int32)
    order = jnp.argsort(owner_of * row_points + scramble, stable=True).astype(jnp.int32)
    rank = jnp.zeros((row_points,), jnp.int32).at[order].set(canonical)
    holder = canonical % N_BLK
    first_sent = span_start[owner_of] + jnp.remainder(holder - span_start[owner_of], N_BLK)
    send_place = (canonical - first_sent) // N_BLK
    owner_rows = owner_of.reshape(PT_DEV, N_BLK).T
    place_rows = send_place.reshape(PT_DEV, N_BLK).T
    receive = jnp.full((N_BLK, N_BLK, CAP), -1, jnp.int32).at[owner_of, holder, send_place].set(rank - span_start[owner_of])
    column = jnp.arange(OWN_CAP, dtype=jnp.int32)
    canonical_at = jnp.clip(span_start[:, None] + column[None, :], 0, row_points - 1)
    is_used = column[None, :] < loads[:, None]
    loop_place = jnp.where(is_used, position_in_loop[canonical_at], 0)
    loop_size = jnp.where(is_used, loop_length[canonical_at], 1)
    return (owner_rows, place_rows, receive, loop_place, loop_size)


def filament_routes(key):
    row_data = [filament_row(jax.random.fold_in(key, 100 + row_index)) for row_index in range(N_REP)]
    return tuple((jnp.swapaxes(jnp.stack([entry[member] for entry in row_data]), 0, 1).reshape(-1).astype(jnp.int32) for member in range(5)))


def draw_send_owner(key, part):
    return filament_routes(key)[0]


def draw_send_slot(key, part):
    return filament_routes(key)[1]


def draw_recv_index(key, part):
    return filament_routes(key)[2]


def draw_loop_pos(key, part):
    return filament_routes(key)[3]


def draw_loop_len(key, part):
    return filament_routes(key)[4]


def level_of(rng, extent, pieces, low, top_value):
    level, own = 1.0, jax.random.fold_in(rng, 6)
    for axis_at, parts in pieces:
        heights = jnp.exp(jax.random.uniform(jax.random.fold_in(own, axis_at), (parts,), jnp.float32, low / len(pieces), top_value / len(pieces)))
        level = level * jnp.repeat(heights, extent[axis_at] // parts).reshape([-1 if axis == axis_at else 1 for axis in range(len(extent))])
    return level


def noise(rng, shape, scale, reach, cuts=(), held_as=jnp.bfloat16):
    result = scale * jax.random.normal(rng, shape, jnp.float32)
    if cuts:
        result = result * level_of(rng, shape, cuts, -0.22, 0.18)
    return jnp.clip(result, -reach, reach).astype(held_as)


def setup_inputs(seed: int = 0) -> dict:
    seeds = jax.random.split(jax.random.key(seed), 8)
    positions = noise(seeds[0], (3, POINTS), 1.0, 6.0, ((1, 512),), jnp.float32)
    normal_flow = noise(seeds[1], (3, POINTS), 1.0, 6.0, ((1, 512),), jnp.float32)
    send_owner = draw_send_owner(jax.random.fold_in(seeds[7], 71), 0)
    send_slot = draw_send_slot(jax.random.fold_in(seeds[7], 71), 0)
    recv_index = draw_recv_index(jax.random.fold_in(seeds[7], 71), 0)
    loop_pos = draw_loop_pos(jax.random.fold_in(seeds[7], 71), 0)
    loop_len = draw_loop_len(jax.random.fold_in(seeds[7], 71), 0)
    return {"positions": positions, "normal_flow": normal_flow, "send_owner": send_owner, "send_slot": send_slot, "recv_index": recv_index, "loop_pos": loop_pos, "loop_len": loop_len}


LOCAL_BETA = 0.3
FRICTION_ALPHA = 0.21
FRICTION_PRIME = 0.06
BIOT_SCALE = 0.01
CORE_SQUARED = 0.25
SPEED_FLOOR = 1.0

def cross_product(left, right):
    return jnp.stack([left[1] * right[2] - left[2] * right[1], left[2] * right[0] - left[0] * right[2], left[0] * right[1] - left[1] * right[0]])

def induced(targets, sources, tangents):
    total_targets = targets.shape[1]
    block_width = min(256, total_targets)
    blocks = targets.reshape(3, total_targets // block_width, block_width).transpose(1, 0, 2)

    def one_block(target_block):
        separation = target_block[:, :, None] - sources[:, None, :]
        radius_sq = lax.optimization_barrier(jnp.sum(separation * separation, axis=0)) + CORE_SQUARED
        weight = 1.0 / (radius_sq * jnp.sqrt(radius_sq))
        turned = cross_product(tangents[:, None, :], separation)
        return lax.optimization_barrier(jnp.sum(turned * weight[None], axis=2))
    return lax.map(one_block, blocks).transpose(1, 0, 2).reshape(3, total_targets)

def along_loops(owned, loop_pos, loop_len):
    point_index = jnp.arange(owned.shape[1], dtype=jnp.int32)
    loop_start = point_index - loop_pos

    def neighbour(offset):
        return jnp.take(owned, loop_start + jnp.remainder(loop_pos + offset, loop_len), axis=1)
    plus_one, minus_one = (neighbour(1), neighbour(-1))
    plus_two, minus_two = (neighbour(2), neighbour(-2))
    first_derivative = (8.0 * (plus_one - minus_one) - (plus_two - minus_two)) / 12.0
    second_derivative = (16.0 * (plus_one + minus_one) - (plus_two + minus_two) - 30.0 * owned) / 12.0
    return (first_derivative, second_derivative)

def reference(positions, normal_flow, send_owner, send_slot, recv_index, loop_pos, loop_len):
    holder = jnp.arange(POINTS, dtype=jnp.int32) // PT_DEV
    holder_column = holder // N_REP
    holder_row = holder % N_REP
    owner_device = send_owner * N_REP + holder_row
    arrival = owner_device * (N_BLK * CAP) + holder_column * CAP + send_slot
    owner_index = owner_device * OWN_CAP + recv_index[arrival]
    owned = jnp.zeros((3, DEVICES * OWN_CAP), jnp.float32).at[:, owner_index].set(positions)
    first_derivative, second_derivative = along_loops(owned, loop_pos, loop_len)
    tangent = first_derivative[:, owner_index]
    curvature = second_derivative[:, owner_index]
    speed_squared = jnp.maximum(lax.optimization_barrier(jnp.sum(tangent * tangent, axis=0)), SPEED_FLOOR)
    local_term = LOCAL_BETA * cross_product(tangent, curvature) / (speed_squared * jnp.sqrt(speed_squared))
    group_size = N_REP * PT_DEV
    grouped_positions = positions.reshape(3, N_BLK, group_size).transpose(1, 0, 2)
    grouped_tangents = tangent.reshape(3, N_BLK, group_size).transpose(1, 0, 2)

    def per_group(group_index):
        targets = grouped_positions[group_index]
        far_total = jnp.zeros((3, group_size), jnp.float32)
        for offset in range(-(STOPS // 2 - 1), STOPS // 2 + 1):
            source_index = jnp.remainder(group_index + offset, N_BLK)
            far_total = far_total + induced(targets, grouped_positions[source_index], grouped_tangents[source_index])
        return far_total
    far_sum = lax.map(per_group, jnp.arange(N_BLK, dtype=jnp.int32))
    far_field = BIOT_SCALE * far_sum.transpose(1, 0, 2).reshape(3, POINTS)
    superfluid = local_term + far_field
    unit_tangent = tangent / jnp.sqrt(speed_squared)
    slip_velocity = normal_flow - superfluid
    first_turn = cross_product(unit_tangent, slip_velocity)
    return superfluid + FRICTION_ALPHA * first_turn - FRICTION_PRIME * cross_product(unit_tangent, first_turn)
```

```python
import functools

import jax
import jax.numpy as jnp
from jax import lax
from jax.experimental import pallas as pl
from jax.experimental.pallas import tpu as pltpu
from jax.sharding import PartitionSpec as P

LOCAL_BETA = 0.3
FRICTION_ALPHA = 0.21
FRICTION_PRIME = 0.06
BIOT_SCALE = 0.01
CORE_SQUARED = 0.25
SPEED_FLOOR = 1.0

BLOCKS = 128
LINE = 8
PLANES = BLOCKS // LINE
REPS = 4
STOPS = 8
BACK = STOPS // 2 - 1
SOURCES = STOPS * REPS
PT = 512
CAP = 10
LANES = 128
SLOT_ROWS = 8
COLUMN_ROWS = 10

MESH = pl.DeviceIdType.MESH
F32 = jnp.float32
BF16 = jnp.bfloat16
I32 = jnp.int32

NT = (((1,), (1,)), ((), ()))
NN = (((1,), (0,)), ((), ()))


def dot(left, right, dims=NN):
    return lax.dot_general(left, right, dims, preferred_element_type=F32)


def rounded(value):
    return value.astype(BF16).astype(F32)


def split(value):
    high = rounded(value)
    rest = value - high
    mid = rounded(rest)
    return high, mid, rest - mid


def iota(shape, dim):
    return lax.broadcasted_iota(I32, shape, dim)


def pick(table, index):
    return jnp.take_along_axis(table, index, axis=1, mode="promise_in_bounds")


def look_up(table, index):
    row, lane = index >> 7, index & 127
    found = jnp.zeros(index.shape, table.dtype)
    for t in range(COLUMN_ROWS):
        piece = jnp.broadcast_to(table[t : t + 1], index.shape)
        found = jnp.where(row == t, pick(piece, lane), found)
    return found


def stop_of(step):
    odd = step % 2
    return odd * ((step + 1) // 2) - (1 - odd) * (step // 2)


def kernel(
    pos_ref, flow_ref, owner_ref, slot_ref, recv_ref, order_ref, count_ref, out_ref,
    out1, in1, turned1, arrived, out2, in2, turned2, returned,
    src_pos, src_tan, target, w_high, w_low, total, index_a, index_b, member,
    send_sem, sem1, sem2, sem3, sem4, pos_sem, tan_sem,
):
    me = lax.axis_index("blk")
    rep = lax.axis_index("rep")
    plane = me // LINE
    place = me % LINE
    mine = BACK * REPS + rep

    def on_line(k):
        return (place + k) % LINE

    def on_plane(k):
        return (plane + k) % PLANES

    def source(step):
        stop = stop_of(step // REPS)
        other = (rep + step % REPS) % REPS
        return stop, other

    barrier = pltpu.get_barrier_semaphore()

    def greet(blk, other):
        pl.semaphore_signal(barrier, inc=1, device_id=(blk, other), device_id_type=MESH)

    for k in range(1, LINE):
        greet(plane * LINE + on_line(k), rep)
    for k in range(1, PLANES):
        greet(on_plane(k) * LINE + place, rep)

    def greet_source(step, carry):
        stop, other = source(step)
        greet((me + stop + BLOCKS) % BLOCKS, other)
        return carry

    lax.fori_loop(1, SOURCES, greet_source, 0)

    pos = pos_ref[...]
    square = jnp.sum(pos * pos, axis=0, keepdims=True)
    src_pos[mine] = jnp.concatenate([pos, square], axis=0)

    owner = owner_ref[...]
    slot = slot_ref[...]
    owner_row = (owner & (LINE - 1)) * PLANES + (owner >> 3)
    is_owner = jnp.where(iota((BLOCKS, PT), 0) == owner_row, 1.0, 0.0).astype(BF16)
    member[...] = is_owner
    pos_twice = jnp.concatenate([pos, pos, jnp.zeros((2, PT), F32)], axis=0)
    slotted = jnp.concatenate(
        [jnp.where(slot == s, pos_twice, 0.0) for s in range(CAP)]
        + [jnp.zeros((LANES - CAP * SLOT_ROWS, PT), F32)],
        axis=0,
    )
    outgoing = sum(dot(is_owner, part.astype(BF16), NT) for part in split(slotted))
    out1[...] = outgoing.reshape(LINE, PLANES, LANES)

    ones = jnp.ones((1, PT), F32)
    none = jnp.zeros((3, PT), F32)
    wanted = jnp.concatenate([-2.0 * pos, ones, square + CORE_SQUARED, none], axis=0)
    th, tm, tl = split(wanted)
    features = jnp.concatenate(
        [th, th, tm, tm, th, tl, tl, tm, jnp.zeros((LANES - 64, PT), F32)], axis=0
    )
    target[...] = features.T.astype(BF16)
    one_row = jnp.concatenate([ones, none], axis=0)
    no_rows = jnp.zeros((LANES - 64, PT), F32)

    def weigh(n):
        sh, sm, sl = split(jnp.concatenate([src_pos[n], one_row], axis=0))
        rows = jnp.concatenate([sh, sm, sh, sm, sl, sh, sm, sl, no_rows], axis=0).astype(BF16)
        for half in range(PT // 256):
            columns = slice(half * 256, half * 256 + 256)
            root = lax.rsqrt(dot(target[...], rows[:, columns]))
            weight = root * root * root
            high = weight.astype(BF16)
            w_high[n, :, columns] = high
            w_low[n, :, columns] = (weight - high.astype(F32)).astype(BF16)

    def block_copy(ref, sem, send, step):
        stop, other = source(step)
        return pltpu.make_async_remote_copy(
            src_ref=ref.at[mine],
            dst_ref=ref.at[(stop + BACK) * REPS + rep],
            send_sem=send,
            recv_sem=sem.at[(stop + BACK) * REPS + rep],
            device_id=((me - stop + BLOCKS) % BLOCKS, other),
            device_id_type=MESH,
        )

    def arriving(ref, sem, send, step):
        stop, other = source(step)
        n = (stop + BACK) * REPS + other
        pltpu.make_async_remote_copy(
            src_ref=ref.at[n],
            dst_ref=ref.at[n],
            send_sem=send,
            recv_sem=sem.at[n],
            device_id=(me, rep),
            device_id_type=MESH,
        ).wait_recv()
        return n

    def send_blocks(ref, sem, send, low, top):
        def one(step, carry):
            block_copy(ref, sem, send, step).start()
            return carry

        lax.fori_loop(low, top, one, 0)

    def weigh_steps(low, top):
        def one(step, carry):
            weigh(arriving(src_pos, pos_sem, send_sem.at[4], step))
            return carry

        lax.fori_loop(low, top, one, 0)

    def line_copy(src, dst, sem, send, k):
        there = on_line(k)
        return pltpu.make_async_remote_copy(
            src_ref=src.at[there],
            dst_ref=dst.at[place],
            send_sem=send,
            recv_sem=sem.at[place],
            device_id=(plane * LINE + there, rep),
            device_id_type=MESH,
        )

    def plane_copy(src, dst, sem, send, k):
        there = on_plane(k)
        return pltpu.make_async_remote_copy(
            src_ref=src.at[there],
            dst_ref=dst.at[plane],
            send_sem=send,
            recv_sem=sem.at[plane],
            device_id=(there * LINE + place, rep),
            device_id_type=MESH,
        )

    def await_piece(dst, sem, send, n):
        pltpu.make_async_remote_copy(
            src_ref=dst.at[n],
            dst_ref=dst.at[n],
            send_sem=send,
            recv_sem=sem.at[n],
            device_id=(me, rep),
            device_id_type=MESH,
        ).wait_recv()

    def await_sent(ref, count, send):
        pltpu.make_async_remote_copy(
            src_ref=ref.at[pl.ds(0, count)],
            dst_ref=ref.at[pl.ds(0, count)],
            send_sem=send,
            recv_sem=sem1.at[0],
            device_id=(me, rep),
            device_id_type=MESH,
        ).wait_send()

    pl.semaphore_wait(barrier, (LINE - 1) + (PLANES - 1) + (SOURCES - 1))

    for k in range(1, LINE):
        line_copy(out1, in1, sem1, send_sem.at[0], k).start()
    in1[place] = out1[place]
    send_blocks(src_pos, pos_sem, send_sem.at[4], 1, 8)

    spot = iota((16, LANES), 1) * CAP + iota((16, LANES), 0)
    column = jnp.where(iota((16, LANES), 0) < CAP, look_up(recv_ref[...], spot), -1)
    column_row, column_lane = column >> 7, column & 127
    holder = iota((16, LANES), 1).astype(F32)
    inverse = jnp.zeros((32, LANES), F32)
    for s in range(CAP):
        hit = column_row[s : s + 1] == iota((16, LANES), 0)
        left = jnp.concatenate(
            [jnp.where(hit, holder, 0.0), jnp.where(hit, float(s), 0.0)], axis=0
        ).astype(BF16)
        right = jnp.where(column_lane[s : s + 1] == iota((LANES, LANES), 0), 1.0, 0.0).astype(BF16)
        inverse = inverse + dot(left, right, NT)
    inverse = (inverse[16:] * float(LANES) + inverse[:16]).astype(I32)
    at = jnp.maximum(column, 0)
    order = look_up(order_ref[...], at)
    count = look_up(count_ref[...], at)

    def neighbour(offset):
        moved = order + offset
        moved = jnp.where(moved < 0, moved + count, jnp.where(moved >= count, moved - count, moved))
        there = jnp.clip(at - order + moved, 0, COLUMN_ROWS * LANES - 1)
        return look_up(inverse, there)

    ahead1, ahead2, behind1, behind2 = (neighbour(k) for k in (1, 2, -1, -2))
    near = iota((SLOT_ROWS, LANES), 0) < 3
    for s in range(CAP):
        index_a[s] = jnp.where(near, ahead1[s : s + 1], ahead2[s : s + 1])
        index_b[s] = jnp.where(near, behind1[s : s + 1], behind2[s : s + 1])

    for k in range(1, LINE):
        await_piece(in1, sem1, send_sem.at[0], on_line(k))
    for j in range(PLANES):
        turned1[j] = in1[:, j, :]
    for k in range(1, PLANES):
        plane_copy(turned1, arrived, sem2, send_sem.at[1], k).start()
    arrived[plane] = turned1[plane]
    send_blocks(src_pos, pos_sem, send_sem.at[4], 8, 20)
    weigh(mine)
    weigh_steps(1, 4)

    for k in range(1, PLANES):
        await_piece(arrived, sem2, send_sem.at[1], on_plane(k))
    tables = arrived[...].reshape(BLOCKS, LANES).T
    middle = iota((SLOT_ROWS, LANES), 0) < 6
    results = []
    for s in range(CAP):
        to_a, to_b = index_a[s], index_b[s]
        row_a, row_b, lane_a, lane_b = to_a >> 7, to_b >> 7, to_a & 127, to_b & 127
        after = jnp.zeros((SLOT_ROWS, LANES), F32)
        before = jnp.zeros((SLOT_ROWS, LANES), F32)
        for t in range(CAP):
            table = tables[t * SLOT_ROWS : (t + 1) * SLOT_ROWS]
            after = jnp.where(row_a == t, pick(table, lane_a), after)
            before = jnp.where(row_b == t, pick(table, lane_b), before)
        here = tables[s * SLOT_ROWS : (s + 1) * SLOT_ROWS]
        gap, both = after - before, after + before
        first = 8.0 * gap - pltpu.roll(gap, SLOT_ROWS - 3, 0)
        second = 16.0 * pltpu.roll(both, 3, 0) - both - 30.0 * here
        results.append(jnp.where(near, first, jnp.where(middle, second, 0.0)) / 12.0)
    results.append(jnp.zeros((LANES - CAP * SLOT_ROWS, LANES), F32))
    out2[...] = jnp.concatenate(results, axis=0).T.reshape(PLANES, LINE, LANES)

    for k in range(1, PLANES):
        plane_copy(out2, in2, sem3, send_sem.at[2], k).start()
    in2[plane] = out2[plane]
    send_blocks(src_pos, pos_sem, send_sem.at[4], 20, SOURCES)
    weigh_steps(4, 8)

    for k in range(1, PLANES):
        await_piece(in2, sem3, send_sem.at[2], on_plane(k))
    for j in range(LINE):
        turned2[j] = in2[:, j, :]
    for k in range(1, LINE):
        line_copy(turned2, returned, sem4, send_sem.at[3], k).start()
    returned[place] = turned2[place]
    weigh_steps(8, 12)

    for k in range(1, LINE):
        await_piece(returned, sem4, send_sem.at[3], on_line(k))
    back = returned[...].reshape(BLOCKS, LANES).T
    is_owner = member[...]
    spread = sum(dot(part.astype(BF16), is_owner) for part in split(back))
    derived = jnp.zeros((SLOT_ROWS, PT), F32)
    for s in range(CAP):
        derived = jnp.where(slot == s, spread[s * SLOT_ROWS : (s + 1) * SLOT_ROWS], derived)
    src_tan[mine] = jnp.concatenate([derived[0:3], jnp.zeros((1, PT), F32)], axis=0)
    send_blocks(src_tan, tan_sem, send_sem.at[5], 1, SOURCES)
    weigh_steps(12, SOURCES)

    def gather_sums(n):
        p, t = src_pos[n], src_tan[n]
        p0, p1, p2 = p[0:1], p[1:2], p[2:3]
        t0, t1, t2 = t[0:1], t[1:2], t[2:3]
        rows = jnp.concatenate(
            [t0, t1, t2, t1 * p2 - t2 * p1, t2 * p0 - t0 * p2, t0 * p1 - t1 * p0,
             jnp.zeros((2, PT), F32)],
            axis=0,
        )
        h, m, l = split(rows)
        right = jnp.concatenate([h, m, l, jnp.zeros((8, PT), F32)], axis=0).astype(BF16)
        return dot(w_high[n], right, NT) + dot(w_low[n], right, NT)

    total[...] = gather_sums(mine)

    def sum_step(step, carry):
        n = arriving(src_tan, tan_sem, send_sem.at[5], step)
        total[...] += gather_sums(n)
        return carry

    lax.fori_loop(1, SOURCES, sum_step, 0)
    sums = total[...].T
    sums = sums[0:8] + sums[8:16] + sums[16:24]

    def cross(a, b):
        return [
            a[1] * b[2] - a[2] * b[1],
            a[2] * b[0] - a[0] * b[2],
            a[0] * b[1] - a[1] * b[0],
        ]

    x = [pos[c : c + 1] for c in range(3)]
    flow = [flow_ref[c : c + 1, :] for c in range(3)]
    tangent = [derived[c : c + 1] for c in range(3)]
    curvature = [derived[c : c + 1] for c in range(3, 6)]
    far = cross([sums[c : c + 1] for c in range(3)], x)
    speed = jnp.maximum(
        tangent[0] * tangent[0] + tangent[1] * tangent[1] + tangent[2] * tangent[2], SPEED_FLOOR
    )
    per_speed = 1.0 / jnp.sqrt(speed)
    scale = LOCAL_BETA * per_speed / speed
    local = cross(tangent, curvature)
    superfluid = [
        scale * local[c] + BIOT_SCALE * (far[c] - sums[3 + c : 4 + c]) for c in range(3)
    ]
    unit = [tangent[c] * per_speed for c in range(3)]
    once = cross(unit, [flow[c] - superfluid[c] for c in range(3)])
    twice = cross(unit, once)
    for c in range(3):
        out_ref[c : c + 1, :] = (
            superfluid[c] + FRICTION_ALPHA * once[c] - FRICTION_PRIME * twice[c]
        )

    await_sent(out1, LINE - 1, send_sem.at[0])
    await_sent(turned1, PLANES - 1, send_sem.at[1])
    await_sent(out2, PLANES - 1, send_sem.at[2])
    await_sent(turned2, LINE - 1, send_sem.at[3])
    await_sent(src_pos, SOURCES - 1, send_sem.at[4])
    await_sent(src_tan, SOURCES - 1, send_sem.at[5])


def shards(positions, normal_flow, send_owner, send_slot, recv_index, loop_pos, loop_len):
    vmem = pl.BlockSpec(memory_space=pltpu.VMEM)
    dma = pltpu.SemaphoreType.DMA
    return pl.pallas_call(
        kernel,
        out_shape=jax.ShapeDtypeStruct((3, PT), F32),
        in_specs=[vmem] * 7,
        out_specs=vmem,
        scratch_shapes=[
            pltpu.VMEM((LINE, PLANES, LANES), F32),
            pltpu.VMEM((LINE, PLANES, LANES), F32),
            pltpu.VMEM((PLANES, LINE, LANES), F32),
            pltpu.VMEM((PLANES, LINE, LANES), F32),
            pltpu.VMEM((PLANES, LINE, LANES), F32),
            pltpu.VMEM((PLANES, LINE, LANES), F32),
            pltpu.VMEM((LINE, PLANES, LANES), F32),
            pltpu.VMEM((LINE, PLANES, LANES), F32),
            pltpu.VMEM((SOURCES, 4, PT), F32),
            pltpu.VMEM((SOURCES, 4, PT), F32),
            pltpu.VMEM((PT, LANES), BF16),
            pltpu.VMEM((SOURCES, PT, PT), BF16),
            pltpu.VMEM((SOURCES, PT, PT), BF16),
            pltpu.VMEM((PT, 32), F32),
            pltpu.VMEM((CAP, SLOT_ROWS, LANES), I32),
            pltpu.VMEM((CAP, SLOT_ROWS, LANES), I32),
            pltpu.VMEM((BLOCKS, PT), BF16),
            dma((6,)),
            dma((LINE,)),
            dma((PLANES,)),
            dma((PLANES,)),
            dma((LINE,)),
            dma((SOURCES,)),
            dma((SOURCES,)),
        ],
        compiler_params=pltpu.CompilerParams(
            collective_id=0, has_side_effects=True, vmem_limit_bytes=56 * 1024 * 1024
        ),
        cost_estimate=pl.CostEstimate(
            flops=2 * PT * SOURCES * PT * 128, bytes_accessed=1 << 20, transcendentals=PT * SOURCES * PT
        ),
    )(
        positions,
        normal_flow,
        send_owner.reshape(1, PT),
        send_slot.reshape(1, PT),
        recv_index.reshape(CAP, BLOCKS),
        loop_pos.reshape(COLUMN_ROWS, LANES),
        loop_len.reshape(COLUMN_ROWS, LANES),
    )


def solution(mesh):
    both = P(("blk", "rep"))
    wide = P(None, ("blk", "rep"))
    return jax.shard_map(
        shards,
        mesh=mesh,
        in_specs=(wide, wide, both, both, both, both, both),
        out_specs=wide,
        check_vma=False,
    )
```

```python
import functools

import jax
import jax.numpy as jnp
from jax import lax
from jax.experimental import pallas as pl
from jax.experimental.pallas import tpu as pltpu
from jax.sharding import PartitionSpec as P

LOCAL_BETA = 0.3
FRICTION_ALPHA = 0.21
FRICTION_PRIME = 0.06
BIOT_SCALE = 0.01
CORE_SQUARED = 0.25
SPEED_FLOOR = 1.0

BLOCKS = 128
LINE = 8
PLANES = BLOCKS // LINE
REPS = 4
STOPS = 8
BACK = STOPS // 2 - 1
SOURCES = STOPS * REPS
PT = 512
CAP = 10
LANES = 128
SLOT_ROWS = 8
COLUMN_ROWS = 10

FEATURES = 64
STOP_ORDER = (0, 1, -1, 2, -2, 3, -3, 4)

MESH = pl.DeviceIdType.MESH
F32 = jnp.float32
BF16 = jnp.bfloat16
I32 = jnp.int32

NT = (((1,), (1,)), ((), ()))
NN = (((1,), (0,)), ((), ()))


def dot(left, right, dims=NN):
    return lax.dot_general(left, right, dims, preferred_element_type=F32)


def rounded(value):
    return value.astype(BF16).astype(F32)


def split(value):
    high = rounded(value)
    rest = value - high
    mid = rounded(rest)
    return high, mid, rest - mid


def iota(shape, dim):
    return lax.broadcasted_iota(I32, shape, dim)


def pick(table, index):
    return jnp.take_along_axis(table, index, axis=1, mode="promise_in_bounds")


def look_up(table, index):
    row, lane = index >> 7, index & 127
    found = jnp.zeros(index.shape, table.dtype)
    for t in range(COLUMN_ROWS):
        piece = jnp.broadcast_to(table[t : t + 1], index.shape)
        found = jnp.where(row == t, pick(piece, lane), found)
    return found


def cross(a, b):
    return [
        a[1] * b[2] - a[2] * b[1],
        a[2] * b[0] - a[0] * b[2],
        a[0] * b[1] - a[1] * b[0],
    ]


def rows_of(value, low, top):
    return [value[c : c + 1] for c in range(low, top)]


def kernel(
    pos_hbm, flow_hbm, owner_hbm, slot_hbm, recv_hbm, order_hbm, count_hbm, out_ref,
    pos_ref, flow_ref, owner_ref, slot_ref, recv_ref, order_ref, count_ref,
    out1, in1, turned1, arrived, out2, in2, turned2, returned,
    targets, src_pos, src_tan, target, weights, right, total, part_out, part_in,
    index_a, index_b, member,
    load_sem, send_sem, phase_sem, rep_sem, pos_sem, tan_sem, part_sem,
):
    me = lax.axis_index("blk")
    rep = lax.axis_index("rep")
    plane = me // LINE
    place = me % LINE

    def on_line(k):
        return (place + k) % LINE

    def on_plane(k):
        return (plane + k) % PLANES

    def on_rep(k):
        return (rep + k) % REPS

    def block(stop):
        return (me + stop + BLOCKS) % BLOCKS

    barrier = pltpu.get_barrier_semaphore()

    def greet(blk, other):
        pl.semaphore_signal(barrier, inc=1, device_id=(blk, other), device_id_type=MESH)

    for k in range(1, LINE):
        greet(plane * LINE + on_line(k), rep)
    for k in range(1, PLANES):
        greet(on_plane(k) * LINE + place, rep)
    for k in range(1, REPS):
        greet(me, on_rep(k))
    for stop in STOP_ORDER[1:]:
        greet(block(stop), rep)

    loads = [
        pltpu.make_async_copy(src, dst, load_sem.at[i])
        for i, (src, dst) in enumerate(
            [
                (pos_hbm, pos_ref), (owner_hbm, owner_ref), (slot_hbm, slot_ref),
                (recv_hbm, recv_ref), (order_hbm, order_ref), (count_hbm, count_ref),
                (flow_hbm, flow_ref),
            ]
        )
    ]
    for load in loads:
        load.start()
    for load in loads[:3]:
        load.wait()

    pos = pos_ref[...]
    owner = owner_ref[...]
    slot = slot_ref[...]
    owner_row = (owner & (LINE - 1)) * PLANES + (owner >> 3)
    is_owner = jnp.where(iota((BLOCKS, PT), 0) == owner_row, 1.0, 0.0).astype(BF16)
    member[...] = is_owner
    pos_twice = jnp.concatenate([pos, pos, jnp.zeros((2, PT), F32)], axis=0)
    slotted = jnp.concatenate(
        [jnp.where(slot == s, pos_twice, 0.0) for s in range(CAP)]
        + [jnp.zeros((LANES - CAP * SLOT_ROWS, PT), F32)],
        axis=0,
    )
    outgoing = sum(dot(is_owner, part.astype(BF16), NT) for part in split(slotted))
    out1[...] = outgoing.reshape(LINE, PLANES, LANES)
    square = jnp.sum(pos * pos, axis=0, keepdims=True)
    pos_rows = jnp.concatenate([pos, square], axis=0)
    src_pos[BACK] = pos_rows
    targets[rep] = pos_rows

    def copy_to(src, dst, send, recv, blk, other):
        pltpu.make_async_remote_copy(
            src_ref=src, dst_ref=dst, send_sem=send_sem.at[send], recv_sem=recv,
            device_id=(blk, other), device_id_type=MESH,
        ).start()

    def send_line(src, dst, phase):
        for k in range(1, LINE):
            there = on_line(k)
            copy_to(src.at[there], dst.at[place], phase, phase_sem.at[phase],
                    plane * LINE + there, rep)

    def send_plane(src, dst, phase):
        for k in range(1, PLANES):
            there = on_plane(k)
            copy_to(src.at[there], dst.at[plane], phase, phase_sem.at[phase],
                    there * LINE + place, rep)

    def await_here(dst, recv):
        pltpu.make_async_remote_copy(
            src_ref=dst, dst_ref=dst, send_sem=send_sem.at[0], recv_sem=recv,
            device_id=(me, rep), device_id_type=MESH,
        ).wait_recv()

    def await_sent(part, send):
        pltpu.make_async_remote_copy(
            src_ref=part, dst_ref=part, send_sem=send_sem.at[send], recv_sem=phase_sem.at[0],
            device_id=(me, rep), device_id_type=MESH,
        ).wait_send()

    ones = jnp.ones((1, PT), F32)
    none = jnp.zeros((3, PT), F32)
    one_row = jnp.concatenate([ones, none], axis=0)

    def aim(other):
        rows = targets[other]
        wanted = jnp.concatenate(
            [-2.0 * rows[0:3], ones, rows[3:4] + CORE_SQUARED, none], axis=0
        )
        th, tm, tl = split(wanted)
        features = jnp.concatenate(
            [th, th, tm, tm, th, tl, tl, tm, jnp.zeros((LANES - FEATURES, PT), F32)], axis=0
        )
        target[other] = features.T[:, :FEATURES].astype(BF16)

    def weigh(stop, reps):
        sh, sm, sl = split(jnp.concatenate([src_pos[stop + BACK], one_row], axis=0))
        rows = jnp.concatenate([sh, sm, sh, sm, sl, sh, sm, sl], axis=0).astype(BF16)
        for k in reps:
            other = on_rep(k)
            for half in range(PT // 256):
                low, top = half * 256, half * 256 + 256
                root = lax.rsqrt(dot(target[other], rows[:, low:top]))
                weight = root * root * root
                high = weight.astype(BF16)
                weights[other, stop + BACK, :, low:top] = high
                weights[other, stop + BACK, :, PT + low : PT + top] = (
                    weight - high.astype(F32)
                ).astype(BF16)

    def weigh_stops(low, top):
        def one(i, carry):
            stop = (i % 2) * ((i + 1) // 2) - (1 - i % 2) * (i // 2)
            await_here(src_pos.at[stop + BACK], pos_sem.at[stop + BACK])
            weigh(stop, range(REPS))
            return carry

        lax.fori_loop(low, top, one, 0)

    aim(rep)
    weigh(0, [0])

    pl.semaphore_wait(barrier, (LINE - 1) + (PLANES - 1) + (REPS - 1) + (STOPS - 1))

    send_line(out1, in1, 0)
    for k in range(1, REPS):
        copy_to(targets.at[rep], targets.at[rep], 4, rep_sem.at[rep], me, on_rep(k))
    for stop in STOP_ORDER[1:]:
        copy_to(src_pos.at[BACK], src_pos.at[stop + BACK], 5, pos_sem.at[stop + BACK],
                block(-stop), rep)
    in1[place] = out1[place]

    for load in loads[3:]:
        load.wait()
    spot = iota((16, LANES), 1) * CAP + iota((16, LANES), 0)
    column = jnp.where(iota((16, LANES), 0) < CAP, look_up(recv_ref[...], spot), -1)
    column_row, column_lane = column >> 7, column & 127
    holder = iota((16, LANES), 1).astype(F32)
    inverse = jnp.zeros((32, LANES), F32)
    for s in range(CAP):
        hit = column_row[s : s + 1] == iota((16, LANES), 0)
        left = jnp.concatenate(
            [jnp.where(hit, holder, 0.0), jnp.where(hit, float(s), 0.0)], axis=0
        ).astype(BF16)
        lane_hit = column_lane[s : s + 1] == iota((LANES, LANES), 0)
        inverse = inverse + dot(left, jnp.where(lane_hit, 1.0, 0.0).astype(BF16), NT)
    inverse = (inverse[16:] * float(LANES) + inverse[:16]).astype(I32)
    at = jnp.maximum(column, 0)
    ring = look_up(order_ref[...] + (count_ref[...] << 11), at)
    order, count = ring & 2047, ring >> 11

    def neighbour(offset):
        moved = order + offset
        moved = jnp.where(moved < 0, moved + count, jnp.where(moved >= count, moved - count, moved))
        there = jnp.clip(at - order + moved, 0, COLUMN_ROWS * LANES - 1)
        return look_up(inverse, there)

    await_here(in1.at[pl.ds(0, LINE - 1)], phase_sem.at[0])
    for j in range(PLANES):
        turned1[j] = in1[:, j, :]
    send_plane(turned1, arrived, 1)
    arrived[plane] = turned1[plane]

    ahead1, ahead2, behind1, behind2 = (neighbour(k) for k in (1, 2, -1, -2))
    near = iota((SLOT_ROWS, LANES), 0) < 3
    for s in range(CAP):
        index_a[s] = jnp.where(near, ahead1[s : s + 1], ahead2[s : s + 1])
        index_b[s] = jnp.where(near, behind1[s : s + 1], behind2[s : s + 1])
    for k in range(1, REPS):
        await_here(targets.at[on_rep(k)], rep_sem.at[on_rep(k)])
        aim(on_rep(k))
    weigh(0, range(1, REPS))

    await_here(arrived.at[pl.ds(0, PLANES - 1)], phase_sem.at[1])
    tables = arrived[...].reshape(BLOCKS, LANES).T
    middle = iota((SLOT_ROWS, LANES), 0) < 6
    results = []
    for s in range(CAP):
        to_a, to_b = index_a[s], index_b[s]
        row_a, row_b, lane_a, lane_b = to_a >> 7, to_b >> 7, to_a & 127, to_b & 127
        after = jnp.zeros((SLOT_ROWS, LANES), F32)
        before = jnp.zeros((SLOT_ROWS, LANES), F32)
        for t in range(CAP):
            table = tables[t * SLOT_ROWS : (t + 1) * SLOT_ROWS]
            after = jnp.where(row_a == t, pick(table, lane_a), after)
            before = jnp.where(row_b == t, pick(table, lane_b), before)
        here = tables[s * SLOT_ROWS : (s + 1) * SLOT_ROWS]
        gap, both = after - before, after + before
        first = 8.0 * gap - pltpu.roll(gap, SLOT_ROWS - 3, 0)
        second = 16.0 * pltpu.roll(both, 3, 0) - both - 30.0 * here
        results.append(jnp.where(near, first, jnp.where(middle, second, 0.0)) / 12.0)
    results.append(jnp.zeros((LANES - CAP * SLOT_ROWS, LANES), F32))
    out2[...] = jnp.concatenate(results, axis=0).T.reshape(PLANES, LINE, LANES)

    send_plane(out2, in2, 2)
    in2[plane] = out2[plane]
    weigh_stops(1, 3)
    await_here(in2.at[pl.ds(0, PLANES - 1)], phase_sem.at[2])
    for j in range(LINE):
        turned2[j] = in2[:, j, :]
    send_line(turned2, returned, 3)
    returned[place] = turned2[place]
    weigh_stops(3, 5)
    await_here(returned.at[pl.ds(0, LINE - 1)], phase_sem.at[3])
    back = returned[...].reshape(BLOCKS, LANES).T
    is_owner = member[...]
    spread = sum(dot(part.astype(BF16), is_owner) for part in split(back))
    derived = jnp.zeros((SLOT_ROWS, PT), F32)
    for s in range(CAP):
        derived = jnp.where(slot == s, spread[s * SLOT_ROWS : (s + 1) * SLOT_ROWS], derived)

    src_tan[BACK] = jnp.concatenate([derived[0:3], jnp.zeros((1, PT), F32)], axis=0)
    for stop in STOP_ORDER[1:]:
        copy_to(src_tan.at[BACK], src_tan.at[stop + BACK], 6, tan_sem.at[stop + BACK],
                block(-stop), rep)
    weigh_stops(5, STOPS)

    def prepare(stop):
        p, t = rows_of(src_pos[stop], 0, 3), rows_of(src_tan[stop], 0, 3)
        h, m, l = split(jnp.concatenate(t + cross(t, p) + [jnp.zeros((2, PT), F32)], axis=0))
        rows = jnp.concatenate([h, m, l, jnp.zeros((8, PT), F32)], axis=0).astype(BF16)
        right[stop, :, :PT] = rows
        right[stop, :, PT:] = rows

    prepare(BACK)
    for stop in STOP_ORDER[1:]:
        await_here(src_tan.at[stop + BACK], tan_sem.at[stop + BACK])
        prepare(stop + BACK)

    def gather_sums(k):
        other = on_rep(k)
        total[...] = jnp.zeros_like(total)

        def one(i, carry):
            total[...] += dot(weights[other, 2 * i], right[2 * i], NT) + dot(
                weights[other, 2 * i + 1], right[2 * i + 1], NT
            )
            return carry

        lax.fori_loop(0, STOPS // 2, one, 0)
        parts = total[...].T
        parts = parts[0:8] + parts[8:16] + parts[16:24]
        far = cross(rows_of(parts, 0, 3), rows_of(targets[other], 0, 3))
        return [far[c] - parts[3 + c : 4 + c] for c in range(3)]

    for k in range(1, REPS):
        part_out[k - 1] = jnp.concatenate(gather_sums(k) + [jnp.zeros((1, PT), F32)], axis=0)
        copy_to(part_out.at[k - 1], part_in.at[k - 1], 7, part_sem.at[k - 1], me, on_rep(k))
    far = gather_sums(0)
    for k in range(1, REPS):
        await_here(part_in.at[k - 1], part_sem.at[k - 1])
    others = part_in[0] + part_in[1] + part_in[2]
    far = [far[c] + others[c : c + 1] for c in range(3)]

    tangent, curvature = rows_of(derived, 0, 3), rows_of(derived, 3, 6)
    speed = jnp.maximum(
        tangent[0] * tangent[0] + tangent[1] * tangent[1] + tangent[2] * tangent[2], SPEED_FLOOR
    )
    per_speed = 1.0 / jnp.sqrt(speed)
    scale = LOCAL_BETA * per_speed / speed
    local = cross(tangent, curvature)
    superfluid = [scale * local[c] + BIOT_SCALE * far[c] for c in range(3)]
    unit = [tangent[c] * per_speed for c in range(3)]
    once = cross(unit, [flow_ref[c : c + 1, :] - superfluid[c] for c in range(3)])
    twice = cross(unit, once)
    for c in range(3):
        out_ref[c : c + 1, :] = (
            superfluid[c] + FRICTION_ALPHA * once[c] - FRICTION_PRIME * twice[c]
        )

    await_sent(out1.at[pl.ds(0, LINE - 1)], 0)
    await_sent(turned1.at[pl.ds(0, PLANES - 1)], 1)
    await_sent(out2.at[pl.ds(0, PLANES - 1)], 2)
    await_sent(turned2.at[pl.ds(0, LINE - 1)], 3)
    await_sent(targets.at[pl.ds(0, REPS - 1)], 4)
    await_sent(src_pos.at[pl.ds(0, STOPS - 1)], 5)
    await_sent(src_tan.at[pl.ds(0, STOPS - 1)], 6)
    await_sent(part_out, 7)


def shards(positions, normal_flow, send_owner, send_slot, recv_index, loop_pos, loop_len):
    dma = pltpu.SemaphoreType.DMA
    by_line = pltpu.VMEM((LINE, PLANES, LANES), F32)
    by_plane = pltpu.VMEM((PLANES, LINE, LANES), F32)
    points = pltpu.VMEM((3, PT), F32)
    point_index = pltpu.VMEM((1, PT), I32)
    columns = pltpu.VMEM((COLUMN_ROWS, LANES), I32)
    return pl.pallas_call(
        kernel,
        out_shape=jax.ShapeDtypeStruct((3, PT), F32),
        in_specs=[pl.BlockSpec(memory_space=pltpu.HBM)] * 7,
        out_specs=pl.BlockSpec(memory_space=pltpu.VMEM),
        scratch_shapes=[
            points, points, point_index, point_index, columns, columns, columns,
            by_line, by_line, by_plane, by_plane, by_plane, by_plane, by_line, by_line,
            pltpu.VMEM((REPS, 4, PT), F32),
            pltpu.VMEM((STOPS, 4, PT), F32),
            pltpu.VMEM((STOPS, 4, PT), F32),
            pltpu.VMEM((REPS, PT, FEATURES), BF16),
            pltpu.VMEM((REPS, STOPS, PT, 2 * PT), BF16),
            pltpu.VMEM((STOPS, 32, 2 * PT), BF16),
            pltpu.VMEM((PT, 32), F32),
            pltpu.VMEM((REPS - 1, 4, PT), F32),
            pltpu.VMEM((REPS - 1, 4, PT), F32),
            pltpu.VMEM((CAP, SLOT_ROWS, LANES), I32),
            pltpu.VMEM((CAP, SLOT_ROWS, LANES), I32),
            pltpu.VMEM((BLOCKS, PT), BF16),
            dma((7,)), dma((8,)), dma((4,)), dma((REPS,)), dma((STOPS,)), dma((STOPS,)),
            dma((REPS - 1,)),
        ],
        compiler_params=pltpu.CompilerParams(
            collective_id=0, has_side_effects=True, vmem_limit_bytes=52 * 1024 * 1024
        ),
        cost_estimate=pl.CostEstimate(
            flops=2 * PT * SOURCES * PT * 128, bytes_accessed=1 << 20,
            transcendentals=PT * SOURCES * PT,
        ),
    )(
        positions,
        normal_flow,
        send_owner.reshape(1, PT),
        send_slot.reshape(1, PT),
        recv_index.reshape(CAP, BLOCKS),
        loop_pos.reshape(COLUMN_ROWS, LANES),
        loop_len.reshape(COLUMN_ROWS, LANES),
    )


def solution(mesh):
    both = P(("blk", "rep"))
    wide = P(None, ("blk", "rep"))
    return jax.shard_map(
        shards,
        mesh=mesh,
        in_specs=(wide, wide, both, both, both, both, both),
        out_specs=wide,
        check_vma=False,
    )
```

```python
import functools

import jax
import jax.numpy as jnp
from jax import lax
from jax.experimental import pallas as pl
from jax.experimental.pallas import tpu as pltpu
from jax.sharding import PartitionSpec as P

LOCAL_BETA = 0.3
FRICTION_ALPHA = 0.21
FRICTION_PRIME = 0.06
BIOT_SCALE = 0.01
CORE_SQUARED = 0.25
SPEED_FLOOR = 1.0

BLOCKS = 128
LINE = 8
PLANES = BLOCKS // LINE
REPS = 4
STOPS = 8
BACK = STOPS // 2 - 1
SOURCES = STOPS * REPS
PT = 512
CAP = 10
LANES = 128
SLOT_ROWS = 8
COLUMN_ROWS = 10

FEATURES = 64
STOP_ORDER = (0, 4, 3, -3, 2, -2, 1, -1)
LINE_ORDER = (4, 3, 5, 2, 6, 1, 7)
PLANE_ORDER = (10, 9, 11, 6, 14, 7, 13, 2, 8, 5, 15, 3, 1, 4, 12)

MESH = pl.DeviceIdType.MESH
F32 = jnp.float32
BF16 = jnp.bfloat16
I32 = jnp.int32

NT = (((1,), (1,)), ((), ()))
NN = (((1,), (0,)), ((), ()))


def dot(left, right, dims=NN):
    return lax.dot_general(left, right, dims, preferred_element_type=F32)


def rounded(value):
    return value.astype(BF16).astype(F32)


def split(value):
    high = rounded(value)
    rest = value - high
    mid = rounded(rest)
    return high, mid, rest - mid


def iota(shape, dim):
    return lax.broadcasted_iota(I32, shape, dim)


def pick(table, index):
    return jnp.take_along_axis(table, index, axis=1, mode="promise_in_bounds")


def look_up(table, index):
    row, lane = index >> 7, index & 127
    found = jnp.zeros(index.shape, table.dtype)
    for t in range(COLUMN_ROWS):
        piece = jnp.broadcast_to(table[t : t + 1], index.shape)
        found = jnp.where(row == t, pick(piece, lane), found)
    return found


def cross(a, b):
    return [
        a[1] * b[2] - a[2] * b[1],
        a[2] * b[0] - a[0] * b[2],
        a[0] * b[1] - a[1] * b[0],
    ]


def rows_of(value, low, top):
    return [value[c : c + 1] for c in range(low, top)]


def kernel(
    pos_hbm, flow_hbm, owner_hbm, slot_hbm, recv_hbm, order_hbm, count_hbm, out_ref,
    pos_ref, flow_ref, owner_ref, slot_ref, recv_ref, order_ref, count_ref,
    out1, in1, turned1, arrived, out2, in2, turned2, returned,
    targets, src_pos, src_tan, target, features, weights, right, total, part_out, part_in,
    index_a, index_b, member,
    load_sem, send_sem, phase_sem, rep_sem, pos_sem, tan_sem, part_sem,
):
    me = lax.axis_index("blk")
    rep = lax.axis_index("rep")
    plane = me // LINE
    place = me % LINE

    def on_line(k):
        return (place + k) % LINE

    def on_plane(k):
        return (plane + k) % PLANES

    def on_rep(k):
        return (rep + k) % REPS

    def block(stop):
        return (me + stop + BLOCKS) % BLOCKS

    barrier = pltpu.get_barrier_semaphore()

    def greet(blk, other):
        pl.semaphore_signal(barrier, inc=1, device_id=(blk, other), device_id_type=MESH)

    for k in LINE_ORDER:
        greet(plane * LINE + on_line(k), rep)
    for k in PLANE_ORDER:
        greet(on_plane(k) * LINE + place, rep)
    for k in range(1, REPS):
        greet(me, on_rep(k))
    for stop in STOP_ORDER[1:]:
        greet(block(stop), rep)

    loads = [
        pltpu.make_async_copy(src, dst, load_sem.at[i])
        for i, (src, dst) in enumerate(
            [
                (pos_hbm, pos_ref), (owner_hbm, owner_ref), (slot_hbm, slot_ref),
                (recv_hbm, recv_ref), (order_hbm, order_ref), (count_hbm, count_ref),
                (flow_hbm, flow_ref),
            ]
        )
    ]
    for load in loads:
        load.start()
    for load in loads[:3]:
        load.wait()

    pos = pos_ref[...]
    owner = owner_ref[...]
    slot = slot_ref[...]
    owner_row = (owner & (LINE - 1)) * PLANES + (owner >> 3)
    is_owner = jnp.where(iota((BLOCKS, PT), 0) == owner_row, 1.0, 0.0).astype(BF16)
    member[...] = is_owner
    pos_twice = jnp.concatenate([pos, pos, jnp.zeros((2, PT), F32)], axis=0)
    slotted = jnp.concatenate(
        [jnp.where(slot == s, pos_twice, 0.0) for s in range(CAP)]
        + [jnp.zeros((LANES - CAP * SLOT_ROWS, PT), F32)],
        axis=0,
    )
    outgoing = sum(dot(is_owner, part.astype(BF16), NT) for part in split(slotted))
    out1[...] = outgoing.reshape(LINE, PLANES, LANES)
    square = jnp.sum(pos * pos, axis=0, keepdims=True)
    pos_rows = jnp.concatenate([pos, square], axis=0)
    src_pos[BACK] = pos_rows
    targets[rep] = pos_rows

    def copy_to(src, dst, send, recv, blk, other):
        pltpu.make_async_remote_copy(
            src_ref=src, dst_ref=dst, send_sem=send_sem.at[send], recv_sem=recv,
            device_id=(blk, other), device_id_type=MESH,
        ).start()

    def send_line(src, dst, phase):
        for k in LINE_ORDER:
            there = on_line(k)
            copy_to(src.at[there], dst.at[place], phase, phase_sem.at[phase],
                    plane * LINE + there, rep)

    def send_plane(src, dst, phase):
        for k in PLANE_ORDER:
            there = on_plane(k)
            copy_to(src.at[there], dst.at[plane], phase, phase_sem.at[phase],
                    there * LINE + place, rep)

    def await_here(dst, recv):
        pltpu.make_async_remote_copy(
            src_ref=dst, dst_ref=dst, send_sem=send_sem.at[0], recv_sem=recv,
            device_id=(me, rep), device_id_type=MESH,
        ).wait_recv()

    def await_sent(part, send):
        pltpu.make_async_remote_copy(
            src_ref=part, dst_ref=part, send_sem=send_sem.at[send], recv_sem=phase_sem.at[0],
            device_id=(me, rep), device_id_type=MESH,
        ).wait_send()

    ones = jnp.ones((1, PT), F32)
    none = jnp.zeros((3, PT), F32)
    one_row = jnp.concatenate([ones, none], axis=0)

    def aim(other):
        rows = targets[other]
        wanted = jnp.concatenate(
            [-2.0 * rows[0:3], ones, rows[3:4] + CORE_SQUARED, none], axis=0
        )
        th, tm, tl = split(wanted)
        rows = jnp.concatenate(
            [th, th, tm, tm, th, tl, tl, tm, jnp.zeros((LANES - FEATURES, PT), F32)], axis=0
        )
        target[other] = rows.T[:, :FEATURES].astype(BF16)

    def describe(stop):
        sh, sm, sl = split(jnp.concatenate([src_pos[stop + BACK], one_row], axis=0))
        features[...] = jnp.concatenate([sh, sm, sh, sm, sl, sh, sm, sl], axis=0).astype(BF16)

    def weigh(stop, low, top):
        def one(k, carry):
            other = on_rep(k)
            for half in range(PT // 256):
                low, top = half * 256, half * 256 + 256
                root = lax.rsqrt(dot(target[other], features[:, low:top]))
                weight = root * root * root
                high = weight.astype(BF16)
                weights[other, stop + BACK, :, low:top] = high
                weights[other, stop + BACK, :, PT + low : PT + top] = (
                    weight - high.astype(F32)
                ).astype(BF16)
            return carry

        lax.fori_loop(low, top, one, 0)

    def weigh_stops(low, top):
        def one(i, carry):
            stop = (i % 2) * ((i + 1) // 2) - (1 - i % 2) * (i // 2)
            await_here(src_pos.at[stop + BACK], pos_sem.at[stop + BACK])
            describe(stop)
            weigh(stop, 0, REPS)
            return carry

        lax.fori_loop(low, top, one, 0)

    aim(rep)
    describe(0)

    pl.semaphore_wait(barrier, (LINE - 1) + (PLANES - 1) + (REPS - 1) + (STOPS - 1))

    send_line(out1, in1, 0)
    for k in range(1, REPS):
        copy_to(targets.at[rep], targets.at[rep], 4, rep_sem.at[rep], me, on_rep(k))
    for stop in STOP_ORDER[1:]:
        copy_to(src_pos.at[BACK], src_pos.at[stop + BACK], 5, pos_sem.at[stop + BACK],
                block(-stop), rep)
    in1[place] = out1[place]

    for load in loads[3:]:
        load.wait()
    spot = iota((16, LANES), 1) * CAP + iota((16, LANES), 0)
    column = jnp.where(iota((16, LANES), 0) < CAP, look_up(recv_ref[...], spot), -1)
    column_row, column_lane = column >> 7, column & 127
    holder = iota((16, LANES), 1).astype(F32)
    inverse = jnp.zeros((32, LANES), F32)
    for s in range(CAP):
        hit = column_row[s : s + 1] == iota((16, LANES), 0)
        left = jnp.concatenate(
            [jnp.where(hit, holder, 0.0), jnp.where(hit, float(s), 0.0)], axis=0
        ).astype(BF16)
        lane_hit = column_lane[s : s + 1] == iota((LANES, LANES), 0)
        inverse = inverse + dot(left, jnp.where(lane_hit, 1.0, 0.0).astype(BF16), NT)
    inverse = (inverse[16:] * float(LANES) + inverse[:16]).astype(I32)
    at = jnp.maximum(column, 0)
    ring = look_up(order_ref[...] + (count_ref[...] << 11), at)
    order, count = ring & 2047, ring >> 11

    def neighbour(offset):
        moved = order + offset
        moved = jnp.where(moved < 0, moved + count, jnp.where(moved >= count, moved - count, moved))
        there = jnp.clip(at - order + moved, 0, COLUMN_ROWS * LANES - 1)
        return look_up(inverse, there)

    await_here(in1.at[pl.ds(0, LINE - 1)], phase_sem.at[0])
    for j in range(PLANES):
        turned1[j] = in1[:, j, :]
    send_plane(turned1, arrived, 1)
    arrived[plane] = turned1[plane]

    ahead1, ahead2, behind1, behind2 = (neighbour(k) for k in (1, 2, -1, -2))
    near = iota((SLOT_ROWS, LANES), 0) < 3
    for s in range(CAP):
        index_a[s] = jnp.where(near, ahead1[s : s + 1], ahead2[s : s + 1])
        index_b[s] = jnp.where(near, behind1[s : s + 1], behind2[s : s + 1])
    for k in range(1, REPS):
        await_here(targets.at[on_rep(k)], rep_sem.at[on_rep(k)])
        aim(on_rep(k))
    weigh(0, 0, REPS)

    await_here(arrived.at[pl.ds(0, PLANES - 1)], phase_sem.at[1])
    tables = arrived[...].reshape(BLOCKS, LANES).T
    middle = iota((SLOT_ROWS, LANES), 0) < 6
    results = []
    for s in range(CAP):
        to_a, to_b = index_a[s], index_b[s]
        row_a, row_b, lane_a, lane_b = to_a >> 7, to_b >> 7, to_a & 127, to_b & 127
        after = jnp.zeros((SLOT_ROWS, LANES), F32)
        before = jnp.zeros((SLOT_ROWS, LANES), F32)
        for t in range(CAP):
            table = tables[t * SLOT_ROWS : (t + 1) * SLOT_ROWS]
            after = jnp.where(row_a == t, pick(table, lane_a), after)
            before = jnp.where(row_b == t, pick(table, lane_b), before)
        here = tables[s * SLOT_ROWS : (s + 1) * SLOT_ROWS]
        gap, both = after - before, after + before
        first = 8.0 * gap - pltpu.roll(gap, SLOT_ROWS - 3, 0)
        second = 16.0 * pltpu.roll(both, 3, 0) - both - 30.0 * here
        results.append(jnp.where(near, first, jnp.where(middle, second, 0.0)) / 12.0)
    results.append(jnp.zeros((LANES - CAP * SLOT_ROWS, LANES), F32))
    out2[...] = jnp.concatenate(results, axis=0).T.reshape(PLANES, LINE, LANES)

    send_plane(out2, in2, 2)
    in2[plane] = out2[plane]
    weigh_stops(1, 3)
    await_here(in2.at[pl.ds(0, PLANES - 1)], phase_sem.at[2])
    for j in range(LINE):
        turned2[j] = in2[:, j, :]
    send_line(turned2, returned, 3)
    returned[place] = turned2[place]
    weigh_stops(3, 5)
    await_here(returned.at[pl.ds(0, LINE - 1)], phase_sem.at[3])
    back = returned[...].reshape(BLOCKS, LANES).T
    is_owner = member[...]
    spread = sum(dot(part.astype(BF16), is_owner) for part in split(back))
    derived = jnp.zeros((SLOT_ROWS, PT), F32)
    for s in range(CAP):
        derived = jnp.where(slot == s, spread[s * SLOT_ROWS : (s + 1) * SLOT_ROWS], derived)

    src_tan[BACK] = jnp.concatenate([derived[0:3], jnp.zeros((1, PT), F32)], axis=0)
    for stop in STOP_ORDER[1:]:
        copy_to(src_tan.at[BACK], src_tan.at[stop + BACK], 6, tan_sem.at[stop + BACK],
                block(-stop), rep)
    weigh_stops(5, STOPS)

    def prepare(stop):
        p, t = rows_of(src_pos[stop], 0, 3), rows_of(src_tan[stop], 0, 3)
        h, m, l = split(jnp.concatenate(t + cross(t, p) + [jnp.zeros((2, PT), F32)], axis=0))
        rows = jnp.concatenate([h, m, l, jnp.zeros((8, PT), F32)], axis=0).astype(BF16)
        right[stop, :, :PT] = rows
        right[stop, :, PT:] = rows

    prepare(BACK)
    for stop in STOP_ORDER[1:]:
        await_here(src_tan.at[stop + BACK], tan_sem.at[stop + BACK])
        prepare(stop + BACK)

    def gather_sums(k):
        other = on_rep(k)
        total[...] = jnp.zeros_like(total)

        def one(i, carry):
            total[...] += dot(weights[other, 2 * i], right[2 * i], NT) + dot(
                weights[other, 2 * i + 1], right[2 * i + 1], NT
            )
            return carry

        lax.fori_loop(0, STOPS // 2, one, 0)
        parts = total[...].T
        parts = parts[0:8] + parts[8:16] + parts[16:24]
        far = cross(rows_of(parts, 0, 3), rows_of(targets[other], 0, 3))
        part_out[k % REPS] = jnp.concatenate(
            [far[c] - parts[3 + c : 4 + c] for c in range(3)] + [jnp.zeros((1, PT), F32)], axis=0
        )

    def sums_of(k, carry):
        gather_sums(k)

        @pl.when(k < REPS)
        def _():
            copy_to(part_out.at[k], part_in.at[k], 7, part_sem.at[k], me, on_rep(k))

        return carry

    lax.fori_loop(1, REPS + 1, sums_of, 0)
    for k in range(1, REPS):
        await_here(part_in.at[k], part_sem.at[k])
    others = part_out[0] + part_in[1] + part_in[2] + part_in[3]
    far = [others[c : c + 1] for c in range(3)]

    tangent, curvature = rows_of(derived, 0, 3), rows_of(derived, 3, 6)
    speed = jnp.maximum(
        tangent[0] * tangent[0] + tangent[1] * tangent[1] + tangent[2] * tangent[2], SPEED_FLOOR
    )
    per_speed = 1.0 / jnp.sqrt(speed)
    scale = LOCAL_BETA * per_speed / speed
    local = cross(tangent, curvature)
    superfluid = [scale * local[c] + BIOT_SCALE * far[c] for c in range(3)]
    unit = [tangent[c] * per_speed for c in range(3)]
    once = cross(unit, [flow_ref[c : c + 1, :] - superfluid[c] for c in range(3)])
    twice = cross(unit, once)
    for c in range(3):
        out_ref[c : c + 1, :] = (
            superfluid[c] + FRICTION_ALPHA * once[c] - FRICTION_PRIME * twice[c]
        )

    await_sent(out1.at[pl.ds(0, LINE - 1)], 0)
    await_sent(turned1.at[pl.ds(0, PLANES - 1)], 1)
    await_sent(out2.at[pl.ds(0, PLANES - 1)], 2)
    await_sent(turned2.at[pl.ds(0, LINE - 1)], 3)
    await_sent(targets.at[pl.ds(0, REPS - 1)], 4)
    await_sent(src_pos.at[pl.ds(0, STOPS - 1)], 5)
    await_sent(src_tan.at[pl.ds(0, STOPS - 1)], 6)
    await_sent(part_out.at[pl.ds(1, REPS - 1)], 7)


def shards(positions, normal_flow, send_owner, send_slot, recv_index, loop_pos, loop_len):
    dma = pltpu.SemaphoreType.DMA
    by_line = pltpu.VMEM((LINE, PLANES, LANES), F32)
    by_plane = pltpu.VMEM((PLANES, LINE, LANES), F32)
    points = pltpu.VMEM((3, PT), F32)
    point_index = pltpu.VMEM((1, PT), I32)
    columns = pltpu.VMEM((COLUMN_ROWS, LANES), I32)
    return pl.pallas_call(
        kernel,
        out_shape=jax.ShapeDtypeStruct((3, PT), F32),
        in_specs=[pl.BlockSpec(memory_space=pltpu.HBM)] * 7,
        out_specs=pl.BlockSpec(memory_space=pltpu.VMEM),
        scratch_shapes=[
            points, points, point_index, point_index, columns, columns, columns,
            by_line, by_line, by_plane, by_plane, by_plane, by_plane, by_line, by_line,
            pltpu.VMEM((REPS, 4, PT), F32),
            pltpu.VMEM((STOPS, 4, PT), F32),
            pltpu.VMEM((STOPS, 4, PT), F32),
            pltpu.VMEM((REPS, PT, FEATURES), BF16),
            pltpu.VMEM((FEATURES, PT), BF16),
            pltpu.VMEM((REPS, STOPS, PT, 2 * PT), BF16),
            pltpu.VMEM((STOPS, 32, 2 * PT), BF16),
            pltpu.VMEM((PT, 32), F32),
            pltpu.VMEM((REPS, 4, PT), F32),
            pltpu.VMEM((REPS, 4, PT), F32),
            pltpu.VMEM((CAP, SLOT_ROWS, LANES), I32),
            pltpu.VMEM((CAP, SLOT_ROWS, LANES), I32),
            pltpu.VMEM((BLOCKS, PT), BF16),
            dma((7,)), dma((8,)), dma((4,)), dma((REPS,)), dma((STOPS,)), dma((STOPS,)),
            dma((REPS,)),
        ],
        compiler_params=pltpu.CompilerParams(
            collective_id=0, has_side_effects=True, vmem_limit_bytes=60 * 1024 * 1024
        ),
        cost_estimate=pl.CostEstimate(
            flops=2 * PT * SOURCES * PT * 128, bytes_accessed=1 << 20,
            transcendentals=PT * SOURCES * PT,
        ),
    )(
        positions,
        normal_flow,
        send_owner.reshape(1, PT),
        send_slot.reshape(1, PT),
        recv_index.reshape(CAP, BLOCKS),
        loop_pos.reshape(COLUMN_ROWS, LANES),
        loop_len.reshape(COLUMN_ROWS, LANES),
    )


def solution(mesh):
    both = P(("blk", "rep"))
    wide = P(None, ("blk", "rep"))
    return jax.shard_map(
        shards,
        mesh=mesh,
        in_specs=(wide, wide, both, both, both, both, both),
        out_specs=wide,
        check_vma=False,
    )
```

```python
import functools

import jax
import jax.numpy as jnp
from jax import lax
from jax.experimental import pallas as pl
from jax.experimental.pallas import tpu as pltpu
from jax.sharding import PartitionSpec as P

LOCAL_BETA = 0.3
FRICTION_ALPHA = 0.21
FRICTION_PRIME = 0.06
BIOT_SCALE = 0.01
CORE_SQUARED = 0.25
SPEED_FLOOR = 1.0

BLOCKS = 128
LINE = 8
PLANES = BLOCKS // LINE
REPS = 4
STOPS = 8
BACK = STOPS // 2 - 1
SOURCES = STOPS * REPS
PT = 512
CAP = 10
LANES = 128
SLOT_ROWS = 8
COLUMN_ROWS = 10

FEATURES = 64
STOP_ORDER = (0, 4, 3, -3, 2, -2, 1, -1)
LINE_ORDER = (4, 3, 5, 2, 6, 1, 7)
PLANE_ORDER = (10, 9, 11, 6, 14, 7, 13, 2, 8, 5, 15, 3, 1, 4, 12)

MESH = pl.DeviceIdType.MESH
F32 = jnp.float32
BF16 = jnp.bfloat16
I32 = jnp.int32

NT = (((1,), (1,)), ((), ()))
NN = (((1,), (0,)), ((), ()))


def dot(left, right, dims=NN):
    return lax.dot_general(left, right, dims, preferred_element_type=F32)


def rounded(value):
    return value.astype(BF16).astype(F32)


def split(value):
    high = rounded(value)
    rest = value - high
    mid = rounded(rest)
    return high, mid, rest - mid


def iota(shape, dim):
    return lax.broadcasted_iota(I32, shape, dim)


def pick(table, index):
    return jnp.take_along_axis(table, index, axis=1, mode="promise_in_bounds")


def look_up(table, index):
    row, lane = index >> 7, index & 127
    found = jnp.zeros(index.shape, table.dtype)
    for t in range(COLUMN_ROWS):
        piece = jnp.broadcast_to(table[t : t + 1], index.shape)
        found = jnp.where(row == t, pick(piece, lane), found)
    return found


def cross(a, b):
    return [
        a[1] * b[2] - a[2] * b[1],
        a[2] * b[0] - a[0] * b[2],
        a[0] * b[1] - a[1] * b[0],
    ]


def rows_of(value, low, top):
    return [value[c : c + 1] for c in range(low, top)]


def kernel(
    pos_hbm, flow_hbm, owner_hbm, slot_hbm, recv_hbm, order_hbm, count_hbm, out_ref,
    pos_ref, flow_ref, owner_ref, slot_ref, recv_ref, order_ref, count_ref,
    out1, in1, turned1, arrived, out2, in2, turned2, returned,
    targets, src_pos, src_tan, target, features, weights, right, part_out, part_in,
    index_a, index_b, member,
    load_sem, send_sem, phase_sem, rep_sem, pos_sem, tan_sem, part_sem,
):
    me = lax.axis_index("blk")
    rep = lax.axis_index("rep")
    plane = me // LINE
    place = me % LINE

    def on_line(k):
        return (place + k) % LINE

    def on_plane(k):
        return (plane + k) % PLANES

    def on_rep(k):
        return (rep + k) % REPS

    def block(stop):
        return (me + stop + BLOCKS) % BLOCKS

    loads = [
        pltpu.make_async_copy(src, dst, load_sem.at[i])
        for i, (src, dst) in enumerate(
            [
                (pos_hbm, pos_ref), (owner_hbm, owner_ref), (slot_hbm, slot_ref),
                (recv_hbm, recv_ref), (order_hbm, order_ref), (count_hbm, count_ref),
                (flow_hbm, flow_ref),
            ]
        )
    ]
    for load in loads[:3]:
        load.start()

    barrier = pltpu.get_barrier_semaphore()

    def greet(blk, other):
        pl.semaphore_signal(barrier, inc=1, device_id=(blk, other), device_id_type=MESH)

    for k in LINE_ORDER:
        greet(plane * LINE + on_line(k), rep)
    for k in PLANE_ORDER:
        greet(on_plane(k) * LINE + place, rep)
    for k in range(1, REPS):
        greet(me, on_rep(k))
    for stop in STOP_ORDER[1:]:
        greet(block(stop), rep)

    for load in loads[3:]:
        load.start()
    for load in loads[:3]:
        load.wait()

    pos = pos_ref[...]
    owner = owner_ref[...]
    slot = slot_ref[...]
    owner_row = (owner & (LINE - 1)) * PLANES + (owner >> 3)
    is_owner = jnp.where(iota((BLOCKS, PT), 0) == owner_row, 1.0, 0.0).astype(BF16)
    member[...] = is_owner
    pos_twice = jnp.concatenate([pos, pos, jnp.zeros((2, PT), F32)], axis=0)
    slotted = jnp.concatenate(
        [jnp.where(slot == s, pos_twice, 0.0) for s in range(CAP)]
        + [jnp.zeros((LANES - CAP * SLOT_ROWS, PT), F32)],
        axis=0,
    )
    outgoing = sum(dot(is_owner, part.astype(BF16), NT) for part in split(slotted))
    out1[...] = outgoing.reshape(LINE, PLANES, LANES)
    square = jnp.sum(pos * pos, axis=0, keepdims=True)
    pos_rows = jnp.concatenate([pos, square], axis=0)
    src_pos[BACK] = pos_rows
    targets[rep] = pos_rows

    def copy_to(src, dst, send, recv, blk, other):
        pltpu.make_async_remote_copy(
            src_ref=src, dst_ref=dst, send_sem=send_sem.at[send], recv_sem=recv,
            device_id=(blk, other), device_id_type=MESH,
        ).start()

    def send_line(src, dst, phase):
        for k in LINE_ORDER:
            there = on_line(k)
            copy_to(src.at[there], dst.at[place], phase, phase_sem.at[phase],
                    plane * LINE + there, rep)

    def send_plane(src, dst, phase):
        for k in PLANE_ORDER:
            there = on_plane(k)
            copy_to(src.at[there], dst.at[plane], phase, phase_sem.at[phase],
                    there * LINE + place, rep)

    def await_here(dst, recv):
        pltpu.make_async_remote_copy(
            src_ref=dst, dst_ref=dst, send_sem=send_sem.at[0], recv_sem=recv,
            device_id=(me, rep), device_id_type=MESH,
        ).wait_recv()

    def await_sent(part, send):
        pltpu.make_async_remote_copy(
            src_ref=part, dst_ref=part, send_sem=send_sem.at[send], recv_sem=phase_sem.at[0],
            device_id=(me, rep), device_id_type=MESH,
        ).wait_send()

    ones = jnp.ones((1, PT), F32)
    none = jnp.zeros((3, PT), F32)
    one_row = jnp.concatenate([ones, none], axis=0)

    def aim(other):
        rows = targets[other]
        wanted = jnp.concatenate(
            [-2.0 * rows[0:3], ones, rows[3:4] + CORE_SQUARED, none], axis=0
        )
        th, tm, tl = split(wanted)
        target[other] = jnp.concatenate([th, th, tm, tm, th, tl, tl, tm], axis=0).astype(BF16)

    def describe(stop):
        sh, sm, sl = split(jnp.concatenate([src_pos[stop + BACK], one_row], axis=0))
        rows = jnp.concatenate(
            [sh, sm, sh, sm, sl, sh, sm, sl, jnp.zeros((LANES - FEATURES, PT), F32)], axis=0
        )
        features[...] = rows.T[:, :FEATURES].astype(BF16)

    def weigh(stop, low, top):
        def one(k, carry):
            other = on_rep(k)
            for half in range(PT // 256):
                low, top = half * 256, half * 256 + 256
                root = lax.rsqrt(dot(features[...], target[other, :, low:top]))
                weight = root * root * root
                high = weight.astype(BF16)
                weights[other, stop + BACK, :PT, low:top] = high
                weights[other, stop + BACK, PT:, low:top] = (
                    weight - high.astype(F32)
                ).astype(BF16)
            return carry

        lax.fori_loop(low, top, one, 0)

    def weigh_stops(low, top):
        def one(i, carry):
            stop = (i % 2) * ((i + 1) // 2) - (1 - i % 2) * (i // 2)
            await_here(src_pos.at[stop + BACK], pos_sem.at[stop + BACK])
            describe(stop)
            weigh(stop, 0, REPS)
            return carry

        lax.fori_loop(low, top, one, 0)


    pl.semaphore_wait(barrier, (LINE - 1) + (PLANES - 1) + (REPS - 1) + (STOPS - 1))

    send_line(out1, in1, 0)
    for k in range(1, REPS):
        copy_to(targets.at[rep], targets.at[rep], 4, rep_sem.at[rep], me, on_rep(k))
    in1[place] = out1[place]

    for load in loads[3:]:
        load.wait()
    spot = iota((16, LANES), 1) * CAP + iota((16, LANES), 0)
    column = jnp.where(iota((16, LANES), 0) < CAP, look_up(recv_ref[...], spot), -1)
    column_row, column_lane = column >> 7, column & 127
    holder = iota((16, LANES), 1).astype(F32)
    inverse = jnp.zeros((32, LANES), F32)
    for s in range(CAP):
        hit = column_row[s : s + 1] == iota((16, LANES), 0)
        left = jnp.concatenate(
            [jnp.where(hit, holder, 0.0), jnp.where(hit, float(s), 0.0)], axis=0
        ).astype(BF16)
        lane_hit = column_lane[s : s + 1] == iota((LANES, LANES), 0)
        inverse = inverse + dot(left, jnp.where(lane_hit, 1.0, 0.0).astype(BF16), NT)
    inverse = (inverse[16:] * float(LANES) + inverse[:16]).astype(I32)
    at = jnp.maximum(column, 0)
    ring = look_up(order_ref[...] + (count_ref[...] << 11), at)
    order, count = ring & 2047, ring >> 11

    def neighbour(offset):
        moved = order + offset
        moved = jnp.where(moved < 0, moved + count, jnp.where(moved >= count, moved - count, moved))
        there = jnp.clip(at - order + moved, 0, COLUMN_ROWS * LANES - 1)
        return look_up(inverse, there)

    aim(rep)
    describe(0)
    await_here(in1.at[pl.ds(0, LINE - 1)], phase_sem.at[0])
    for j in range(PLANES):
        turned1[j] = in1[:, j, :]
    send_plane(turned1, arrived, 1)
    arrived[plane] = turned1[plane]
    for stop in STOP_ORDER[1:]:
        copy_to(src_pos.at[BACK], src_pos.at[stop + BACK], 5, pos_sem.at[stop + BACK],
                block(-stop), rep)

    ahead1, ahead2, behind1, behind2 = (neighbour(k) for k in (1, 2, -1, -2))
    near = iota((SLOT_ROWS, LANES), 0) < 3
    for s in range(CAP):
        index_a[s] = jnp.where(near, ahead1[s : s + 1], ahead2[s : s + 1])
        index_b[s] = jnp.where(near, behind1[s : s + 1], behind2[s : s + 1])
    for k in range(1, REPS):
        await_here(targets.at[on_rep(k)], rep_sem.at[on_rep(k)])
        aim(on_rep(k))
    weigh(0, 0, REPS)

    await_here(arrived.at[pl.ds(0, PLANES - 1)], phase_sem.at[1])
    tables = arrived[...].reshape(BLOCKS, LANES).T
    middle = iota((SLOT_ROWS, LANES), 0) < 6
    results = []
    for s in range(CAP):
        to_a, to_b = index_a[s], index_b[s]
        row_a, row_b, lane_a, lane_b = to_a >> 7, to_b >> 7, to_a & 127, to_b & 127
        after = jnp.zeros((SLOT_ROWS, LANES), F32)
        before = jnp.zeros((SLOT_ROWS, LANES), F32)
        for t in range(CAP):
            table = tables[t * SLOT_ROWS : (t + 1) * SLOT_ROWS]
            after = jnp.where(row_a == t, pick(table, lane_a), after)
            before = jnp.where(row_b == t, pick(table, lane_b), before)
        here = tables[s * SLOT_ROWS : (s + 1) * SLOT_ROWS]
        gap, both = after - before, after + before
        first = 8.0 * gap - pltpu.roll(gap, SLOT_ROWS - 3, 0)
        second = 16.0 * pltpu.roll(both, 3, 0) - both - 30.0 * here
        results.append(jnp.where(near, first, jnp.where(middle, second, 0.0)) / 12.0)
    results.append(jnp.zeros((LANES - CAP * SLOT_ROWS, LANES), F32))
    out2[...] = jnp.concatenate(results, axis=0).T.reshape(PLANES, LINE, LANES)

    send_plane(out2, in2, 2)
    in2[plane] = out2[plane]
    weigh_stops(1, 3)
    await_here(in2.at[pl.ds(0, PLANES - 1)], phase_sem.at[2])
    for j in range(LINE):
        turned2[j] = in2[:, j, :]
    send_line(turned2, returned, 3)
    returned[place] = turned2[place]
    weigh_stops(3, 5)
    await_here(returned.at[pl.ds(0, LINE - 1)], phase_sem.at[3])
    back = returned[...].reshape(BLOCKS, LANES).T
    is_owner = member[...]
    spread = sum(dot(part.astype(BF16), is_owner) for part in split(back))
    derived = jnp.zeros((SLOT_ROWS, PT), F32)
    for s in range(CAP):
        derived = jnp.where(slot == s, spread[s * SLOT_ROWS : (s + 1) * SLOT_ROWS], derived)

    src_tan[BACK] = jnp.concatenate([derived[0:3], jnp.zeros((1, PT), F32)], axis=0)
    for stop in STOP_ORDER[1:]:
        copy_to(src_tan.at[BACK], src_tan.at[stop + BACK], 6, tan_sem.at[stop + BACK],
                block(-stop), rep)
    weigh_stops(5, STOPS)

    def prepare(stop):
        p, t = rows_of(src_pos[stop], 0, 3), rows_of(src_tan[stop], 0, 3)
        h, m, l = split(jnp.concatenate(t + cross(t, p) + [jnp.zeros((2, PT), F32)], axis=0))
        rows = jnp.concatenate([h, m, l, jnp.zeros((8, PT), F32)], axis=0).astype(BF16)
        right[stop, :, :PT] = rows
        right[stop, :, PT:] = rows

    prepare(BACK)
    for stop in STOP_ORDER[1:]:
        await_here(src_tan.at[stop + BACK], tan_sem.at[stop + BACK])
        prepare(stop + BACK)

    def gather_sums(k):
        other = on_rep(k)

        def some(i, sums):
            for j in range(4):
                sums = sums + dot(right[4 * i + j], weights[other, 4 * i + j])
            return sums

        parts = lax.fori_loop(0, STOPS // 4, some, jnp.zeros((32, PT), F32))
        parts = parts[0:8] + parts[8:16] + parts[16:24]
        far = cross(rows_of(parts, 0, 3), rows_of(targets[other], 0, 3))
        part_out[k % REPS] = jnp.concatenate(
            [far[c] - parts[3 + c : 4 + c] for c in range(3)] + [jnp.zeros((1, PT), F32)], axis=0
        )

    def sums_of(k, carry):
        gather_sums(k)

        @pl.when(k < REPS)
        def _():
            copy_to(part_out.at[k], part_in.at[k], 7, part_sem.at[k], me, on_rep(k))

        return carry

    lax.fori_loop(1, REPS + 1, sums_of, 0)
    for k in range(1, REPS):
        await_here(part_in.at[k], part_sem.at[k])
    others = part_out[0] + part_in[1] + part_in[2] + part_in[3]
    far = [others[c : c + 1] for c in range(3)]

    tangent, curvature = rows_of(derived, 0, 3), rows_of(derived, 3, 6)
    speed = jnp.maximum(
        tangent[0] * tangent[0] + tangent[1] * tangent[1] + tangent[2] * tangent[2], SPEED_FLOOR
    )
    per_speed = 1.0 / jnp.sqrt(speed)
    scale = LOCAL_BETA * per_speed / speed
    local = cross(tangent, curvature)
    superfluid = [scale * local[c] + BIOT_SCALE * far[c] for c in range(3)]
    unit = [tangent[c] * per_speed for c in range(3)]
    once = cross(unit, [flow_ref[c : c + 1, :] - superfluid[c] for c in range(3)])
    twice = cross(unit, once)
    for c in range(3):
        out_ref[c : c + 1, :] = (
            superfluid[c] + FRICTION_ALPHA * once[c] - FRICTION_PRIME * twice[c]
        )

    await_sent(out1.at[pl.ds(0, LINE - 1)], 0)
    await_sent(turned1.at[pl.ds(0, PLANES - 1)], 1)
    await_sent(out2.at[pl.ds(0, PLANES - 1)], 2)
    await_sent(turned2.at[pl.ds(0, LINE - 1)], 3)
    await_sent(targets.at[pl.ds(0, REPS - 1)], 4)
    await_sent(src_pos.at[pl.ds(0, STOPS - 1)], 5)
    await_sent(src_tan.at[pl.ds(0, STOPS - 1)], 6)
    await_sent(part_out.at[pl.ds(1, REPS - 1)], 7)


def shards(positions, normal_flow, send_owner, send_slot, recv_index, loop_pos, loop_len):
    dma = pltpu.SemaphoreType.DMA
    by_line = pltpu.VMEM((LINE, PLANES, LANES), F32)
    by_plane = pltpu.VMEM((PLANES, LINE, LANES), F32)
    points = pltpu.VMEM((3, PT), F32)
    point_index = pltpu.VMEM((1, PT), I32)
    columns = pltpu.VMEM((COLUMN_ROWS, LANES), I32)
    return pl.pallas_call(
        kernel,
        out_shape=jax.ShapeDtypeStruct((3, PT), F32),
        in_specs=[pl.BlockSpec(memory_space=pltpu.HBM)] * 7,
        out_specs=pl.BlockSpec(memory_space=pltpu.VMEM),
        scratch_shapes=[
            points, points, point_index, point_index, columns, columns, columns,
            by_line, by_line, by_plane, by_plane, by_plane, by_plane, by_line, by_line,
            pltpu.VMEM((REPS, 4, PT), F32),
            pltpu.VMEM((STOPS, 4, PT), F32),
            pltpu.VMEM((STOPS, 4, PT), F32),
            pltpu.VMEM((REPS, FEATURES, PT), BF16),
            pltpu.VMEM((PT, FEATURES), BF16),
            pltpu.VMEM((REPS, STOPS, 2 * PT, PT), BF16),
            pltpu.VMEM((STOPS, 32, 2 * PT), BF16),
            pltpu.VMEM((REPS, 4, PT), F32),
            pltpu.VMEM((REPS, 4, PT), F32),
            pltpu.VMEM((CAP, SLOT_ROWS, LANES), I32),
            pltpu.VMEM((CAP, SLOT_ROWS, LANES), I32),
            pltpu.VMEM((BLOCKS, PT), BF16),
            dma((7,)), dma((8,)), dma((4,)), dma((REPS,)), dma((STOPS,)), dma((STOPS,)),
            dma((REPS,)),
        ],
        compiler_params=pltpu.CompilerParams(
            collective_id=0, has_side_effects=True, vmem_limit_bytes=60 * 1024 * 1024
        ),
        cost_estimate=pl.CostEstimate(
            flops=2 * PT * SOURCES * PT * 128, bytes_accessed=1 << 20,
            transcendentals=PT * SOURCES * PT,
        ),
    )(
        positions,
        normal_flow,
        send_owner.reshape(1, PT),
        send_slot.reshape(1, PT),
        recv_index.reshape(CAP, BLOCKS),
        loop_pos.reshape(COLUMN_ROWS, LANES),
        loop_len.reshape(COLUMN_ROWS, LANES),
    )


def solution(mesh):
    both = P(("blk", "rep"))
    wide = P(None, ("blk", "rep"))
    return jax.shard_map(
        shards,
        mesh=mesh,
        in_specs=(wide, wide, both, both, both, both, both),
        out_specs=wide,
        check_vma=False,
    )
```

```python
import functools

import jax
import jax.numpy as jnp
from jax import lax
from jax.experimental import pallas as pl
from jax.experimental.pallas import tpu as pltpu
from jax.sharding import PartitionSpec as P

LOCAL_BETA = 0.3
FRICTION_ALPHA = 0.21
FRICTION_PRIME = 0.06
BIOT_SCALE = 0.01
CORE_SQUARED = 0.25
SPEED_FLOOR = 1.0

BLOCKS = 128
LINE = 8
PLANES = BLOCKS // LINE
REPS = 4
STOPS = 8
BACK = STOPS // 2 - 1
SOURCES = STOPS * REPS
PT = 512
CAP = 10
LANES = 128
SLOT_ROWS = 8
COLUMN_ROWS = 10

FEATURES = 64
STOP_ORDER = (0, 4, 3, -3, 2, -2, 1, -1)
LINE_ORDER = (4, 3, 5, 2, 6, 1, 7)
LATE = 6
PLANE_ORDER = (10, 9, 11, 6, 14, 7, 13, 2, 8, 5, 15, 3, 1, 4, 12)

MESH = pl.DeviceIdType.MESH
F32 = jnp.float32
BF16 = jnp.bfloat16
I32 = jnp.int32

NT = (((1,), (1,)), ((), ()))
NN = (((1,), (0,)), ((), ()))


def dot(left, right, dims=NN):
    return lax.dot_general(left, right, dims, preferred_element_type=F32)


def rounded(value):
    return value.astype(BF16).astype(F32)


def split(value):
    high = rounded(value)
    rest = value - high
    mid = rounded(rest)
    return high, mid, rest - mid


def iota(shape, dim):
    return lax.broadcasted_iota(I32, shape, dim)


def pick(table, index):
    return jnp.take_along_axis(table, index, axis=1, mode="promise_in_bounds")


def look_up(table, index):
    row, lane = index >> 7, index & 127
    found = jnp.zeros(index.shape, table.dtype)
    for t in range(COLUMN_ROWS):
        piece = jnp.broadcast_to(table[t : t + 1], index.shape)
        found = jnp.where(row == t, pick(piece, lane), found)
    return found


def cross(a, b):
    return [
        a[1] * b[2] - a[2] * b[1],
        a[2] * b[0] - a[0] * b[2],
        a[0] * b[1] - a[1] * b[0],
    ]


def rows_of(value, low, top):
    return [value[c : c + 1] for c in range(low, top)]


def kernel(
    pos_hbm, flow_hbm, owner_hbm, slot_hbm, recv_hbm, order_hbm, count_hbm, out_ref,
    pos_ref, flow_ref, owner_ref, slot_ref, recv_ref, order_ref, count_ref,
    out1, in1, turned1, arrived, out2, in2, turned2, returned,
    targets, src_pos, src_tan, target, features, weights, right, part_out, part_in,
    index_a, index_b, member,
    load_sem, ready, send_sem, phase_sem, rep_sem, pos_sem, tan_sem, part_sem,
):
    me = lax.axis_index("blk")
    rep = lax.axis_index("rep")
    plane = me // LINE
    place = me % LINE

    def on_line(k):
        return (place + k) % LINE

    def on_plane(k):
        return (plane + k) % PLANES

    def on_rep(k):
        return (rep + k) % REPS

    def block(stop):
        return (me + stop + BLOCKS) % BLOCKS

    loads = [
        pltpu.make_async_copy(src, dst, load_sem.at[i])
        for i, (src, dst) in enumerate(
            [
                (pos_hbm, pos_ref), (owner_hbm, owner_ref), (slot_hbm, slot_ref),
                (recv_hbm, recv_ref), (order_hbm, order_ref), (count_hbm, count_ref),
                (flow_hbm, flow_ref),
            ]
        )
    ]
    for load in loads[:3]:
        load.start()

    barrier = pltpu.get_barrier_semaphore()

    def greet(blk, other):
        pl.semaphore_signal(barrier, inc=1, device_id=(blk, other), device_id_type=MESH)

    def loop(low, top, act):
        def one(i, carry):
            act(i)
            return carry

        lax.fori_loop(low, top, one, 0)

    def step_in(t):
        return (t - place + BACK + LINE) % LINE - BACK

    def step_out(t):
        return (t - place + BACK + 1 + LINE) % LINE - BACK - 1

    def greet_block(t):
        greet(block(step_in(t)), rep)

        @pl.when(t - place == STOPS // 2)
        def _():
            greet(block(-STOPS // 2), rep)

    loop(place + 1, LINE, lambda t: greet(plane * LINE + t, rep))
    loop(place + 1, LINE, greet_block)
    loop(plane + 1, PLANES, lambda t: greet(t * LINE + place, rep))
    loop(rep + 1, REPS, lambda t: greet(me, t))

    for load in loads[3:]:
        load.start()
    lower = 2 * place + place // (STOPS // 2) + plane + rep

    @pl.when(lower > 0)
    def _():
        pl.semaphore_wait(barrier, lower)

    def accept(kind, blk):
        pl.semaphore_signal(
            ready.at[kind], inc=1, device_id=(blk, rep), device_id_type=MESH
        )

    loop(0, place, lambda t: accept(0, plane * LINE + t))
    loop(0, plane, lambda t: accept(1, t * LINE + place))

    @pl.when(place >= STOPS // 2)
    def _():
        accept(2, block(STOPS // 2))

    for load in loads[:3]:
        load.wait()

    def copy_to(src, dst, send, recv, blk, other):
        pltpu.make_async_remote_copy(
            src_ref=src, dst_ref=dst, send_sem=send_sem.at[send], recv_sem=recv,
            device_id=(blk, other), device_id_type=MESH,
        ).start()

    def send_pos(t):
        step = step_out(t)
        copy_to(src_pos.at[BACK], src_pos.at[BACK - step], 5, pos_sem.at[BACK - step],
                block(step), rep)

    def send_target(t):
        copy_to(targets.at[rep], targets.at[rep], 4, rep_sem.at[rep], me, t)

    pos = pos_ref[...]
    square = jnp.sum(pos * pos, axis=0, keepdims=True)
    pos_rows = jnp.concatenate([pos, square], axis=0)
    src_pos[BACK] = pos_rows
    targets[rep] = pos_rows
    loop(0, place, send_pos)
    loop(0, rep, send_target)
    owner = owner_ref[...]
    slot = slot_ref[...]
    owner_row = (owner & (LINE - 1)) * PLANES + (owner >> 3)
    is_owner = jnp.where(iota((BLOCKS, PT), 0) == owner_row, 1.0, 0.0).astype(BF16)
    member[...] = is_owner
    pos_twice = jnp.concatenate([pos, pos, jnp.zeros((2, PT), F32)], axis=0)
    slotted = jnp.concatenate(
        [jnp.where(slot == s, pos_twice, 0.0) for s in range(CAP)]
        + [jnp.zeros((LANES - CAP * SLOT_ROWS, PT), F32)],
        axis=0,
    )
    outgoing = sum(dot(is_owner, part.astype(BF16), NT) for part in split(slotted))
    out1[...] = outgoing.reshape(LINE, PLANES, LANES)
    def send_line(src, dst, phase):
        for k in LINE_ORDER:
            there = on_line(k)
            copy_to(src.at[there], dst.at[place], phase, phase_sem.at[phase],
                    plane * LINE + there, rep)

    def send_plane(src, dst, phase):
        for k in PLANE_ORDER:
            there = on_plane(k)
            copy_to(src.at[there], dst.at[plane], phase, phase_sem.at[phase],
                    there * LINE + place, rep)

    def await_here(dst, recv):
        pltpu.make_async_remote_copy(
            src_ref=dst, dst_ref=dst, send_sem=send_sem.at[0], recv_sem=recv,
            device_id=(me, rep), device_id_type=MESH,
        ).wait_recv()

    def await_sent(part, send):
        pltpu.make_async_remote_copy(
            src_ref=part, dst_ref=part, send_sem=send_sem.at[send], recv_sem=phase_sem.at[0],
            device_id=(me, rep), device_id_type=MESH,
        ).wait_send()

    ones = jnp.ones((1, PT), F32)
    none = jnp.zeros((3, PT), F32)
    one_row = jnp.concatenate([ones, none], axis=0)

    def aim(other):
        rows = targets[other]
        wanted = jnp.concatenate(
            [-2.0 * rows[0:3], ones, rows[3:4] + CORE_SQUARED, none], axis=0
        )
        th, tm, tl = split(wanted)
        target[other] = jnp.concatenate([th, th, tm, tm, th, tl, tl, tm], axis=0).astype(BF16)

    def describe(stop):
        sh, sm, sl = split(jnp.concatenate([src_pos[stop + BACK], one_row], axis=0))
        rows = jnp.concatenate(
            [sh, sm, sh, sm, sl, sh, sm, sl, jnp.zeros((LANES - FEATURES, PT), F32)], axis=0
        )
        features[...] = rows.T[:, :FEATURES].astype(BF16)

    def weigh(t):
        stop = step_in(t)
        describe(stop)

        def one(other):
            for half in range(PT // 256):
                low, top = half * 256, half * 256 + 256
                root = lax.rsqrt(dot(features[...], target[other, :, low:top]))
                weight = root * root * root
                high = weight.astype(BF16)
                weights[other, stop + BACK, :PT, low:top] = high
                weights[other, stop + BACK, PT:, low:top] = (
                    weight - high.astype(F32)
                ).astype(BF16)

        loop(0, REPS, one)

    def await_pos(t):
        await_here(src_pos.at[step_in(t) + BACK], pos_sem.at[step_in(t) + BACK])

    def higher_reps():
        def one(t):
            await_here(targets.at[t], rep_sem.at[t])
            send_target(t)

        loop(rep + 1, REPS, one)

    def lower_reps():
        loop(0, rep, lambda t: await_here(targets.at[t], rep_sem.at[t]))
        loop(0, REPS, aim)

    early = place < LATE
    low_count = jnp.where(place < 2, place, jnp.where(place < 3, 2, jnp.where(early, 5 - place, 0)))
    high_top = jnp.where(place < 3, 5 - place, place)

    def in_turn(i):
        return jnp.where(i == 0, place, jnp.where(i <= place, i - 1, i))

    def is_early(t):
        return early & jnp.where(t == place, True, jnp.where(t < place, t < low_count, t <= high_top))

    def serve(i):
        t = in_turn(i)

        @pl.when(t > place)
        def _():
            await_pos(t)

            @pl.when(t - place == STOPS // 2)
            def _():
                pl.semaphore_wait(ready.at[2], 1)

            send_pos(t)

        @pl.when(is_early(t))
        def _():
            @pl.when(t < place)
            def _():
                await_pos(t)

            weigh(t)

    def finish(i):
        t = in_turn(i)

        @pl.when(jnp.logical_not(is_early(t) | (early & (t >= LATE))))
        def _():
            @pl.when(t < place)
            def _():
                await_pos(t)

            weigh(t)

    @pl.when(early)
    def _():
        higher_reps()
        lower_reps()

    loop(0, LINE, serve)

    @pl.when(place < LINE - 1)
    def _():
        pl.semaphore_wait(ready.at[0], LINE - 1 - place)

    send_line(out1, in1, 0)
    in1[place] = out1[place]

    for load in loads[3:]:
        load.wait()
    spot = iota((16, LANES), 1) * CAP + iota((16, LANES), 0)
    column = jnp.where(iota((16, LANES), 0) < CAP, look_up(recv_ref[...], spot), -1)
    column_row, column_lane = column >> 7, column & 127
    holder = iota((16, LANES), 1).astype(F32)
    inverse = jnp.zeros((32, LANES), F32)
    for s in range(CAP):
        hit = column_row[s : s + 1] == iota((16, LANES), 0)
        left = jnp.concatenate(
            [jnp.where(hit, holder, 0.0), jnp.where(hit, float(s), 0.0)], axis=0
        ).astype(BF16)
        lane_hit = column_lane[s : s + 1] == iota((LANES, LANES), 0)
        inverse = inverse + dot(left, jnp.where(lane_hit, 1.0, 0.0).astype(BF16), NT)
    inverse = (inverse[16:] * float(LANES) + inverse[:16]).astype(I32)
    at = jnp.maximum(column, 0)
    ring = look_up(order_ref[...] + (count_ref[...] << 11), at)
    order, count = ring & 2047, ring >> 11

    def neighbour(offset):
        moved = order + offset
        moved = jnp.where(moved < 0, moved + count, jnp.where(moved >= count, moved - count, moved))
        there = jnp.clip(at - order + moved, 0, COLUMN_ROWS * LANES - 1)
        return look_up(inverse, there)

    await_here(in1.at[pl.ds(0, LINE - 1)], phase_sem.at[0])
    for j in range(PLANES):
        turned1[j] = in1[:, j, :]

    @pl.when(plane < PLANES - 1)
    def _():
        pl.semaphore_wait(ready.at[1], PLANES - 1 - plane)

    send_plane(turned1, arrived, 1)
    arrived[plane] = turned1[plane]

    ahead1, ahead2, behind1, behind2 = (neighbour(k) for k in (1, 2, -1, -2))
    near = iota((SLOT_ROWS, LANES), 0) < 3
    for s in range(CAP):
        index_a[s] = jnp.where(near, ahead1[s : s + 1], ahead2[s : s + 1])
        index_b[s] = jnp.where(near, behind1[s : s + 1], behind2[s : s + 1])
    await_here(arrived.at[pl.ds(0, PLANES - 1)], phase_sem.at[1])
    tables = arrived[...].reshape(BLOCKS, LANES).T
    middle = iota((SLOT_ROWS, LANES), 0) < 6
    results = []
    for s in range(CAP):
        to_a, to_b = index_a[s], index_b[s]
        row_a, row_b, lane_a, lane_b = to_a >> 7, to_b >> 7, to_a & 127, to_b & 127
        after = jnp.zeros((SLOT_ROWS, LANES), F32)
        before = jnp.zeros((SLOT_ROWS, LANES), F32)
        for t in range(CAP):
            table = tables[t * SLOT_ROWS : (t + 1) * SLOT_ROWS]
            after = jnp.where(row_a == t, pick(table, lane_a), after)
            before = jnp.where(row_b == t, pick(table, lane_b), before)
        here = tables[s * SLOT_ROWS : (s + 1) * SLOT_ROWS]
        gap, both = after - before, after + before
        first = 8.0 * gap - pltpu.roll(gap, SLOT_ROWS - 3, 0)
        second = 16.0 * pltpu.roll(both, 3, 0) - both - 30.0 * here
        results.append(jnp.where(near, first, jnp.where(middle, second, 0.0)) / 12.0)
    results.append(jnp.zeros((LANES - CAP * SLOT_ROWS, LANES), F32))
    out2[...] = jnp.concatenate(results, axis=0).T.reshape(PLANES, LINE, LANES)

    send_plane(out2, in2, 2)
    in2[plane] = out2[plane]

    @pl.when(early)
    def _():
        weigh(LATE)

    @pl.when(jnp.logical_not(early))
    def _():
        higher_reps()

    await_here(in2.at[pl.ds(0, PLANES - 1)], phase_sem.at[2])
    for j in range(LINE):
        turned2[j] = in2[:, j, :]
    send_line(turned2, returned, 3)
    returned[place] = turned2[place]

    @pl.when(early)
    def _():
        weigh(LATE + 1)

    await_here(returned.at[pl.ds(0, LINE - 1)], phase_sem.at[3])
    back = returned[...].reshape(BLOCKS, LANES).T
    is_owner = member[...]
    spread = sum(dot(part.astype(BF16), is_owner) for part in split(back))
    derived = jnp.zeros((SLOT_ROWS, PT), F32)
    for s in range(CAP):
        derived = jnp.where(slot == s, spread[s * SLOT_ROWS : (s + 1) * SLOT_ROWS], derived)

    src_tan[BACK] = jnp.concatenate([derived[0:3], jnp.zeros((1, PT), F32)], axis=0)
    for stop in STOP_ORDER[1:]:
        copy_to(src_tan.at[BACK], src_tan.at[stop + BACK], 6, tan_sem.at[stop + BACK],
                block(-stop), rep)

    @pl.when(jnp.logical_not(early))
    def _():
        lower_reps()

    loop(0, LINE, finish)

    def prepare(stop):
        p, t = rows_of(src_pos[stop], 0, 3), rows_of(src_tan[stop], 0, 3)
        h, m, l = split(jnp.concatenate(t + cross(t, p) + [jnp.zeros((2, PT), F32)], axis=0))
        rows = jnp.concatenate([h, m, l, jnp.zeros((8, PT), F32)], axis=0).astype(BF16)
        right[stop, :, :PT] = rows
        right[stop, :, PT:] = rows

    prepare(BACK)
    for stop in STOP_ORDER[1:]:
        await_here(src_tan.at[stop + BACK], tan_sem.at[stop + BACK])
        prepare(stop + BACK)

    def gather_sums(k):
        other = on_rep(k)

        def some(i, sums):
            for j in range(4):
                sums = sums + dot(right[4 * i + j], weights[other, 4 * i + j])
            return sums

        parts = lax.fori_loop(0, STOPS // 4, some, jnp.zeros((32, PT), F32))
        parts = parts[0:8] + parts[8:16] + parts[16:24]
        far = cross(rows_of(parts, 0, 3), rows_of(targets[other], 0, 3))
        part_out[k % REPS] = jnp.concatenate(
            [far[c] - parts[3 + c : 4 + c] for c in range(3)] + [jnp.zeros((1, PT), F32)], axis=0
        )

    def sums_of(k, carry):
        gather_sums(k)

        @pl.when(k < REPS)
        def _():
            copy_to(part_out.at[k], part_in.at[k], 7, part_sem.at[k], me, on_rep(k))

        return carry

    lax.fori_loop(1, REPS + 1, sums_of, 0)
    for k in range(1, REPS):
        await_here(part_in.at[k], part_sem.at[k])
    others = part_out[0] + part_in[1] + part_in[2] + part_in[3]
    far = [others[c : c + 1] for c in range(3)]

    tangent, curvature = rows_of(derived, 0, 3), rows_of(derived, 3, 6)
    speed = jnp.maximum(
        tangent[0] * tangent[0] + tangent[1] * tangent[1] + tangent[2] * tangent[2], SPEED_FLOOR
    )
    per_speed = 1.0 / jnp.sqrt(speed)
    scale = LOCAL_BETA * per_speed / speed
    local = cross(tangent, curvature)
    superfluid = [scale * local[c] + BIOT_SCALE * far[c] for c in range(3)]
    unit = [tangent[c] * per_speed for c in range(3)]
    once = cross(unit, [flow_ref[c : c + 1, :] - superfluid[c] for c in range(3)])
    twice = cross(unit, once)
    for c in range(3):
        out_ref[c : c + 1, :] = (
            superfluid[c] + FRICTION_ALPHA * once[c] - FRICTION_PRIME * twice[c]
        )

    await_sent(out1.at[pl.ds(0, LINE - 1)], 0)
    await_sent(turned1.at[pl.ds(0, PLANES - 1)], 1)
    await_sent(out2.at[pl.ds(0, PLANES - 1)], 2)
    await_sent(turned2.at[pl.ds(0, LINE - 1)], 3)
    await_sent(targets.at[pl.ds(0, REPS - 1)], 4)
    await_sent(src_pos.at[pl.ds(0, STOPS - 1)], 5)
    await_sent(src_tan.at[pl.ds(0, STOPS - 1)], 6)
    await_sent(part_out.at[pl.ds(1, REPS - 1)], 7)


def shards(positions, normal_flow, send_owner, send_slot, recv_index, loop_pos, loop_len):
    dma = pltpu.SemaphoreType.DMA
    by_line = pltpu.VMEM((LINE, PLANES, LANES), F32)
    by_plane = pltpu.VMEM((PLANES, LINE, LANES), F32)
    points = pltpu.VMEM((3, PT), F32)
    point_index = pltpu.VMEM((1, PT), I32)
    columns = pltpu.VMEM((COLUMN_ROWS, LANES), I32)
    return pl.pallas_call(
        kernel,
        out_shape=jax.ShapeDtypeStruct((3, PT), F32),
        in_specs=[pl.BlockSpec(memory_space=pltpu.HBM)] * 7,
        out_specs=pl.BlockSpec(memory_space=pltpu.VMEM),
        scratch_shapes=[
            points, points, point_index, point_index, columns, columns, columns,
            by_line, by_line, by_plane, by_plane, by_plane, by_plane, by_line, by_line,
            pltpu.VMEM((REPS, 4, PT), F32),
            pltpu.VMEM((STOPS, 4, PT), F32),
            pltpu.VMEM((STOPS, 4, PT), F32),
            pltpu.VMEM((REPS, FEATURES, PT), BF16),
            pltpu.VMEM((PT, FEATURES), BF16),
            pltpu.VMEM((REPS, STOPS, 2 * PT, PT), BF16),
            pltpu.VMEM((STOPS, 32, 2 * PT), BF16),
            pltpu.VMEM((REPS, 4, PT), F32),
            pltpu.VMEM((REPS, 4, PT), F32),
            pltpu.VMEM((CAP, SLOT_ROWS, LANES), I32),
            pltpu.VMEM((CAP, SLOT_ROWS, LANES), I32),
            pltpu.VMEM((BLOCKS, PT), BF16),
            dma((7,)), pltpu.SemaphoreType.REGULAR((3,)), dma((8,)), dma((4,)), dma((REPS,)), dma((STOPS,)), dma((STOPS,)),
            dma((REPS,)),
        ],
        compiler_params=pltpu.CompilerParams(
            collective_id=0, has_side_effects=True, vmem_limit_bytes=60 * 1024 * 1024
        ),
        cost_estimate=pl.CostEstimate(
            flops=2 * PT * SOURCES * PT * 128, bytes_accessed=1 << 20,
            transcendentals=PT * SOURCES * PT,
        ),
    )(
        positions,
        normal_flow,
        send_owner.reshape(1, PT),
        send_slot.reshape(1, PT),
        recv_index.reshape(CAP, BLOCKS),
        loop_pos.reshape(COLUMN_ROWS, LANES),
        loop_len.reshape(COLUMN_ROWS, LANES),
    )


def solution(mesh):
    both = P(("blk", "rep"))
    wide = P(None, ("blk", "rep"))
    return jax.shard_map(
        shards,
        mesh=mesh,
        in_specs=(wide, wide, both, both, both, both, both),
        out_specs=wide,
        check_vma=False,
    )
```

```python
import functools

import jax
import jax.numpy as jnp
from jax import lax
from jax.experimental import pallas as pl
from jax.experimental.pallas import tpu as pltpu
from jax.sharding import PartitionSpec as P

LOCAL_BETA = 0.3
FRICTION_ALPHA = 0.21
FRICTION_PRIME = 0.06
BIOT_SCALE = 0.01
CORE_SQUARED = 0.25
SPEED_FLOOR = 1.0

BLOCKS = 128
LINE = 8
PLANES = BLOCKS // LINE
REPS = 4
STOPS = 8
BACK = STOPS // 2 - 1
SOURCES = STOPS * REPS
PT = 512
CAP = 10
LANES = 128
COLUMN_ROWS = 10

FEATURES = 64
STOP_ORDER = (0, 4, 3, -3, 2, -2, 1, -1)
LINE_ORDER = (4, 3, 5, 2, 6, 1, 7)
PLANE_ORDER = (10, 9, 11, 6, 14, 7, 13, 2, 8, 5, 15, 3, 1, 4, 12)

MESH = pl.DeviceIdType.MESH
F32 = jnp.float32
BF16 = jnp.bfloat16
I32 = jnp.int32

NT = (((1,), (1,)), ((), ()))
NN = (((1,), (0,)), ((), ()))


def dot(left, right, dims=NN):
    return lax.dot_general(left, right, dims, preferred_element_type=F32)


def rounded(value):
    return value.astype(BF16).astype(F32)


def split(value):
    high = rounded(value)
    rest = value - high
    mid = rounded(rest)
    return high, mid, rest - mid


def iota(shape, dim):
    return lax.broadcasted_iota(I32, shape, dim)


def pick(table, index):
    return jnp.take_along_axis(table, index, axis=1, mode="promise_in_bounds")


def look_up(table, index):
    row, lane = index >> 7, index & 127
    found = jnp.zeros(index.shape, table.dtype)
    for t in range(COLUMN_ROWS):
        piece = jnp.broadcast_to(table[t : t + 1], index.shape)
        found = jnp.where(row == t, pick(piece, lane), found)
    return found


def cross(a, b):
    return [
        a[1] * b[2] - a[2] * b[1],
        a[2] * b[0] - a[0] * b[2],
        a[0] * b[1] - a[1] * b[0],
    ]


def rows_of(value, low, top):
    return [value[c : c + 1] for c in range(low, top)]


def kernel(
    pos_hbm, flow_hbm, owner_hbm, slot_hbm, recv_hbm, order_hbm, count_hbm, out_ref,
    pos_ref, flow_ref, owner_ref, slot_ref, recv_ref, order_ref, count_ref,
    out1, in1, turned1, arrived, out2, in2, turned2, returned,
    targets, src_pos, src_tan, target, features, weights, right, part_out, part_in,
    index, member,
    load_sem, send_sem, phase_sem, rep_sem, pos_sem, tan_sem, part_sem,
):
    me = lax.axis_index("blk")
    rep = lax.axis_index("rep")
    plane = me // LINE
    place = me % LINE

    def on_line(k):
        return (place + k) % LINE

    def on_plane(k):
        return (plane + k) % PLANES

    def on_rep(k):
        return (rep + k) % REPS

    def block(stop):
        return (me + stop + BLOCKS) % BLOCKS

    loads = [
        pltpu.make_async_copy(src, dst, load_sem.at[i])
        for i, (src, dst) in enumerate(
            [
                (pos_hbm, pos_ref), (owner_hbm, owner_ref), (slot_hbm, slot_ref),
                (recv_hbm, recv_ref), (order_hbm, order_ref), (count_hbm, count_ref),
                (flow_hbm, flow_ref),
            ]
        )
    ]
    for load in loads[:3]:
        load.start()

    barrier = pltpu.get_barrier_semaphore()

    def greet(blk, other):
        pl.semaphore_signal(barrier, inc=1, device_id=(blk, other), device_id_type=MESH)

    for k in LINE_ORDER:
        greet(plane * LINE + on_line(k), rep)
    for k in PLANE_ORDER:
        greet(on_plane(k) * LINE + place, rep)
    for k in range(1, REPS):
        greet(me, on_rep(k))
    for stop in STOP_ORDER[1:]:
        greet(block(stop), rep)

    for load in loads[3:]:
        load.start()
    for load in loads[:3]:
        load.wait()

    pos = pos_ref[...]
    owner = owner_ref[...]
    slot = slot_ref[...]
    owner_place, owner_plane = owner & (LINE - 1), owner >> 3
    member_row = (owner_plane >> 3) * 64 + owner_place * 8 + (owner_plane & 7)
    member[...] = jnp.where(iota((BLOCKS, PT), 0) == member_row, 1.0, 0.0).astype(BF16)
    message_row = owner_place * 4 + (owner_plane >> 2)
    to_row = jnp.where(iota((32, PT), 0) == message_row, 1.0, 0.0).astype(BF16)
    lane = iota((LANES, PT), 0)
    value = lane & 31
    component = jnp.where(value < CAP, 0, jnp.where(value < 2 * CAP, 1, 2))
    here = (lane >> 5) * 16 + value - component * CAP == (owner_plane & 3) * 16 + slot
    slotted = jnp.where(component == 0, pos[0:1], jnp.where(component == 1, pos[1:2], pos[2:3]))
    slotted = jnp.where(here, slotted, 0.0)
    outgoing = sum(dot(to_row, part.astype(BF16), NT) for part in split(slotted))
    out1[...] = outgoing.reshape(LINE, PLANES // 4, LANES)
    square = jnp.sum(pos * pos, axis=0, keepdims=True)
    pos_rows = jnp.concatenate([pos, square], axis=0)
    src_pos[BACK] = pos_rows
    targets[rep] = pos_rows

    def copy_to(src, dst, send, recv, blk, other):
        pltpu.make_async_remote_copy(
            src_ref=src, dst_ref=dst, send_sem=send_sem.at[send], recv_sem=recv,
            device_id=(blk, other), device_id_type=MESH,
        ).start()

    def send_line(src, dst, phase):
        for k in LINE_ORDER:
            there = on_line(k)
            copy_to(src.at[there], dst.at[place], phase, phase_sem.at[phase],
                    plane * LINE + there, rep)

    def send_plane(src, dst, phase):
        for k in PLANE_ORDER:
            there = on_plane(k)
            copy_to(src.at[there], dst.at[plane], phase, phase_sem.at[phase],
                    there * LINE + place, rep)

    def await_here(dst, recv):
        pltpu.make_async_remote_copy(
            src_ref=dst, dst_ref=dst, send_sem=send_sem.at[0], recv_sem=recv,
            device_id=(me, rep), device_id_type=MESH,
        ).wait_recv()

    def await_sent(part, send):
        pltpu.make_async_remote_copy(
            src_ref=part, dst_ref=part, send_sem=send_sem.at[send], recv_sem=phase_sem.at[0],
            device_id=(me, rep), device_id_type=MESH,
        ).wait_send()

    ones = jnp.ones((1, PT), F32)
    none = jnp.zeros((3, PT), F32)
    one_row = jnp.concatenate([ones, none], axis=0)

    def aim(other):
        rows = targets[other]
        wanted = jnp.concatenate(
            [-2.0 * rows[0:3], ones, rows[3:4] + CORE_SQUARED, none], axis=0
        )
        th, tm, tl = split(wanted)
        target[other] = jnp.concatenate([th, th, tm, tm, th, tl, tl, tm], axis=0).astype(BF16)

    def describe(stop):
        sh, sm, sl = split(jnp.concatenate([src_pos[stop + BACK], one_row], axis=0))
        rows = jnp.concatenate(
            [sh, sm, sh, sm, sl, sh, sm, sl, jnp.zeros((LANES - FEATURES, PT), F32)], axis=0
        )
        features[...] = rows.T[:, :FEATURES].astype(BF16)

    def weigh(stop, low, top):
        def one(k, carry):
            other = on_rep(k)
            for half in range(PT // 256):
                low, top = half * 256, half * 256 + 256
                root = lax.rsqrt(dot(features[...], target[other, :, low:top]))
                weight = root * root * root
                high = weight.astype(BF16)
                weights[other, stop + BACK, :PT, low:top] = high
                weights[other, stop + BACK, PT:, low:top] = (
                    weight - high.astype(F32)
                ).astype(BF16)
            return carry

        lax.fori_loop(low, top, one, 0)

    def weigh_stops(low, top):
        def one(i, carry):
            stop = (i % 2) * ((i + 1) // 2) - (1 - i % 2) * (i // 2)
            await_here(src_pos.at[stop + BACK], pos_sem.at[stop + BACK])
            describe(stop)
            weigh(stop, 0, REPS)
            return carry

        lax.fori_loop(low, top, one, 0)


    pl.semaphore_wait(barrier, (LINE - 1) + (PLANES - 1) + (REPS - 1) + (STOPS - 1))

    send_line(out1, in1, 0)
    for k in range(1, REPS):
        copy_to(targets.at[rep], targets.at[rep], 4, rep_sem.at[rep], me, on_rep(k))
    in1[place] = out1[place]

    for load in loads[3:]:
        load.wait()
    lane = iota((16, LANES), 1)
    spot = (((lane & 31) >> 1) * LINE + (lane >> 5) * 2 + (lane & 1)) * CAP + iota((16, LANES), 0)
    column = jnp.where(iota((16, LANES), 0) < CAP, look_up(recv_ref[...], spot), -1)
    column_row, column_lane = column >> 7, column & 127
    holder = iota((16, LANES), 1).astype(F32)
    inverse = jnp.zeros((32, LANES), F32)
    for s in range(CAP):
        hit = column_row[s : s + 1] == iota((16, LANES), 0)
        left = jnp.concatenate(
            [jnp.where(hit, holder, 0.0), jnp.where(hit, float(s), 0.0)], axis=0
        ).astype(BF16)
        lane_hit = column_lane[s : s + 1] == iota((LANES, LANES), 0)
        inverse = inverse + dot(left, jnp.where(lane_hit, 1.0, 0.0).astype(BF16), NT)
    inverse = (inverse[16:] * float(LANES) + inverse[:16]).astype(I32)
    at = jnp.maximum(column, 0)
    ring = look_up(order_ref[...] + (count_ref[...] << 11), at)
    order, count = ring & 2047, ring >> 11

    def neighbour(offset):
        moved = order + offset
        moved = jnp.where(moved < 0, moved + count, jnp.where(moved >= count, moved - count, moved))
        there = jnp.clip(at - order + moved, 0, COLUMN_ROWS * LANES - 1)
        return look_up(inverse, there)

    aim(rep)
    describe(0)
    await_here(in1.at[pl.ds(0, LINE - 1)], phase_sem.at[0])
    place_bits, plane_bits = iota((LINE, LANES), 0) >> 1, iota((LINE, LANES), 1) >> 5
    for q in range(PLANES // 4):
        rows = in1[:, q, :]
        down = pltpu.roll(pltpu.roll(rows, LINE - 2, 0), 32, 1)
        up = pltpu.roll(pltpu.roll(rows, 2, 0), LANES - 32, 1)
        rows = jnp.where(
            (place_bits & 1) == (plane_bits & 1), rows, jnp.where((place_bits & 1) == 0, down, up)
        )
        far_rows = pltpu.roll(pltpu.roll(rows, 4, 0), 64, 1)
        rows = jnp.where((place_bits >> 1) == (plane_bits >> 1), rows, far_rows)
        for p in range(4):
            turned1[4 * q + p] = rows[2 * p : 2 * p + 2]
    send_plane(turned1, arrived, 1)
    arrived[plane] = turned1[plane]
    for stop in STOP_ORDER[1:]:
        copy_to(src_pos.at[BACK], src_pos.at[stop + BACK], 5, pos_sem.at[stop + BACK],
                block(-stop), rep)

    ahead1, ahead2, behind1, behind2 = (neighbour(k) for k in (1, 2, -1, -2))
    for i, table in enumerate((ahead1, ahead2, behind1, behind2)):
        index[i] = table
    for k in range(1, REPS):
        await_here(targets.at[on_rep(k)], rep_sem.at[on_rep(k)])
        aim(on_rep(k))
    weigh(0, 0, REPS)

    await_here(arrived.at[pl.ds(0, PLANES - 1)], phase_sem.at[1])
    rows = arrived[...].reshape(2 * PLANES, LANES)
    tables = jnp.concatenate(
        [rows] + [pltpu.roll(rows, LANES - 32 * i, 1) for i in range(1, 4)], axis=0
    ).T
    moved = []
    for i in range(4):
        at_row, at_lane = index[i] >> 7, index[i] & 127
        found = [jnp.zeros((16, LANES), F32) for _ in range(3)]
        for t in range(CAP):
            hit = at_row == t
            for c in range(3):
                table = jnp.broadcast_to(tables[c * CAP + t : c * CAP + t + 1], (16, LANES))
                found[c] = jnp.where(hit, pick(table, at_lane), found[c])
        moved.append(found)
    results = [[], []]
    for c in range(3):
        a1, a2, b1, b2 = (found[c][:CAP] for found in moved)
        center = tables[c * CAP : (c + 1) * CAP]
        results[0].append((8.0 * (a1 - b1) - (a2 - b2)) / 12.0)
        results[1].append((16.0 * (a1 + b1) - (a2 + b2) - 30.0 * center) / 12.0)
    values = jnp.concatenate(
        results[0] + results[1] + [jnp.zeros((64 - 6 * CAP, LANES), F32)], axis=0
    )
    values = jnp.concatenate([values, pltpu.roll(values, 64, 1)], axis=0).T
    for i in range(2):
        out2[:, i] = values[32 * i : 32 * i + 32].reshape(PLANES, 2, LANES)

    send_plane(out2, in2, 2)
    in2[plane] = out2[plane]
    weigh_stops(1, 3)
    await_here(in2.at[pl.ds(0, PLANES - 1)], phase_sem.at[2])
    left_half = iota((8, LANES), 1) < 64
    for i in range(2):
        for j in range(2):
            rows = in2[:, i, j, :]
            a, b = rows[:8], rows[8:]
            turned2[2 * i + j] = jnp.where(left_half, a, pltpu.roll(b, 64, 1))
            turned2[4 + 2 * i + j] = jnp.where(left_half, pltpu.roll(a, 64, 1), b)
    send_line(turned2, returned, 3)
    returned[place] = turned2[place]
    weigh_stops(3, 5)
    await_here(returned.at[pl.ds(0, LINE - 1)], phase_sem.at[3])
    rows = returned[...].reshape(64, LANES)
    back = jnp.concatenate([rows, pltpu.roll(rows, 64, 1)], axis=0).T[:64]
    is_owner = member[...]
    spread = sum(dot(part.astype(BF16), is_owner) for part in split(back))
    derived = []
    for q in range(6):
        chosen = jnp.where(iota((CAP, PT), 0) == slot, spread[q * CAP : (q + 1) * CAP], 0.0)
        derived.append(jnp.sum(chosen, axis=0, keepdims=True))

    src_tan[BACK] = jnp.concatenate(derived[0:3] + [jnp.zeros((1, PT), F32)], axis=0)
    for stop in STOP_ORDER[1:]:
        copy_to(src_tan.at[BACK], src_tan.at[stop + BACK], 6, tan_sem.at[stop + BACK],
                block(-stop), rep)
    weigh_stops(5, STOPS)

    def prepare(stop):
        p, t = rows_of(src_pos[stop], 0, 3), rows_of(src_tan[stop], 0, 3)
        h, m, l = split(jnp.concatenate(t + cross(t, p) + [jnp.zeros((2, PT), F32)], axis=0))
        rows = jnp.concatenate([h, m, l, jnp.zeros((8, PT), F32)], axis=0).astype(BF16)
        right[stop, :, :PT] = rows
        right[stop, :, PT:] = rows

    prepare(BACK)
    for stop in STOP_ORDER[1:]:
        await_here(src_tan.at[stop + BACK], tan_sem.at[stop + BACK])
        prepare(stop + BACK)

    def gather_sums(k):
        other = on_rep(k)

        def some(i, sums):
            for j in range(4):
                sums = sums + dot(right[4 * i + j], weights[other, 4 * i + j])
            return sums

        parts = lax.fori_loop(0, STOPS // 4, some, jnp.zeros((32, PT), F32))
        parts = parts[0:8] + parts[8:16] + parts[16:24]
        far = cross(rows_of(parts, 0, 3), rows_of(targets[other], 0, 3))
        part_out[k % REPS] = jnp.concatenate(
            [far[c] - parts[3 + c : 4 + c] for c in range(3)] + [jnp.zeros((1, PT), F32)], axis=0
        )

    def sums_of(k, carry):
        gather_sums(k)

        @pl.when(k < REPS)
        def _():
            copy_to(part_out.at[k], part_in.at[k], 7, part_sem.at[k], me, on_rep(k))

        return carry

    lax.fori_loop(1, REPS + 1, sums_of, 0)
    for k in range(1, REPS):
        await_here(part_in.at[k], part_sem.at[k])
    others = part_out[0] + part_in[1] + part_in[2] + part_in[3]
    far = [others[c : c + 1] for c in range(3)]

    tangent, curvature = derived[0:3], derived[3:6]
    speed = jnp.maximum(
        tangent[0] * tangent[0] + tangent[1] * tangent[1] + tangent[2] * tangent[2], SPEED_FLOOR
    )
    per_speed = 1.0 / jnp.sqrt(speed)
    scale = LOCAL_BETA * per_speed / speed
    local = cross(tangent, curvature)
    superfluid = [scale * local[c] + BIOT_SCALE * far[c] for c in range(3)]
    unit = [tangent[c] * per_speed for c in range(3)]
    once = cross(unit, [flow_ref[c : c + 1, :] - superfluid[c] for c in range(3)])
    twice = cross(unit, once)
    for c in range(3):
        out_ref[c : c + 1, :] = (
            superfluid[c] + FRICTION_ALPHA * once[c] - FRICTION_PRIME * twice[c]
        )

    await_sent(out1.at[pl.ds(0, LINE - 1)], 0)
    await_sent(turned1.at[pl.ds(0, PLANES - 1)], 1)
    await_sent(out2.at[pl.ds(0, PLANES - 1)], 2)
    await_sent(turned2.at[pl.ds(0, LINE - 1)], 3)
    await_sent(targets.at[pl.ds(0, REPS - 1)], 4)
    await_sent(src_pos.at[pl.ds(0, STOPS - 1)], 5)
    await_sent(src_tan.at[pl.ds(0, STOPS - 1)], 6)
    await_sent(part_out.at[pl.ds(1, REPS - 1)], 7)


def shards(positions, normal_flow, send_owner, send_slot, recv_index, loop_pos, loop_len):
    dma = pltpu.SemaphoreType.DMA
    first = pltpu.VMEM((LINE, PLANES // 4, LANES), F32)
    second = pltpu.VMEM((PLANES, 2, LANES), F32)
    third = pltpu.VMEM((PLANES, 2, 2, LANES), F32)
    fourth = pltpu.VMEM((LINE, 8, LANES), F32)
    points = pltpu.VMEM((3, PT), F32)
    point_index = pltpu.VMEM((1, PT), I32)
    columns = pltpu.VMEM((COLUMN_ROWS, LANES), I32)
    return pl.pallas_call(
        kernel,
        out_shape=jax.ShapeDtypeStruct((3, PT), F32),
        in_specs=[pl.BlockSpec(memory_space=pltpu.HBM)] * 7,
        out_specs=pl.BlockSpec(memory_space=pltpu.VMEM),
        scratch_shapes=[
            points, points, point_index, point_index, columns, columns, columns,
            first, first, second, second, third, third, fourth, fourth,
            pltpu.VMEM((REPS, 4, PT), F32),
            pltpu.VMEM((STOPS, 4, PT), F32),
            pltpu.VMEM((STOPS, 4, PT), F32),
            pltpu.VMEM((REPS, FEATURES, PT), BF16),
            pltpu.VMEM((PT, FEATURES), BF16),
            pltpu.VMEM((REPS, STOPS, 2 * PT, PT), BF16),
            pltpu.VMEM((STOPS, 32, 2 * PT), BF16),
            pltpu.VMEM((REPS, 4, PT), F32),
            pltpu.VMEM((REPS, 4, PT), F32),
            pltpu.VMEM((4, 16, LANES), I32),
            pltpu.VMEM((BLOCKS, PT), BF16),
            dma((7,)), dma((8,)), dma((4,)), dma((REPS,)), dma((STOPS,)), dma((STOPS,)),
            dma((REPS,)),
        ],
        compiler_params=pltpu.CompilerParams(
            collective_id=0, has_side_effects=True, vmem_limit_bytes=60 * 1024 * 1024
        ),
        cost_estimate=pl.CostEstimate(
            flops=2 * PT * SOURCES * PT * 128, bytes_accessed=1 << 20,
            transcendentals=PT * SOURCES * PT,
        ),
    )(
        positions,
        normal_flow,
        send_owner.reshape(1, PT),
        send_slot.reshape(1, PT),
        recv_index.reshape(CAP, BLOCKS),
        loop_pos.reshape(COLUMN_ROWS, LANES),
        loop_len.reshape(COLUMN_ROWS, LANES),
    )


def solution(mesh):
    both = P(("blk", "rep"))
    wide = P(None, ("blk", "rep"))
    return jax.shard_map(
        shards,
        mesh=mesh,
        in_specs=(wide, wide, both, both, both, both, both),
        out_specs=wide,
        check_vma=False,
    )
```

```python
import functools

import jax
import jax.numpy as jnp
from jax import lax
from jax.experimental import pallas as pl
from jax.experimental.pallas import tpu as pltpu
from jax.sharding import PartitionSpec as P

LOCAL_BETA = 0.3
FRICTION_ALPHA = 0.21
FRICTION_PRIME = 0.06
BIOT_SCALE = 0.01
CORE_SQUARED = 0.25
SPEED_FLOOR = 1.0

BLOCKS = 128
LINE = 8
PLANES = BLOCKS // LINE
REPS = 4
STOPS = 8
BACK = STOPS // 2 - 1
SOURCES = STOPS * REPS
PT = 512
CAP = 10
LANES = 128
COLUMN_ROWS = 10

FEATURES = 64
STOP_ORDER = (0, 4, 3, -3, 2, -2, 1, -1)
LINE_ORDER = (4, 3, 5, 2, 6, 1, 7)
PLANE_ORDER = (10, 9, 11, 6, 14, 7, 13, 2, 8, 5, 15, 3, 1, 4, 12)

MESH = pl.DeviceIdType.MESH
F32 = jnp.float32
BF16 = jnp.bfloat16
I32 = jnp.int32

NT = (((1,), (1,)), ((), ()))
NN = (((1,), (0,)), ((), ()))


def dot(left, right, dims=NN):
    return lax.dot_general(left, right, dims, preferred_element_type=F32)


def rounded(value):
    return value.astype(BF16).astype(F32)


def split(value):
    high = rounded(value)
    rest = value - high
    mid = rounded(rest)
    return high, mid, rest - mid


def iota(shape, dim):
    return lax.broadcasted_iota(I32, shape, dim)


def pick(table, index):
    return jnp.take_along_axis(table, index, axis=1, mode="promise_in_bounds")


def look_up(table, index):
    row, lane = index >> 7, index & 127
    found = jnp.zeros(index.shape, table.dtype)
    for t in range(COLUMN_ROWS):
        piece = jnp.broadcast_to(table[t : t + 1], index.shape)
        found = jnp.where(row == t, pick(piece, lane), found)
    return found


def cross(a, b):
    return [
        a[1] * b[2] - a[2] * b[1],
        a[2] * b[0] - a[0] * b[2],
        a[0] * b[1] - a[1] * b[0],
    ]


def rows_of(value, low, top):
    return [value[c : c + 1] for c in range(low, top)]


def kernel(
    pos_hbm, flow_hbm, owner_hbm, slot_hbm, recv_hbm, order_hbm, count_hbm, out_ref,
    pos_ref, flow_ref, owner_ref, slot_ref, recv_ref, order_ref, count_ref,
    out1, in1, turned1, arrived, out2, in2, turned2, returned,
    targets, src_pos, src_tan, target, features, weights, right, own_sums, part_out, part_in,
    index, member,
    load_sem, ready, send_sem, phase_sem, rep_sem, pos_sem, tan_sem, part_sem,
):
    me = lax.axis_index("blk")
    rep = lax.axis_index("rep")
    plane = me // LINE
    place = me % LINE

    def on_line(k):
        return (place + k) % LINE

    def on_plane(k):
        return (plane + k) % PLANES

    def beside_x(k):
        return (plane + 4 * k) % PLANES

    def beside_y(k):
        return plane // 4 * 4 + (plane + k) % 4

    def on_rep(k):
        return (rep + k) % REPS

    def block(stop):
        return (me + stop + BLOCKS) % BLOCKS

    loads = [
        pltpu.make_async_copy(src, dst, load_sem.at[i])
        for i, (src, dst) in enumerate(
            [
                (pos_hbm, pos_ref), (owner_hbm, owner_ref), (slot_hbm, slot_ref),
                (recv_hbm, recv_ref), (order_hbm, order_ref), (count_hbm, count_ref),
                (flow_hbm, flow_ref),
            ]
        )
    ]
    for load in loads[:3]:
        load.start()

    barrier = pltpu.get_barrier_semaphore()

    def greet(blk, other):
        pl.semaphore_signal(barrier, inc=1, device_id=(blk, other), device_id_type=MESH)

    for k in LINE_ORDER:
        greet(plane * LINE + on_line(k), rep)
    for k in range(1, 4):
        greet(beside_x(k) * LINE + place, rep)
        greet(beside_y(k) * LINE + place, rep)
    for k in range(1, REPS):
        greet(me, on_rep(k))
    for stop in STOP_ORDER[1:]:

        @pl.when((place + stop < 0) | (place + stop >= LINE))
        def _():
            greet(block(stop), rep)

    for load in loads[3:]:
        load.start()
    for load in loads[:3]:
        load.wait()

    pos = pos_ref[...]
    owner = owner_ref[...]
    slot = slot_ref[...]
    owner_place, owner_plane = owner & (LINE - 1), owner >> 3
    member_row = (owner_plane >> 3) * 64 + owner_place * 8 + (owner_plane & 7)
    member[...] = jnp.where(iota((BLOCKS, PT), 0) == member_row, 1.0, 0.0).astype(BF16)
    message_row = owner_place * 4 + (owner_plane >> 2)
    to_row = jnp.where(iota((32, PT), 0) == message_row, 1.0, 0.0).astype(BF16)
    lane = iota((LANES, PT), 0)
    value = lane & 31
    component = jnp.where(value < CAP, 0, jnp.where(value < 2 * CAP, 1, 2))
    here = (lane >> 5) * 16 + value - component * CAP == (owner_plane & 3) * 16 + slot
    slotted = jnp.where(component == 0, pos[0:1], jnp.where(component == 1, pos[1:2], pos[2:3]))
    slotted = jnp.where(here, slotted, 0.0)
    outgoing = sum(dot(to_row, part.astype(BF16), NT) for part in split(slotted))
    out1[...] = outgoing.reshape(LINE, PLANES // 4, LANES)
    square = jnp.sum(pos * pos, axis=0, keepdims=True)
    pos_rows = jnp.concatenate([pos, square], axis=0)
    src_pos[BACK] = pos_rows
    targets[rep] = pos_rows

    def copy_to(src, dst, send, recv, blk, other):
        pltpu.make_async_remote_copy(
            src_ref=src, dst_ref=dst, send_sem=send_sem.at[send], recv_sem=recv,
            device_id=(blk, other), device_id_type=MESH,
        ).start()

    def send_line(src, dst, phase):
        for k in LINE_ORDER:
            there = on_line(k)
            copy_to(src.at[there], dst.at[place], phase, phase_sem.at[phase],
                    plane * LINE + there, rep)

    def send_plane(src, dst, phase):
        for k in PLANE_ORDER:
            there = on_plane(k)
            copy_to(src.at[there], dst.at[plane], phase, phase_sem.at[phase],
                    there * LINE + place, rep)

    def await_here(dst, recv):
        pltpu.make_async_remote_copy(
            src_ref=dst, dst_ref=dst, send_sem=send_sem.at[0], recv_sem=recv,
            device_id=(me, rep), device_id_type=MESH,
        ).wait_recv()

    def await_sent(part, send):
        pltpu.make_async_remote_copy(
            src_ref=part, dst_ref=part, send_sem=send_sem.at[send], recv_sem=phase_sem.at[0],
            device_id=(me, rep), device_id_type=MESH,
        ).wait_send()

    ones = jnp.ones((1, PT), F32)
    none = jnp.zeros((3, PT), F32)
    one_row = jnp.concatenate([ones, none], axis=0)

    def aim(other):
        rows = targets[other]
        wanted = jnp.concatenate(
            [-2.0 * rows[0:3], ones, rows[3:4] + CORE_SQUARED, none], axis=0
        )
        th, tm, tl = split(wanted)
        target[other] = jnp.concatenate([th, th, tm, tm, th, tl, tl, tm], axis=0).astype(BF16)

    def describe(stop):
        sh, sm, sl = split(jnp.concatenate([src_pos[stop + BACK], one_row], axis=0))
        rows = jnp.concatenate(
            [sh, sm, sh, sm, sl, sh, sm, sl, jnp.zeros((LANES - FEATURES, PT), F32)], axis=0
        )
        features[...] = rows.T[:, :FEATURES].astype(BF16)

    def weigh(low, top):
        def one(unit, carry):
            i = unit // REPS
            stop = (i % 2) * ((i + 1) // 2) - (1 - i % 2) * (i // 2)
            other = on_rep(unit % REPS)

            @pl.when((unit % REPS == 0) & (i > 0))
            def _():
                await_here(src_pos.at[stop + BACK], pos_sem.at[stop + BACK])

            @pl.when(unit % REPS == 0)
            def _():
                describe(stop)

            for half in range(PT // 256):
                low, top = half * 256, half * 256 + 256
                root = lax.rsqrt(dot(features[...], target[other, :, low:top]))
                weight = root * root * root
                high = weight.astype(BF16)
                weights[other, stop + BACK, :PT, low:top] = high
                weights[other, stop + BACK, PT:, low:top] = (
                    weight - high.astype(F32)
                ).astype(BF16)
            return carry

        lax.fori_loop(low, top, one, 0)

    across = jnp.where(place < STOPS // 2, STOPS // 2 - place, place - STOPS // 2)
    pl.semaphore_wait(barrier, (LINE - 1) + 3 + 3 + (REPS - 1) + across)

    send_line(out1, in1, 0)
    for k in range(1, 4):
        pl.semaphore_signal(
            ready, inc=1, device_id=(beside_x(k) * LINE + place, rep), device_id_type=MESH
        )
    for k in range(1, REPS):
        copy_to(targets.at[rep], targets.at[rep], 4, rep_sem.at[rep], me, on_rep(k))
    in1[place] = out1[place]

    for load in loads[3:]:
        load.wait()
    lane = iota((16, LANES), 1)
    spot = (((lane & 31) >> 1) * LINE + (lane >> 5) * 2 + (lane & 1)) * CAP + iota((16, LANES), 0)
    column = jnp.where(iota((16, LANES), 0) < CAP, look_up(recv_ref[...], spot), -1)
    column_row, column_lane = column >> 7, column & 127
    holder = iota((16, LANES), 1).astype(F32)
    inverse = jnp.zeros((32, LANES), F32)
    for s in range(CAP):
        hit = column_row[s : s + 1] == iota((16, LANES), 0)
        left = jnp.concatenate(
            [jnp.where(hit, holder, 0.0), jnp.where(hit, float(s), 0.0)], axis=0
        ).astype(BF16)
        lane_hit = column_lane[s : s + 1] == iota((LANES, LANES), 0)
        inverse = inverse + dot(left, jnp.where(lane_hit, 1.0, 0.0).astype(BF16), NT)
    inverse = (inverse[16:] * float(LANES) + inverse[:16]).astype(I32)
    at = jnp.maximum(column, 0)
    ring = look_up(order_ref[...] + (count_ref[...] << 11), at)
    order, count = ring & 2047, ring >> 11

    def neighbour(offset):
        moved = order + offset
        moved = jnp.where(moved < 0, moved + count, jnp.where(moved >= count, moved - count, moved))
        there = jnp.clip(at - order + moved, 0, COLUMN_ROWS * LANES - 1)
        return look_up(inverse, there)

    ahead1, ahead2, behind1, behind2 = (neighbour(k) for k in (1, 2, -1, -2))
    for i, table in enumerate((ahead1, ahead2, behind1, behind2)):
        index[i] = table
    aim(rep)
    weigh(0, 1)
    await_here(in1.at[pl.ds(0, LINE - 1)], phase_sem.at[0])
    place_bits, plane_bits = iota((LINE, LANES), 0) >> 1, iota((LINE, LANES), 1) >> 5
    for q in range(PLANES // 4):
        rows = in1[:, q, :]
        down = pltpu.roll(pltpu.roll(rows, LINE - 2, 0), 32, 1)
        up = pltpu.roll(pltpu.roll(rows, 2, 0), LANES - 32, 1)
        rows = jnp.where(
            (place_bits & 1) == (plane_bits & 1), rows, jnp.where((place_bits & 1) == 0, down, up)
        )
        far_rows = pltpu.roll(pltpu.roll(rows, 4, 0), 64, 1)
        rows = jnp.where((place_bits >> 1) == (plane_bits >> 1), rows, far_rows)
        for p in range(4):
            turned1[4 * q + p] = rows[2 * p : 2 * p + 2]
    pl.semaphore_wait(ready, 3)
    send_plane(turned1, arrived, 1)
    arrived[plane] = turned1[plane]
    for stop in STOP_ORDER[1:]:
        copy_to(src_pos.at[BACK], src_pos.at[stop + BACK], 5, pos_sem.at[stop + BACK],
                block(-stop), rep)

    for k in range(1, REPS):
        await_here(targets.at[on_rep(k)], rep_sem.at[on_rep(k)])
        aim(on_rep(k))
    weigh(1, 4)

    await_here(arrived.at[pl.ds(0, PLANES - 1)], phase_sem.at[1])
    rows = arrived[...].reshape(2 * PLANES, LANES)
    tables = jnp.concatenate(
        [rows] + [pltpu.roll(rows, LANES - 32 * i, 1) for i in range(1, 4)], axis=0
    ).T
    moved = []
    for i in range(4):
        at_row, at_lane = index[i] >> 7, index[i] & 127
        found = [jnp.zeros((16, LANES), F32) for _ in range(3)]
        for t in range(CAP):
            hit = at_row == t
            for c in range(3):
                table = jnp.broadcast_to(tables[c * CAP + t : c * CAP + t + 1], (16, LANES))
                found[c] = jnp.where(hit, pick(table, at_lane), found[c])
        moved.append(found)
    results = [[], []]
    for c in range(3):
        a1, a2, b1, b2 = (found[c][:CAP] for found in moved)
        center = tables[c * CAP : (c + 1) * CAP]
        results[0].append((8.0 * (a1 - b1) - (a2 - b2)) / 12.0)
        results[1].append((16.0 * (a1 + b1) - (a2 + b2) - 30.0 * center) / 12.0)
    values = jnp.concatenate(
        results[0] + results[1] + [jnp.zeros((64 - 6 * CAP, LANES), F32)], axis=0
    )
    values = jnp.concatenate([values, pltpu.roll(values, 64, 1)], axis=0).T
    for i in range(2):
        out2[:, i] = values[32 * i : 32 * i + 32].reshape(PLANES, 2, LANES)

    send_plane(out2, in2, 2)
    in2[plane] = out2[plane]
    weigh(4, 14)
    await_here(in2.at[pl.ds(0, PLANES - 1)], phase_sem.at[2])
    left_half = iota((8, LANES), 1) < 64
    for i in range(2):
        for j in range(2):
            rows = in2[:, i, j, :]
            a, b = rows[:8], rows[8:]
            turned2[2 * i + j] = jnp.where(left_half, a, pltpu.roll(b, 64, 1))
            turned2[4 + 2 * i + j] = jnp.where(left_half, pltpu.roll(a, 64, 1), b)
    send_line(turned2, returned, 3)
    returned[place] = turned2[place]
    weigh(14, 24)
    await_here(returned.at[pl.ds(0, LINE - 1)], phase_sem.at[3])
    rows = returned[...].reshape(64, LANES)
    back = jnp.concatenate([rows, pltpu.roll(rows, 64, 1)], axis=0).T[:64]
    is_owner = member[...]
    spread = sum(dot(part.astype(BF16), is_owner) for part in split(back))
    derived = []
    for q in range(6):
        chosen = jnp.where(iota((CAP, PT), 0) == slot, spread[q * CAP : (q + 1) * CAP], 0.0)
        derived.append(jnp.sum(chosen, axis=0, keepdims=True))

    src_tan[BACK] = jnp.concatenate(derived[0:3] + [jnp.zeros((1, PT), F32)], axis=0)
    for stop in STOP_ORDER[1:]:
        copy_to(src_tan.at[BACK], src_tan.at[stop + BACK], 6, tan_sem.at[stop + BACK],
                block(-stop), rep)
    weigh(24, SOURCES)

    def prepare(stop):
        p, t = rows_of(src_pos[stop], 0, 3), rows_of(src_tan[stop], 0, 3)
        h, m, l = split(jnp.concatenate(t + cross(t, p) + [jnp.zeros((2, PT), F32)], axis=0))
        rows = jnp.concatenate([h, m, l, jnp.zeros((8, PT), F32)], axis=0).astype(BF16)
        right[stop, :, :PT] = rows
        right[stop, :, PT:] = rows

    prepare(BACK)
    for k in range(REPS):
        own_sums[k] = dot(right[BACK], weights[k, BACK])
    for stop in STOP_ORDER[1:]:
        await_here(src_tan.at[stop + BACK], tan_sem.at[stop + BACK])
        prepare(stop + BACK)

    def gather_sums(k):
        other = on_rep(k)

        parts = own_sums[other]
        for stop in STOP_ORDER[:0:-1]:
            parts = parts + dot(right[stop + BACK], weights[other, stop + BACK])
        parts = parts[0:8] + parts[8:16] + parts[16:24]
        far = cross(rows_of(parts, 0, 3), rows_of(targets[other], 0, 3))
        part_out[k % REPS] = jnp.concatenate(
            [far[c] - parts[3 + c : 4 + c] for c in range(3)] + [jnp.zeros((1, PT), F32)], axis=0
        )

    def sums_of(k, carry):
        gather_sums(k)

        @pl.when(k < REPS)
        def _():
            copy_to(part_out.at[k], part_in.at[k], 7, part_sem.at[k], me, on_rep(k))

        return carry

    lax.fori_loop(1, REPS + 1, sums_of, 0)
    for k in range(1, REPS):
        await_here(part_in.at[k], part_sem.at[k])
    others = part_out[0] + part_in[1] + part_in[2] + part_in[3]
    far = [others[c : c + 1] for c in range(3)]

    tangent, curvature = derived[0:3], derived[3:6]
    speed = jnp.maximum(
        tangent[0] * tangent[0] + tangent[1] * tangent[1] + tangent[2] * tangent[2], SPEED_FLOOR
    )
    per_speed = 1.0 / jnp.sqrt(speed)
    scale = LOCAL_BETA * per_speed / speed
    local = cross(tangent, curvature)
    superfluid = [scale * local[c] + BIOT_SCALE * far[c] for c in range(3)]
    unit = [tangent[c] * per_speed for c in range(3)]
    once = cross(unit, [flow_ref[c : c + 1, :] - superfluid[c] for c in range(3)])
    twice = cross(unit, once)
    for c in range(3):
        out_ref[c : c + 1, :] = (
            superfluid[c] + FRICTION_ALPHA * once[c] - FRICTION_PRIME * twice[c]
        )

    await_sent(out1.at[pl.ds(0, LINE - 1)], 0)
    await_sent(turned1.at[pl.ds(0, PLANES - 1)], 1)
    await_sent(out2.at[pl.ds(0, PLANES - 1)], 2)
    await_sent(turned2.at[pl.ds(0, LINE - 1)], 3)
    await_sent(targets.at[pl.ds(0, REPS - 1)], 4)
    await_sent(src_pos.at[pl.ds(0, STOPS - 1)], 5)
    await_sent(src_tan.at[pl.ds(0, STOPS - 1)], 6)
    await_sent(part_out.at[pl.ds(1, REPS - 1)], 7)


def shards(positions, normal_flow, send_owner, send_slot, recv_index, loop_pos, loop_len):
    dma = pltpu.SemaphoreType.DMA
    first = pltpu.VMEM((LINE, PLANES // 4, LANES), F32)
    second = pltpu.VMEM((PLANES, 2, LANES), F32)
    third = pltpu.VMEM((PLANES, 2, 2, LANES), F32)
    fourth = pltpu.VMEM((LINE, 8, LANES), F32)
    points = pltpu.VMEM((3, PT), F32)
    point_index = pltpu.VMEM((1, PT), I32)
    columns = pltpu.VMEM((COLUMN_ROWS, LANES), I32)
    return pl.pallas_call(
        kernel,
        out_shape=jax.ShapeDtypeStruct((3, PT), F32),
        in_specs=[pl.BlockSpec(memory_space=pltpu.HBM)] * 7,
        out_specs=pl.BlockSpec(memory_space=pltpu.VMEM),
        scratch_shapes=[
            points, points, point_index, point_index, columns, columns, columns,
            first, first, second, second, third, third, fourth, fourth,
            pltpu.VMEM((REPS, 4, PT), F32),
            pltpu.VMEM((STOPS, 4, PT), F32),
            pltpu.VMEM((STOPS, 4, PT), F32),
            pltpu.VMEM((REPS, FEATURES, PT), BF16),
            pltpu.VMEM((PT, FEATURES), BF16),
            pltpu.VMEM((REPS, STOPS, 2 * PT, PT), BF16),
            pltpu.VMEM((STOPS, 32, 2 * PT), BF16),
            pltpu.VMEM((REPS, 32, PT), F32),
            pltpu.VMEM((REPS, 4, PT), F32),
            pltpu.VMEM((REPS, 4, PT), F32),
            pltpu.VMEM((4, 16, LANES), I32),
            pltpu.VMEM((BLOCKS, PT), BF16),
            dma((7,)), pltpu.SemaphoreType.REGULAR, dma((8,)), dma((4,)), dma((REPS,)), dma((STOPS,)), dma((STOPS,)),
            dma((REPS,)),
        ],
        compiler_params=pltpu.CompilerParams(
            collective_id=0, has_side_effects=True, vmem_limit_bytes=48 * 1024 * 1024
        ),
        cost_estimate=pl.CostEstimate(
            flops=2 * PT * SOURCES * PT * 128, bytes_accessed=1 << 20,
            transcendentals=PT * SOURCES * PT,
        ),
    )(
        *(
            pltpu.with_memory_space_constraint(operand, pltpu.HBM)
            for operand in (
                positions,
                normal_flow,
                send_owner.reshape(1, PT),
                send_slot.reshape(1, PT),
                recv_index.reshape(CAP, BLOCKS),
                loop_pos.reshape(COLUMN_ROWS, LANES),
                loop_len.reshape(COLUMN_ROWS, LANES),
            )
        )
    )


def solution(mesh):
    both = P(("blk", "rep"))
    wide = P(None, ("blk", "rep"))
    return jax.shard_map(
        shards,
        mesh=mesh,
        in_specs=(wide, wide, both, both, both, both, both),
        out_specs=wide,
        check_vma=False,
    )
```

```python
import functools

import jax
import jax.numpy as jnp
from jax import lax
from jax.experimental import pallas as pl
from jax.experimental.pallas import tpu as pltpu
from jax.sharding import PartitionSpec as P

LOCAL_BETA = 0.3
FRICTION_ALPHA = 0.21
FRICTION_PRIME = 0.06
BIOT_SCALE = 0.01
CORE_SQUARED = 0.25
SPEED_FLOOR = 1.0

BLOCKS = 128
LINE = 8
PLANES = BLOCKS // LINE
REPS = 4
STOPS = 8
BACK = STOPS // 2 - 1
SOURCES = STOPS * REPS
PT = 512
CAP = 10
LANES = 128
COLUMN_ROWS = 10

FEATURES = 64
STOP_ORDER = (0, 4, 3, -3, 2, -2, 1, -1)
LINE_ORDER = (4, 3, 5, 2, 6, 1, 7)
PLANE_ORDER = (10, 9, 11, 6, 14, 7, 13, 2, 8, 5, 15, 3, 1, 4, 12)

MESH = pl.DeviceIdType.MESH
F32 = jnp.float32
BF16 = jnp.bfloat16
I32 = jnp.int32

NT = (((1,), (1,)), ((), ()))
NN = (((1,), (0,)), ((), ()))


def dot(left, right, dims=NN):
    return lax.dot_general(left, right, dims, preferred_element_type=F32)


def rounded(value):
    return value.astype(BF16).astype(F32)


def split(value):
    high = rounded(value)
    rest = value - high
    mid = rounded(rest)
    return high, mid, rest - mid


def iota(shape, dim):
    return lax.broadcasted_iota(I32, shape, dim)


def pick(table, index):
    return jnp.take_along_axis(table, index, axis=1, mode="promise_in_bounds")


def look_up(table, index):
    row, lane = index >> 7, index & 127
    found = jnp.zeros(index.shape, table.dtype)
    for t in range(COLUMN_ROWS):
        piece = jnp.broadcast_to(table[t : t + 1], index.shape)
        found = jnp.where(row == t, pick(piece, lane), found)
    return found


def cross(a, b):
    return [
        a[1] * b[2] - a[2] * b[1],
        a[2] * b[0] - a[0] * b[2],
        a[0] * b[1] - a[1] * b[0],
    ]


def rows_of(value, low, top):
    return [value[c : c + 1] for c in range(low, top)]


def kernel(
    pos_hbm, flow_hbm, owner_hbm, slot_hbm, recv_hbm, order_hbm, count_hbm, out_ref,
    pos_ref, flow_ref, owner_ref, slot_ref, recv_ref, order_ref, count_ref,
    out1, in1, turned1, arrived, out2, in2, turned2, returned,
    targets, src_pos, src_tan, target, features, weights, weights_a, weights_b, right, own_sums, part_out, part_in,
    index, member,
    load_sem, ready, send_sem, phase_sem, rep_sem, pos_sem, tan_sem, part_sem,
):
    me = lax.axis_index("blk")
    rep = lax.axis_index("rep")
    plane = me // LINE
    place = me % LINE

    def on_line(k):
        return (place + k) % LINE

    def on_plane(k):
        return (plane + k) % PLANES

    def beside_x(k):
        return (plane + 4 * k) % PLANES

    def beside_y(k):
        return plane // 4 * 4 + (plane + k) % 4

    def on_rep(k):
        return (rep + k) % REPS

    def block(stop):
        return (me + stop + BLOCKS) % BLOCKS

    loads = [
        pltpu.make_async_copy(src, dst, load_sem.at[i])
        for i, (src, dst) in enumerate(
            [
                (pos_hbm, pos_ref), (owner_hbm, owner_ref), (slot_hbm, slot_ref),
                (recv_hbm, recv_ref), (order_hbm, order_ref), (count_hbm, count_ref),
                (flow_hbm, flow_ref),
            ]
        )
    ]
    for load in loads[:3]:
        load.start()

    barrier = pltpu.get_barrier_semaphore()

    def greet(blk, other):
        pl.semaphore_signal(barrier, inc=1, device_id=(blk, other), device_id_type=MESH)

    for k in LINE_ORDER:
        greet(plane * LINE + on_line(k), rep)
    for k in range(1, 4):
        greet(beside_x(k) * LINE + place, rep)
        greet(beside_y(k) * LINE + place, rep)
    for k in range(1, REPS):
        greet(me, on_rep(k))
    for stop in STOP_ORDER[1:]:

        @pl.when((place + stop < 0) | (place + stop >= LINE))
        def _():
            greet(block(stop), rep)

    for load in loads[3:]:
        load.start()
    for load in loads[:3]:
        load.wait()

    pos = pos_ref[...]
    owner = owner_ref[...]
    slot = slot_ref[...]
    owner_place, owner_plane = owner & (LINE - 1), owner >> 3
    member_row = (owner_plane >> 3) * 64 + owner_place * 8 + (owner_plane & 7)
    member[...] = jnp.where(iota((BLOCKS, PT), 0) == member_row, 1.0, 0.0).astype(BF16)
    message_row = owner_place * 4 + (owner_plane >> 2)
    to_row = jnp.where(iota((32, PT), 0) == message_row, 1.0, 0.0).astype(BF16)
    lane = iota((LANES, PT), 0)
    value = lane & 31
    component = jnp.where(value < CAP, 0, jnp.where(value < 2 * CAP, 1, 2))
    here = (lane >> 5) * 16 + value - component * CAP == (owner_plane & 3) * 16 + slot
    slotted = jnp.where(component == 0, pos[0:1], jnp.where(component == 1, pos[1:2], pos[2:3]))
    slotted = jnp.where(here, slotted, 0.0)
    outgoing = sum(dot(to_row, part.astype(BF16), NT) for part in split(slotted))
    out1[...] = outgoing.reshape(LINE, PLANES // 4, LANES)
    square = jnp.sum(pos * pos, axis=0, keepdims=True)
    pos_rows = jnp.concatenate([pos, square], axis=0)
    src_pos[BACK] = pos_rows
    targets[rep] = pos_rows

    def copy_to(src, dst, send, recv, blk, other):
        pltpu.make_async_remote_copy(
            src_ref=src, dst_ref=dst, send_sem=send_sem.at[send], recv_sem=recv,
            device_id=(blk, other), device_id_type=MESH,
        ).start()

    def send_line(src, dst, phase):
        for k in LINE_ORDER:
            there = on_line(k)
            copy_to(src.at[there], dst.at[place], phase, phase_sem.at[phase],
                    plane * LINE + there, rep)

    def send_plane(src, dst, phase):
        for k in PLANE_ORDER:
            there = on_plane(k)
            copy_to(src.at[there], dst.at[plane], phase, phase_sem.at[phase],
                    there * LINE + place, rep)

    def await_here(dst, recv):
        pltpu.make_async_remote_copy(
            src_ref=dst, dst_ref=dst, send_sem=send_sem.at[0], recv_sem=recv,
            device_id=(me, rep), device_id_type=MESH,
        ).wait_recv()

    def await_sent(part, send):
        pltpu.make_async_remote_copy(
            src_ref=part, dst_ref=part, send_sem=send_sem.at[send], recv_sem=phase_sem.at[0],
            device_id=(me, rep), device_id_type=MESH,
        ).wait_send()

    ones = jnp.ones((1, PT), F32)
    none = jnp.zeros((3, PT), F32)
    one_row = jnp.concatenate([ones, none], axis=0)

    def aim(other):
        rows = targets[other]
        wanted = jnp.concatenate(
            [-2.0 * rows[0:3], ones, rows[3:4] + CORE_SQUARED, none], axis=0
        )
        th, tm, tl = split(wanted)
        target[other] = jnp.concatenate([th, th, tm, tm, th, tl, tl, tm], axis=0).astype(BF16)

    def describe(stop):
        sh, sm, sl = split(jnp.concatenate([src_pos[stop + BACK], one_row], axis=0))
        rows = jnp.concatenate(
            [sh, sm, sh, sm, sl, sh, sm, sl, jnp.zeros((LANES - FEATURES, PT), F32)], axis=0
        )
        features[...] = rows.T[:, :FEATURES].astype(BF16)

    def weigh(stop, held, beside=None):
        describe(stop)
        for other in range(REPS):
            for half in range(PT // 256):
                low, top = half * 256, half * 256 + 256
                root = lax.rsqrt(dot(features[...], target[other, :, low:top]))
                weight = root * root * root
                high = weight.astype(BF16)
                held[other, :PT, low:top] = high
                held[other, PT:, low:top] = (weight - high.astype(F32)).astype(BF16)
            if beside is not None:
                beside(other)

    def await_pos(stop):
        await_here(src_pos.at[stop + BACK], pos_sem.at[stop + BACK])

    def weigh_stops(low, top):
        def one(i, carry):
            stop = (i % 2) * ((i + 1) // 2) - (1 - i % 2) * (i // 2)
            await_pos(stop)
            weigh(stop, weights.at[stop + BACK - 1])
            return carry

        lax.fori_loop(low, top, one, 0)

    across = jnp.where(place < STOPS // 2, STOPS // 2 - place, place - STOPS // 2)
    pl.semaphore_wait(barrier, (LINE - 1) + 3 + 3 + (REPS - 1) + across)

    send_line(out1, in1, 0)
    for k in range(1, 4):
        pl.semaphore_signal(
            ready, inc=1, device_id=(beside_x(k) * LINE + place, rep), device_id_type=MESH
        )
    for k in range(1, REPS):
        copy_to(targets.at[rep], targets.at[rep], 4, rep_sem.at[rep], me, on_rep(k))
    in1[place] = out1[place]

    for load in loads[3:]:
        load.wait()
    lane = iota((16, LANES), 1)
    spot = (((lane & 31) >> 1) * LINE + (lane >> 5) * 2 + (lane & 1)) * CAP + iota((16, LANES), 0)
    column = jnp.where(iota((16, LANES), 0) < CAP, look_up(recv_ref[...], spot), -1)
    column_row, column_lane = column >> 7, column & 127
    holder = iota((16, LANES), 1).astype(F32)
    inverse = jnp.zeros((32, LANES), F32)
    for s in range(CAP):
        hit = column_row[s : s + 1] == iota((16, LANES), 0)
        left = jnp.concatenate(
            [jnp.where(hit, holder, 0.0), jnp.where(hit, float(s), 0.0)], axis=0
        ).astype(BF16)
        lane_hit = column_lane[s : s + 1] == iota((LANES, LANES), 0)
        inverse = inverse + dot(left, jnp.where(lane_hit, 1.0, 0.0).astype(BF16), NT)
    inverse = (inverse[16:] * float(LANES) + inverse[:16]).astype(I32)
    at = jnp.maximum(column, 0)
    ring = look_up(order_ref[...] + (count_ref[...] << 11), at)
    order, count = ring & 2047, ring >> 11

    def neighbour(offset):
        moved = order + offset
        moved = jnp.where(moved < 0, moved + count, jnp.where(moved >= count, moved - count, moved))
        there = jnp.clip(at - order + moved, 0, COLUMN_ROWS * LANES - 1)
        return look_up(inverse, there)

    ahead1, ahead2, behind1, behind2 = (neighbour(k) for k in (1, 2, -1, -2))
    for i, table in enumerate((ahead1, ahead2, behind1, behind2)):
        index[i] = table
    aim(rep)
    await_here(in1.at[pl.ds(0, LINE - 1)], phase_sem.at[0])
    place_bits, plane_bits = iota((LINE, LANES), 0) >> 1, iota((LINE, LANES), 1) >> 5
    for q in range(PLANES // 4):
        rows = in1[:, q, :]
        down = pltpu.roll(pltpu.roll(rows, LINE - 2, 0), 32, 1)
        up = pltpu.roll(pltpu.roll(rows, 2, 0), LANES - 32, 1)
        rows = jnp.where(
            (place_bits & 1) == (plane_bits & 1), rows, jnp.where((place_bits & 1) == 0, down, up)
        )
        far_rows = pltpu.roll(pltpu.roll(rows, 4, 0), 64, 1)
        rows = jnp.where((place_bits >> 1) == (plane_bits >> 1), rows, far_rows)
        for p in range(4):
            turned1[4 * q + p] = rows[2 * p : 2 * p + 2]
    pl.semaphore_wait(ready, 3)
    send_plane(turned1, arrived, 1)
    arrived[plane] = turned1[plane]
    for stop in STOP_ORDER[1:]:
        copy_to(src_pos.at[BACK], src_pos.at[stop + BACK], 5, pos_sem.at[stop + BACK],
                block(-stop), rep)

    for k in range(1, REPS):
        await_here(targets.at[on_rep(k)], rep_sem.at[on_rep(k)])
        aim(on_rep(k))
    weigh(0, weights.at[BACK - 1])

    await_here(arrived.at[pl.ds(0, PLANES - 1)], phase_sem.at[1])
    rows = arrived[...].reshape(2 * PLANES, LANES)
    tables = jnp.concatenate(
        [rows] + [pltpu.roll(rows, LANES - 32 * i, 1) for i in range(1, 4)], axis=0
    ).T
    moved = []
    for i in range(4):
        at_row, at_lane = index[i] >> 7, index[i] & 127
        found = [jnp.zeros((16, LANES), F32) for _ in range(3)]
        for t in range(CAP):
            hit = at_row == t
            for c in range(3):
                table = jnp.broadcast_to(tables[c * CAP + t : c * CAP + t + 1], (16, LANES))
                found[c] = jnp.where(hit, pick(table, at_lane), found[c])
        moved.append(found)
    results = [[], []]
    for c in range(3):
        a1, a2, b1, b2 = (found[c][:CAP] for found in moved)
        center = tables[c * CAP : (c + 1) * CAP]
        results[0].append((8.0 * (a1 - b1) - (a2 - b2)) / 12.0)
        results[1].append((16.0 * (a1 + b1) - (a2 + b2) - 30.0 * center) / 12.0)
    values = jnp.concatenate(
        results[0] + results[1] + [jnp.zeros((64 - 6 * CAP, LANES), F32)], axis=0
    )
    values = jnp.concatenate([values, pltpu.roll(values, 64, 1)], axis=0).T
    for i in range(2):
        out2[:, i] = values[32 * i : 32 * i + 32].reshape(PLANES, 2, LANES)

    send_plane(out2, in2, 2)
    in2[plane] = out2[plane]
    weigh_stops(1, 3)
    await_here(in2.at[pl.ds(0, PLANES - 1)], phase_sem.at[2])
    left_half = iota((8, LANES), 1) < 64
    for i in range(2):
        for j in range(2):
            rows = in2[:, i, j, :]
            a, b = rows[:8], rows[8:]
            turned2[2 * i + j] = jnp.where(left_half, a, pltpu.roll(b, 64, 1))
            turned2[4 + 2 * i + j] = jnp.where(left_half, pltpu.roll(a, 64, 1), b)
    send_line(turned2, returned, 3)
    returned[place] = turned2[place]
    weigh_stops(3, 5)
    await_here(returned.at[pl.ds(0, LINE - 1)], phase_sem.at[3])
    rows = returned[...].reshape(64, LANES)
    back = jnp.concatenate([rows, pltpu.roll(rows, 64, 1)], axis=0).T[:64]
    is_owner = member[...]
    spread = sum(dot(part.astype(BF16), is_owner) for part in split(back))
    derived = []
    for q in range(6):
        chosen = jnp.where(iota((CAP, PT), 0) == slot, spread[q * CAP : (q + 1) * CAP], 0.0)
        derived.append(jnp.sum(chosen, axis=0, keepdims=True))

    src_tan[BACK] = jnp.concatenate(derived[0:3] + [jnp.zeros((1, PT), F32)], axis=0)
    for stop in STOP_ORDER[1:]:
        copy_to(src_tan.at[BACK], src_tan.at[stop + BACK], 6, tan_sem.at[stop + BACK],
                block(-stop), rep)

    def prepare(stop):
        p, t = rows_of(src_pos[stop], 0, 3), rows_of(src_tan[stop], 0, 3)
        h, m, l = split(jnp.concatenate(t + cross(t, p) + [jnp.zeros((2, PT), F32)], axis=0))
        rows = jnp.concatenate([h, m, l, jnp.zeros((8, PT), F32)], axis=0).astype(BF16)
        right[stop, :, :PT] = rows
        right[stop, :, PT:] = rows

    def held_of(stop):
        return weights_a if stop == -3 else weights_b if stop == 4 else weights.at[stop + BACK - 1]

    def add_sums(stops):
        def one(other):
            sums = [dot(right[stop + BACK], held_of(stop)[other]) for stop in stops]
            sums = functools.reduce(jnp.add, sums)
            own_sums[other] = sums if 0 in stops else own_sums[other] + sums

        return one

    def receive(stops):
        for stop in stops:
            await_here(src_tan.at[stop + BACK], tan_sem.at[stop + BACK])
            prepare(stop + BACK)

    prepare(BACK)
    await_pos(3)
    weigh(3, weights.at[3 + BACK - 1], add_sums([0]))
    await_pos(-3)
    receive([1, -1, 2])
    weigh(-3, weights_a, add_sums([1, -1, 2]))
    await_pos(4)
    receive([-2, 3])
    weigh(4, weights_b, add_sums([-2, 3]))
    receive([-3, 4])

    def gather_sums(k):
        other = on_rep(k)
        parts = (
            own_sums[other]
            + dot(right[BACK - 3], weights_a[other])
            + dot(right[BACK + 4], weights_b[other])
        )
        parts = parts[0:8] + parts[8:16] + parts[16:24]
        far = cross(rows_of(parts, 0, 3), rows_of(targets[other], 0, 3))
        part_out[k % REPS] = jnp.concatenate(
            [far[c] - parts[3 + c : 4 + c] for c in range(3)] + [jnp.zeros((1, PT), F32)], axis=0
        )

    def sums_of(k, carry):
        gather_sums(k)

        @pl.when(k < REPS)
        def _():
            copy_to(part_out.at[k], part_in.at[k], 7, part_sem.at[k], me, on_rep(k))

        return carry

    lax.fori_loop(1, REPS + 1, sums_of, 0)
    for k in range(1, REPS):
        await_here(part_in.at[k], part_sem.at[k])
    others = part_out[0] + part_in[1] + part_in[2] + part_in[3]
    far = [others[c : c + 1] for c in range(3)]

    tangent, curvature = derived[0:3], derived[3:6]
    speed = jnp.maximum(
        tangent[0] * tangent[0] + tangent[1] * tangent[1] + tangent[2] * tangent[2], SPEED_FLOOR
    )
    per_speed = 1.0 / jnp.sqrt(speed)
    scale = LOCAL_BETA * per_speed / speed
    local = cross(tangent, curvature)
    superfluid = [scale * local[c] + BIOT_SCALE * far[c] for c in range(3)]
    unit = [tangent[c] * per_speed for c in range(3)]
    once = cross(unit, [flow_ref[c : c + 1, :] - superfluid[c] for c in range(3)])
    twice = cross(unit, once)
    for c in range(3):
        out_ref[c : c + 1, :] = (
            superfluid[c] + FRICTION_ALPHA * once[c] - FRICTION_PRIME * twice[c]
        )

    await_sent(out1.at[pl.ds(0, LINE - 1)], 0)
    await_sent(turned1.at[pl.ds(0, PLANES - 1)], 1)
    await_sent(out2.at[pl.ds(0, PLANES - 1)], 2)
    await_sent(turned2.at[pl.ds(0, LINE - 1)], 3)
    await_sent(targets.at[pl.ds(0, REPS - 1)], 4)
    await_sent(src_pos.at[pl.ds(0, STOPS - 1)], 5)
    await_sent(src_tan.at[pl.ds(0, STOPS - 1)], 6)
    await_sent(part_out.at[pl.ds(1, REPS - 1)], 7)


def shards(positions, normal_flow, send_owner, send_slot, recv_index, loop_pos, loop_len):
    dma = pltpu.SemaphoreType.DMA
    first = pltpu.VMEM((LINE, PLANES // 4, LANES), F32)
    second = pltpu.VMEM((PLANES, 2, LANES), F32)
    third = pltpu.VMEM((PLANES, 2, 2, LANES), F32)
    fourth = pltpu.VMEM((LINE, 8, LANES), F32)
    points = pltpu.VMEM((3, PT), F32)
    point_index = pltpu.VMEM((1, PT), I32)
    columns = pltpu.VMEM((COLUMN_ROWS, LANES), I32)
    return pl.pallas_call(
        kernel,
        out_shape=jax.ShapeDtypeStruct((3, PT), F32),
        in_specs=[pl.BlockSpec(memory_space=pltpu.HBM)] * 7,
        out_specs=pl.BlockSpec(memory_space=pltpu.VMEM),
        scratch_shapes=[
            points, points, point_index, point_index, columns, columns, columns,
            first, first, second, second, third, third, fourth, fourth,
            pltpu.VMEM((REPS, 4, PT), F32),
            pltpu.VMEM((STOPS, 4, PT), F32),
            pltpu.VMEM((STOPS, 4, PT), F32),
            pltpu.VMEM((REPS, FEATURES, PT), BF16),
            pltpu.VMEM((PT, FEATURES), BF16),
            pltpu.VMEM((STOPS - 2, REPS, 2 * PT, PT), BF16),
            pltpu.VMEM((REPS, 2 * PT, PT), BF16),
            pltpu.VMEM((REPS, 2 * PT, PT), BF16),
            pltpu.VMEM((STOPS, 32, 2 * PT), BF16),
            pltpu.VMEM((REPS, 32, PT), F32),
            pltpu.VMEM((REPS, 4, PT), F32),
            pltpu.VMEM((REPS, 4, PT), F32),
            pltpu.VMEM((4, 16, LANES), I32),
            pltpu.VMEM((BLOCKS, PT), BF16),
            dma((7,)), pltpu.SemaphoreType.REGULAR, dma((8,)), dma((4,)), dma((REPS,)), dma((STOPS,)), dma((STOPS,)),
            dma((REPS,)),
        ],
        compiler_params=pltpu.CompilerParams(
            collective_id=0, has_side_effects=True, vmem_limit_bytes=48 * 1024 * 1024
        ),
        cost_estimate=pl.CostEstimate(
            flops=2 * PT * SOURCES * PT * 128, bytes_accessed=1 << 20,
            transcendentals=PT * SOURCES * PT,
        ),
    )(
        *(
            pltpu.with_memory_space_constraint(operand, pltpu.HBM)
            for operand in (
                positions,
                normal_flow,
                send_owner.reshape(1, PT),
                send_slot.reshape(1, PT),
                recv_index.reshape(CAP, BLOCKS),
                loop_pos.reshape(COLUMN_ROWS, LANES),
                loop_len.reshape(COLUMN_ROWS, LANES),
            )
        )
    )


def solution(mesh):
    both = P(("blk", "rep"))
    wide = P(None, ("blk", "rep"))
    return jax.shard_map(
        shards,
        mesh=mesh,
        in_specs=(wide, wide, both, both, both, both, both),
        out_specs=wide,
        check_vma=False,
    )
```

```python
import functools

import jax
import jax.numpy as jnp
from jax import lax
from jax.experimental import pallas as pl
from jax.experimental.pallas import tpu as pltpu
from jax.sharding import PartitionSpec as P

LOCAL_BETA = 0.3
FRICTION_ALPHA = 0.21
FRICTION_PRIME = 0.06
BIOT_SCALE = 0.01
CORE_SQUARED = 0.25
SPEED_FLOOR = 1.0

BLOCKS = 128
LINE = 8
PLANES = BLOCKS // LINE
REPS = 4
STOPS = 8
BACK = STOPS // 2 - 1
SOURCES = STOPS * REPS
PT = 512
CAP = 10
LANES = 128
COLUMN_ROWS = 10

FEATURES = 64
STOP_ORDER = (0, 4, 3, -3, 2, -2, 1, -1)
LINE_ORDER = (4, 3, 5, 2, 6, 1, 7)
PLANE_ORDER = (10, 9, 11, 6, 14, 7, 13, 2, 8, 5, 15, 3, 1, 4, 12)

MESH = pl.DeviceIdType.MESH
F32 = jnp.float32
BF16 = jnp.bfloat16
I32 = jnp.int32

NT = (((1,), (1,)), ((), ()))
NN = (((1,), (0,)), ((), ()))


def dot(left, right, dims=NN):
    return lax.dot_general(left, right, dims, preferred_element_type=F32)


def rounded(value):
    return value.astype(BF16).astype(F32)


def split(value):
    high = rounded(value)
    rest = value - high
    mid = rounded(rest)
    return high, mid, rest - mid


def iota(shape, dim):
    return lax.broadcasted_iota(I32, shape, dim)


def pick(table, index):
    return jnp.take_along_axis(table, index, axis=1, mode="promise_in_bounds")


def look_up(table, index):
    row, lane = index >> 7, index & 127
    found = jnp.zeros(index.shape, table.dtype)
    for t in range(COLUMN_ROWS):
        piece = jnp.broadcast_to(table[t : t + 1], index.shape)
        found = jnp.where(row == t, pick(piece, lane), found)
    return found


def cross(a, b):
    return [
        a[1] * b[2] - a[2] * b[1],
        a[2] * b[0] - a[0] * b[2],
        a[0] * b[1] - a[1] * b[0],
    ]


def rows_of(value, low, top):
    return [value[c : c + 1] for c in range(low, top)]


def kernel(
    pos_hbm, flow_hbm, owner_hbm, slot_hbm, recv_hbm, order_hbm, count_hbm, out_ref,
    pos_ref, flow_ref, owner_ref, slot_ref, recv_ref, order_ref, count_ref,
    out1, in1, turned1, arrived, out2, in2, turned2, returned,
    targets, src_pos, src_tan, target, features, weights, right, own_sums, part_out, part_in,
    index, member,
    load_sem, ready, send_sem, phase_sem, rep_sem, pos_sem, tan_sem, part_sem,
):
    me = lax.axis_index("blk")
    rep = lax.axis_index("rep")
    plane = me // LINE
    place = me % LINE

    def on_line(k):
        return (place + k) % LINE

    def on_plane(k):
        return (plane + k) % PLANES

    def beside_x(k):
        return (plane + 4 * k) % PLANES

    def beside_y(k):
        return plane // 4 * 4 + (plane + k) % 4

    def on_rep(k):
        return (rep + k) % REPS

    def block(stop):
        return (me + stop + BLOCKS) % BLOCKS

    loads = [
        pltpu.make_async_copy(src, dst, load_sem.at[i])
        for i, (src, dst) in enumerate(
            [
                (pos_hbm, pos_ref), (owner_hbm, owner_ref), (slot_hbm, slot_ref),
                (recv_hbm, recv_ref), (order_hbm, order_ref), (count_hbm, count_ref),
                (flow_hbm, flow_ref),
            ]
        )
    ]
    for load in loads[:3]:
        load.start()

    barrier = pltpu.get_barrier_semaphore()

    def greet(blk, other):
        pl.semaphore_signal(barrier, inc=1, device_id=(blk, other), device_id_type=MESH)

    for k in LINE_ORDER:
        greet(plane * LINE + on_line(k), rep)
    for k in range(1, 4):
        greet(beside_x(k) * LINE + place, rep)
        greet(beside_y(k) * LINE + place, rep)
    for k in range(1, REPS):
        greet(me, on_rep(k))
    for stop in STOP_ORDER[1:]:

        @pl.when((place + stop < 0) | (place + stop >= LINE))
        def _():
            greet(block(stop), rep)

    for load in loads[3:]:
        load.start()
    for load in loads[:3]:
        load.wait()

    pos = pos_ref[...]
    owner = owner_ref[...]
    slot = slot_ref[...]
    owner_place, owner_plane = owner & (LINE - 1), owner >> 3
    member_row = (owner_plane >> 3) * 64 + owner_place * 8 + (owner_plane & 7)
    member[...] = jnp.where(iota((BLOCKS, PT), 0) == member_row, 1.0, 0.0).astype(BF16)
    message_row = owner_place * 4 + (owner_plane >> 2)
    to_row = jnp.where(iota((32, PT), 0) == message_row, 1.0, 0.0).astype(BF16)
    lane = iota((LANES, PT), 0)
    value = lane & 31
    component = jnp.where(value < CAP, 0, jnp.where(value < 2 * CAP, 1, 2))
    here = (lane >> 5) * 16 + value - component * CAP == (owner_plane & 3) * 16 + slot
    slotted = jnp.where(component == 0, pos[0:1], jnp.where(component == 1, pos[1:2], pos[2:3]))
    slotted = jnp.where(here, slotted, 0.0)
    outgoing = sum(dot(to_row, part.astype(BF16), NT) for part in split(slotted))
    out1[...] = outgoing.reshape(LINE, PLANES // 4, LANES)
    square = jnp.sum(pos * pos, axis=0, keepdims=True)
    pos_rows = jnp.concatenate([pos, square], axis=0)
    src_pos[BACK] = pos_rows
    targets[rep] = pos_rows

    def copy_to(src, dst, send, recv, blk, other):
        pltpu.make_async_remote_copy(
            src_ref=src, dst_ref=dst, send_sem=send_sem.at[send], recv_sem=recv,
            device_id=(blk, other), device_id_type=MESH,
        ).start()

    def send_line(src, dst, phase):
        for k in LINE_ORDER:
            there = on_line(k)
            copy_to(src.at[there], dst.at[place], phase, phase_sem.at[phase],
                    plane * LINE + there, rep)

    def send_plane(src, dst, phase):
        for k in PLANE_ORDER:
            there = on_plane(k)
            copy_to(src.at[there], dst.at[plane], phase, phase_sem.at[phase],
                    there * LINE + place, rep)

    def await_here(dst, recv):
        pltpu.make_async_remote_copy(
            src_ref=dst, dst_ref=dst, send_sem=send_sem.at[0], recv_sem=recv,
            device_id=(me, rep), device_id_type=MESH,
        ).wait_recv()

    def await_sent(part, send):
        pltpu.make_async_remote_copy(
            src_ref=part, dst_ref=part, send_sem=send_sem.at[send], recv_sem=phase_sem.at[0],
            device_id=(me, rep), device_id_type=MESH,
        ).wait_send()

    ones = jnp.ones((1, PT), F32)
    none = jnp.zeros((3, PT), F32)
    one_row = jnp.concatenate([ones, none], axis=0)

    def aim(other):
        rows = targets[other]
        wanted = jnp.concatenate(
            [-2.0 * rows[0:3], ones, rows[3:4] + CORE_SQUARED, none], axis=0
        )
        th, tm, tl = split(wanted)
        target[other] = jnp.concatenate([th, th, tm, tm, th, tl, tl, tm], axis=0).astype(BF16)

    def describe(stop):
        sh, sm, sl = split(jnp.concatenate([src_pos[stop + BACK], one_row], axis=0))
        rows = jnp.concatenate(
            [sh, sm, sh, sm, sl, sh, sm, sl, jnp.zeros((LANES - FEATURES, PT), F32)], axis=0
        )
        features[...] = rows.T[:, :FEATURES].astype(BF16)

    def weigh(low, top):
        def one(unit, carry):
            i = unit // REPS
            stop = (i % 2) * ((i + 1) // 2) - (1 - i % 2) * (i // 2)
            other = on_rep(unit % REPS)

            @pl.when((unit % REPS == 0) & (i > 0))
            def _():
                await_here(src_pos.at[stop + BACK], pos_sem.at[stop + BACK])

            @pl.when(unit % REPS == 0)
            def _():
                describe(stop)

            for half in range(PT // 256):
                low, top = half * 256, half * 256 + 256
                root = lax.rsqrt(dot(features[...], target[other, :, low:top]))
                weight = root * root * root
                high = weight.astype(BF16)
                weights[other, stop + BACK, :PT, low:top] = high
                weights[other, stop + BACK, PT:, low:top] = (
                    weight - high.astype(F32)
                ).astype(BF16)
            return carry

        lax.fori_loop(low, top, one, 0)

    across = jnp.where(place < STOPS // 2, STOPS // 2 - place, place - STOPS // 2)
    pl.semaphore_wait(barrier, (LINE - 1) + 3 + 3 + (REPS - 1) + across)

    send_line(out1, in1, 0)
    for k in range(1, 4):
        pl.semaphore_signal(
            ready, inc=1, device_id=(beside_x(k) * LINE + place, rep), device_id_type=MESH
        )
    for k in range(1, REPS):
        copy_to(targets.at[rep], targets.at[rep], 4, rep_sem.at[rep], me, on_rep(k))
    in1[place] = out1[place]

    for load in loads[3:]:
        load.wait()
    lane = iota((16, LANES), 1)
    spot = (((lane & 31) >> 1) * LINE + (lane >> 5) * 2 + (lane & 1)) * CAP + iota((16, LANES), 0)
    column = jnp.where(iota((16, LANES), 0) < CAP, look_up(recv_ref[...], spot), -1)
    column_row, column_lane = column >> 7, column & 127
    holder = iota((16, LANES), 1).astype(F32)
    inverse = jnp.zeros((32, LANES), F32)
    for s in range(CAP):
        hit = column_row[s : s + 1] == iota((16, LANES), 0)
        left = jnp.concatenate(
            [jnp.where(hit, holder, 0.0), jnp.where(hit, float(s), 0.0)], axis=0
        ).astype(BF16)
        lane_hit = column_lane[s : s + 1] == iota((LANES, LANES), 0)
        inverse = inverse + dot(left, jnp.where(lane_hit, 1.0, 0.0).astype(BF16), NT)
    inverse = (inverse[16:] * float(LANES) + inverse[:16]).astype(I32)
    at = jnp.maximum(column, 0)
    ring = look_up(order_ref[...] + (count_ref[...] << 11), at)
    order, count = ring & 2047, ring >> 11

    def neighbour(offset):
        moved = order + offset
        moved = jnp.where(moved < 0, moved + count, jnp.where(moved >= count, moved - count, moved))
        there = jnp.clip(at - order + moved, 0, COLUMN_ROWS * LANES - 1)
        return look_up(inverse, there)

    ahead1, ahead2, behind1, behind2 = (neighbour(k) for k in (1, 2, -1, -2))
    for i, table in enumerate((ahead1, ahead2, behind1, behind2)):
        index[i] = table
    aim(rep)
    weigh(0, 1)
    await_here(in1.at[pl.ds(0, LINE - 1)], phase_sem.at[0])
    place_bits, plane_bits = iota((LINE, LANES), 0) >> 1, iota((LINE, LANES), 1) >> 5
    for q in range(PLANES // 4):
        rows = in1[:, q, :]
        down = pltpu.roll(pltpu.roll(rows, LINE - 2, 0), 32, 1)
        up = pltpu.roll(pltpu.roll(rows, 2, 0), LANES - 32, 1)
        rows = jnp.where(
            (place_bits & 1) == (plane_bits & 1), rows, jnp.where((place_bits & 1) == 0, down, up)
        )
        far_rows = pltpu.roll(pltpu.roll(rows, 4, 0), 64, 1)
        rows = jnp.where((place_bits >> 1) == (plane_bits >> 1), rows, far_rows)
        for p in range(4):
            turned1[4 * q + p] = rows[2 * p : 2 * p + 2]
    pl.semaphore_wait(ready, 3)
    send_plane(turned1, arrived, 1)
    arrived[plane] = turned1[plane]
    for stop in STOP_ORDER[1:]:
        copy_to(src_pos.at[BACK], src_pos.at[stop + BACK], 5, pos_sem.at[stop + BACK],
                block(-stop), rep)

    for k in range(1, REPS):
        await_here(targets.at[on_rep(k)], rep_sem.at[on_rep(k)])
        aim(on_rep(k))
    weigh(1, 4)

    await_here(arrived.at[pl.ds(0, PLANES - 1)], phase_sem.at[1])
    rows = arrived[...].reshape(2 * PLANES, LANES)
    tables = jnp.concatenate(
        [rows] + [pltpu.roll(rows, LANES - 32 * i, 1) for i in range(1, 4)], axis=0
    ).T
    moved = []
    for i in range(4):
        at_row, at_lane = index[i] >> 7, index[i] & 127
        found = [jnp.zeros((16, LANES), F32) for _ in range(3)]
        for t in range(CAP):
            hit = at_row == t
            for c in range(3):
                table = jnp.broadcast_to(tables[c * CAP + t : c * CAP + t + 1], (16, LANES))
                found[c] = jnp.where(hit, pick(table, at_lane), found[c])
        moved.append(found)
    results = [[], []]
    for c in range(3):
        a1, a2, b1, b2 = (found[c][:CAP] for found in moved)
        center = tables[c * CAP : (c + 1) * CAP]
        results[0].append((8.0 * (a1 - b1) - (a2 - b2)) / 12.0)
        results[1].append((16.0 * (a1 + b1) - (a2 + b2) - 30.0 * center) / 12.0)
    values = jnp.concatenate(
        results[0] + results[1] + [jnp.zeros((64 - 6 * CAP, LANES), F32)], axis=0
    )
    values = jnp.concatenate([values, pltpu.roll(values, 64, 1)], axis=0).T
    for i in range(2):
        out2[:, i] = values[32 * i : 32 * i + 32].reshape(PLANES, 2, LANES)

    send_plane(out2, in2, 2)
    in2[plane] = out2[plane]
    weigh(4, 14)
    await_here(in2.at[pl.ds(0, PLANES - 1)], phase_sem.at[2])
    left_half = iota((8, LANES), 1) < 64
    for i in range(2):
        for j in range(2):
            rows = in2[:, i, j, :]
            a, b = rows[:8], rows[8:]
            turned2[2 * i + j] = jnp.where(left_half, a, pltpu.roll(b, 64, 1))
            turned2[4 + 2 * i + j] = jnp.where(left_half, pltpu.roll(a, 64, 1), b)
    send_line(turned2, returned, 3)
    returned[place] = turned2[place]
    weigh(14, 24)
    await_here(returned.at[pl.ds(0, LINE - 1)], phase_sem.at[3])
    rows = returned[...].reshape(64, LANES)
    back = jnp.concatenate([rows, pltpu.roll(rows, 64, 1)], axis=0).T[:64]
    is_owner = member[...]
    spread = sum(dot(part.astype(BF16), is_owner) for part in split(back))
    derived = []
    for q in range(6):
        chosen = jnp.where(iota((CAP, PT), 0) == slot, spread[q * CAP : (q + 1) * CAP], 0.0)
        derived.append(jnp.sum(chosen, axis=0, keepdims=True))

    src_tan[BACK] = jnp.concatenate(derived[0:3] + [jnp.zeros((1, PT), F32)], axis=0)
    for stop in STOP_ORDER[1:]:
        copy_to(src_tan.at[BACK], src_tan.at[stop + BACK], 6, tan_sem.at[stop + BACK],
                block(-stop), rep)
    weigh(24, SOURCES)

    def prepare(stop):
        p, t = rows_of(src_pos[stop], 0, 3), rows_of(src_tan[stop], 0, 3)
        h, m, l = split(jnp.concatenate(t + cross(t, p) + [jnp.zeros((2, PT), F32)], axis=0))
        rows = jnp.concatenate([h, m, l, jnp.zeros((8, PT), F32)], axis=0).astype(BF16)
        rows = jnp.concatenate([rows, rows], axis=1)
        right[stop] = rows
        return rows

    prepare(BACK)
    for k in range(REPS):
        own_sums[k] = dot(right[BACK], weights[k, BACK])
    for stop in STOP_ORDER[1:]:
        await_here(src_tan.at[stop + BACK], tan_sem.at[stop + BACK])

    def finish_sums(i, other, parts):
        parts = parts[0:8] + parts[8:16] + parts[16:24]
        far = cross(rows_of(parts, 0, 3), rows_of(targets[other], 0, 3))
        part_out[i] = jnp.concatenate(
            [far[c] - parts[3 + c : 4 + c] for c in range(3)] + [jnp.zeros((1, PT), F32)], axis=0
        )

    def send_sums(i, other):
        copy_to(part_out.at[i], part_in.at[i], 7, part_sem.at[i], me, other)

    other = (rep + 2) % REPS
    parts = own_sums[other]
    for stop in STOP_ORDER[:0:-1]:
        parts = parts + dot(prepare(stop + BACK), weights[other, stop + BACK])
    finish_sums(0, other, parts)
    send_sums(0, other)

    def sums_of(i, carry):
        other = jnp.where(
            i == 1, REPS - 1 - rep, jnp.where(i == 2, rep + 1 - 2 * (rep % 2), rep)
        )
        parts = own_sums[other]
        for stop in STOP_ORDER[:0:-1]:
            parts = parts + dot(right[stop + BACK], weights[other, stop + BACK])
        finish_sums(i, other, parts)

        @pl.when(i < REPS - 1)
        def _():
            send_sums(i, other)

        return carry

    lax.fori_loop(1, REPS, sums_of, 0)
    for i in range(REPS - 1):
        await_here(part_in.at[i], part_sem.at[i])
    others = part_out[REPS - 1] + part_in[0] + part_in[1] + part_in[2]
    far = [others[c : c + 1] for c in range(3)]

    tangent, curvature = derived[0:3], derived[3:6]
    speed = jnp.maximum(
        tangent[0] * tangent[0] + tangent[1] * tangent[1] + tangent[2] * tangent[2], SPEED_FLOOR
    )
    per_speed = 1.0 / jnp.sqrt(speed)
    scale = LOCAL_BETA * per_speed / speed
    local = cross(tangent, curvature)
    superfluid = [scale * local[c] + BIOT_SCALE * far[c] for c in range(3)]
    unit = [tangent[c] * per_speed for c in range(3)]
    once = cross(unit, [flow_ref[c : c + 1, :] - superfluid[c] for c in range(3)])
    twice = cross(unit, once)
    for c in range(3):
        out_ref[c : c + 1, :] = (
            superfluid[c] + FRICTION_ALPHA * once[c] - FRICTION_PRIME * twice[c]
        )

    await_sent(out1.at[pl.ds(0, LINE - 1)], 0)
    await_sent(turned1.at[pl.ds(0, PLANES - 1)], 1)
    await_sent(out2.at[pl.ds(0, PLANES - 1)], 2)
    await_sent(turned2.at[pl.ds(0, LINE - 1)], 3)
    await_sent(targets.at[pl.ds(0, REPS - 1)], 4)
    await_sent(src_pos.at[pl.ds(0, STOPS - 1)], 5)
    await_sent(src_tan.at[pl.ds(0, STOPS - 1)], 6)
    await_sent(part_out.at[pl.ds(0, REPS - 1)], 7)


def shards(positions, normal_flow, send_owner, send_slot, recv_index, loop_pos, loop_len):
    dma = pltpu.SemaphoreType.DMA
    first = pltpu.VMEM((LINE, PLANES // 4, LANES), F32)
    second = pltpu.VMEM((PLANES, 2, LANES), F32)
    third = pltpu.VMEM((PLANES, 2, 2, LANES), F32)
    fourth = pltpu.VMEM((LINE, 8, LANES), F32)
    points = pltpu.VMEM((3, PT), F32)
    point_index = pltpu.VMEM((1, PT), I32)
    columns = pltpu.VMEM((COLUMN_ROWS, LANES), I32)
    return pl.pallas_call(
        kernel,
        out_shape=jax.ShapeDtypeStruct((3, PT), F32),
        in_specs=[pl.BlockSpec(memory_space=pltpu.HBM)] * 7,
        out_specs=pl.BlockSpec(memory_space=pltpu.VMEM),
        scratch_shapes=[
            points, points, point_index, point_index, columns, columns, columns,
            first, first, second, second, third, third, fourth, fourth,
            pltpu.VMEM((REPS, 4, PT), F32),
            pltpu.VMEM((STOPS, 4, PT), F32),
            pltpu.VMEM((STOPS, 4, PT), F32),
            pltpu.VMEM((REPS, FEATURES, PT), BF16),
            pltpu.VMEM((PT, FEATURES), BF16),
            pltpu.VMEM((REPS, STOPS, 2 * PT, PT), BF16),
            pltpu.VMEM((STOPS, 32, 2 * PT), BF16),
            pltpu.VMEM((REPS, 32, PT), F32),
            pltpu.VMEM((REPS, 4, PT), F32),
            pltpu.VMEM((REPS, 4, PT), F32),
            pltpu.VMEM((4, 16, LANES), I32),
            pltpu.VMEM((BLOCKS, PT), BF16),
            dma((7,)), pltpu.SemaphoreType.REGULAR, dma((8,)), dma((4,)), dma((REPS,)), dma((STOPS,)), dma((STOPS,)),
            dma((REPS,)),
        ],
        compiler_params=pltpu.CompilerParams(
            collective_id=0, has_side_effects=True, vmem_limit_bytes=48 * 1024 * 1024
        ),
        cost_estimate=pl.CostEstimate(
            flops=2 * PT * SOURCES * PT * 128, bytes_accessed=1 << 20,
            transcendentals=PT * SOURCES * PT,
        ),
    )(
        *(
            pltpu.with_memory_space_constraint(operand, pltpu.HBM)
            for operand in (
                positions,
                normal_flow,
                send_owner.reshape(1, PT),
                send_slot.reshape(1, PT),
                recv_index.reshape(CAP, BLOCKS),
                loop_pos.reshape(COLUMN_ROWS, LANES),
                loop_len.reshape(COLUMN_ROWS, LANES),
            )
        )
    )


def solution(mesh):
    both = P(("blk", "rep"))
    wide = P(None, ("blk", "rep"))
    return jax.shard_map(
        shards,
        mesh=mesh,
        in_specs=(wide, wide, both, both, both, both, both),
        out_specs=wide,
        check_vma=False,
    )
```

```python
import functools

import jax
import jax.numpy as jnp
from jax import lax
from jax.experimental import pallas as pl
from jax.experimental.pallas import tpu as pltpu
from jax.sharding import PartitionSpec as P

LOCAL_BETA = 0.3
FRICTION_ALPHA = 0.21
FRICTION_PRIME = 0.06
BIOT_SCALE = 0.01
CORE_SQUARED = 0.25
SPEED_FLOOR = 1.0

BLOCKS = 128
LINE = 8
PLANES = BLOCKS // LINE
REPS = 4
STOPS = 8
BACK = STOPS // 2 - 1
SOURCES = STOPS * REPS
PT = 512
CAP = 10
LANES = 128
COLUMN_ROWS = 10

FEATURES = 64
STOP_ORDER = (0, 4, 3, -3, 2, -2, 1, -1)
LINE_ORDER = (4, 3, 5, 2, 6, 1, 7)
PLANE_ORDER = (10, 9, 11, 6, 14, 7, 13, 2, 8, 5, 15, 3, 1, 4, 12)

MESH = pl.DeviceIdType.MESH
F32 = jnp.float32
BF16 = jnp.bfloat16
I32 = jnp.int32
F8 = jnp.float8_e4m3fn
LOW_SCALE = 8192.0

NT = (((1,), (1,)), ((), ()))
NN = (((1,), (0,)), ((), ()))


def dot(left, right, dims=NN):
    return lax.dot_general(left, right, dims, preferred_element_type=F32)


def rounded(value):
    return value.astype(BF16).astype(F32)


def split(value):
    high = rounded(value)
    rest = value - high
    mid = rounded(rest)
    return high, mid, rest - mid


def iota(shape, dim):
    return lax.broadcasted_iota(I32, shape, dim)


def pick(table, index):
    return jnp.take_along_axis(table, index, axis=1, mode="promise_in_bounds")


def look_up(table, index):
    row, lane = index >> 7, index & 127
    found = jnp.zeros(index.shape, table.dtype)
    for t in range(COLUMN_ROWS):
        piece = jnp.broadcast_to(table[t : t + 1], index.shape)
        found = jnp.where(row == t, pick(piece, lane), found)
    return found


def cross(a, b):
    return [
        a[1] * b[2] - a[2] * b[1],
        a[2] * b[0] - a[0] * b[2],
        a[0] * b[1] - a[1] * b[0],
    ]


def rows_of(value, low, top):
    return [value[c : c + 1] for c in range(low, top)]


def kernel(
    pos_hbm, flow_hbm, owner_hbm, slot_hbm, recv_hbm, order_hbm, count_hbm, out_ref,
    pos_ref, flow_ref, owner_ref, slot_ref, recv_ref, order_ref, count_ref,
    out1, in1, turned1, arrived, out2, in2, turned2, returned,
    targets, src_pos, src_tan, target, features, weights, weights_low, right, right_low, own_sums, part_out, part_in,
    index, member,
    load_sem, ready, send_sem, phase_sem, rep_sem, pos_sem, tan_sem, part_sem,
):
    me = lax.axis_index("blk")
    rep = lax.axis_index("rep")
    plane = me // LINE
    place = me % LINE

    def on_line(k):
        return (place + k) % LINE

    def on_plane(k):
        return (plane + k) % PLANES

    def beside_x(k):
        return (plane + 4 * k) % PLANES

    def beside_y(k):
        return plane // 4 * 4 + (plane + k) % 4

    def on_rep(k):
        return (rep + k) % REPS

    def block(stop):
        return (me + stop + BLOCKS) % BLOCKS

    loads = [
        pltpu.make_async_copy(src, dst, load_sem.at[i])
        for i, (src, dst) in enumerate(
            [
                (pos_hbm, pos_ref), (owner_hbm, owner_ref), (slot_hbm, slot_ref),
                (recv_hbm, recv_ref), (order_hbm, order_ref), (count_hbm, count_ref),
                (flow_hbm, flow_ref),
            ]
        )
    ]
    for load in loads[:3]:
        load.start()

    barrier = pltpu.get_barrier_semaphore()

    def greet(blk, other):
        pl.semaphore_signal(barrier, inc=1, device_id=(blk, other), device_id_type=MESH)

    for k in LINE_ORDER:
        greet(plane * LINE + on_line(k), rep)
    for k in range(1, 4):
        greet(beside_x(k) * LINE + place, rep)
        greet(beside_y(k) * LINE + place, rep)
    for k in range(1, REPS):
        greet(me, on_rep(k))
    for stop in STOP_ORDER[1:]:

        @pl.when((place + stop < 0) | (place + stop >= LINE))
        def _():
            greet(block(stop), rep)

    for load in loads[3:]:
        load.start()
    for load in loads[:3]:
        load.wait()

    pos = pos_ref[...]
    owner = owner_ref[...]
    slot = slot_ref[...]
    owner_place, owner_plane = owner & (LINE - 1), owner >> 3
    member_row = (owner_plane >> 3) * 64 + owner_place * 8 + (owner_plane & 7)
    member[...] = jnp.where(iota((BLOCKS, PT), 0) == member_row, 1.0, 0.0).astype(BF16)
    message_row = owner_place * 4 + (owner_plane >> 2)
    to_row = jnp.where(iota((32, PT), 0) == message_row, 1.0, 0.0).astype(BF16)
    lane = iota((LANES, PT), 0)
    value = lane & 31
    component = jnp.where(value < CAP, 0, jnp.where(value < 2 * CAP, 1, 2))
    here = (lane >> 5) * 16 + value - component * CAP == (owner_plane & 3) * 16 + slot
    slotted = jnp.where(component == 0, pos[0:1], jnp.where(component == 1, pos[1:2], pos[2:3]))
    slotted = jnp.where(here, slotted, 0.0)
    outgoing = sum(dot(to_row, part.astype(BF16), NT) for part in split(slotted))
    out1[...] = outgoing.reshape(LINE, PLANES // 4, LANES)
    square = jnp.sum(pos * pos, axis=0, keepdims=True)
    pos_rows = jnp.concatenate([pos, square], axis=0)
    src_pos[BACK] = pos_rows
    targets[rep] = pos_rows

    def copy_to(src, dst, send, recv, blk, other):
        pltpu.make_async_remote_copy(
            src_ref=src, dst_ref=dst, send_sem=send_sem.at[send], recv_sem=recv,
            device_id=(blk, other), device_id_type=MESH,
        ).start()

    def send_line(src, dst, phase):
        for k in range(1, LINE) if phase == 0 else LINE_ORDER:
            late = jnp.where(LINE - k > place, LINE - k, LINE - 1 - k)
            there = late if phase == 0 else on_line(k)
            copy_to(src.at[there], dst.at[place], phase, phase_sem.at[phase],
                    plane * LINE + there, rep)

    def send_plane(src, dst, phase):
        for k in PLANE_ORDER:
            there = on_plane(k)
            copy_to(src.at[there], dst.at[plane], phase, phase_sem.at[phase],
                    there * LINE + place, rep)

    def await_here(dst, recv):
        pltpu.make_async_remote_copy(
            src_ref=dst, dst_ref=dst, send_sem=send_sem.at[0], recv_sem=recv,
            device_id=(me, rep), device_id_type=MESH,
        ).wait_recv()

    def await_sent(part, send):
        pltpu.make_async_remote_copy(
            src_ref=part, dst_ref=part, send_sem=send_sem.at[send], recv_sem=phase_sem.at[0],
            device_id=(me, rep), device_id_type=MESH,
        ).wait_send()

    ones = jnp.ones((1, PT), F32)
    none = jnp.zeros((3, PT), F32)
    one_row = jnp.concatenate([ones, none], axis=0)

    def aim(other):
        rows = targets[other]
        wanted = jnp.concatenate(
            [-2.0 * rows[0:3], ones, rows[3:4] + CORE_SQUARED, none], axis=0
        )
        th, tm, tl = split(wanted)
        target[other] = jnp.concatenate([th, th, tm, tm, th, tl, tl, tm], axis=0).astype(BF16)

    def describe(stop):
        sh, sm, sl = split(jnp.concatenate([src_pos[stop + BACK], one_row], axis=0))
        rows = jnp.concatenate(
            [sh, sm, sh, sm, sl, sh, sm, sl, jnp.zeros((LANES - FEATURES, PT), F32)], axis=0
        )
        features[...] = rows.T[:, :FEATURES].astype(BF16)

    def weigh(low, top):
        def one(unit, carry):
            i = unit // REPS
            stop = (i % 2) * ((i + 1) // 2) - (1 - i % 2) * (i // 2)
            other = on_rep(unit % REPS)

            @pl.when((unit % REPS == 0) & (i > 0))
            def _():
                await_here(src_pos.at[stop + BACK], pos_sem.at[stop + BACK])

            @pl.when(unit % REPS == 0)
            def _():
                describe(stop)

            for half in range(PT // 256):
                low, top = half * 256, half * 256 + 256
                root = lax.rsqrt(dot(features[...], target[other, :, low:top]))
                weight = root * root * root
                high = weight.astype(BF16)
                weights[other, stop + BACK, :, low:top] = high
                rest = (weight - high.astype(F32)) * LOW_SCALE
                weights_low[other, stop + BACK, :, low:top] = rest.astype(F8)
            return carry

        lax.fori_loop(low, top, one, 0)

    across = jnp.where(place < STOPS // 2, STOPS // 2 - place, place - STOPS // 2)
    pl.semaphore_wait(barrier, (LINE - 1) + 3 + 3 + (REPS - 1) + across)

    send_line(out1, in1, 0)
    for k in range(1, 4):
        pl.semaphore_signal(
            ready, inc=1, device_id=(beside_x(k) * LINE + place, rep), device_id_type=MESH
        )
    for k in range(1, REPS):
        copy_to(targets.at[rep], targets.at[rep], 4, rep_sem.at[rep], me, on_rep(k))
    in1[place] = out1[place]

    for load in loads[3:]:
        load.wait()
    lane = iota((16, LANES), 1)
    spot = (((lane & 31) >> 1) * LINE + (lane >> 5) * 2 + (lane & 1)) * CAP + iota((16, LANES), 0)
    column = jnp.where(iota((16, LANES), 0) < CAP, look_up(recv_ref[...], spot), -1)
    column_row, column_lane = column >> 7, column & 127
    holder = iota((16, LANES), 1).astype(F32)
    inverse = jnp.zeros((32, LANES), F32)
    for s in range(CAP):
        hit = column_row[s : s + 1] == iota((16, LANES), 0)
        left = jnp.concatenate(
            [jnp.where(hit, holder, 0.0), jnp.where(hit, float(s), 0.0)], axis=0
        ).astype(BF16)
        lane_hit = column_lane[s : s + 1] == iota((LANES, LANES), 0)
        inverse = inverse + dot(left, jnp.where(lane_hit, 1.0, 0.0).astype(BF16), NT)
    inverse = (inverse[16:] * float(LANES) + inverse[:16]).astype(I32)
    at = jnp.maximum(column, 0)
    ring = look_up(order_ref[...] + (count_ref[...] << 11), at)
    order, count = ring & 2047, ring >> 11

    def neighbour(offset):
        moved = order + offset
        moved = jnp.where(moved < 0, moved + count, jnp.where(moved >= count, moved - count, moved))
        there = jnp.clip(at - order + moved, 0, COLUMN_ROWS * LANES - 1)
        return look_up(inverse, there)

    ahead1, ahead2, behind1, behind2 = (neighbour(k) for k in (1, 2, -1, -2))
    for i, table in enumerate((ahead1, ahead2, behind1, behind2)):
        index[i] = table
    aim(rep)
    weigh(0, 1)
    await_here(in1.at[pl.ds(0, LINE - 1)], phase_sem.at[0])
    place_bits, plane_bits = iota((LINE, LANES), 0) >> 1, iota((LINE, LANES), 1) >> 5
    for q in range(PLANES // 4):
        rows = in1[:, q, :]
        down = pltpu.roll(pltpu.roll(rows, LINE - 2, 0), 32, 1)
        up = pltpu.roll(pltpu.roll(rows, 2, 0), LANES - 32, 1)
        rows = jnp.where(
            (place_bits & 1) == (plane_bits & 1), rows, jnp.where((place_bits & 1) == 0, down, up)
        )
        far_rows = pltpu.roll(pltpu.roll(rows, 4, 0), 64, 1)
        rows = jnp.where((place_bits >> 1) == (plane_bits >> 1), rows, far_rows)
        for p in range(4):
            turned1[4 * q + p] = rows[2 * p : 2 * p + 2]
    pl.semaphore_wait(ready, 3)
    send_plane(turned1, arrived, 1)
    arrived[plane] = turned1[plane]
    for stop in STOP_ORDER[1:]:
        copy_to(src_pos.at[BACK], src_pos.at[stop + BACK], 5, pos_sem.at[stop + BACK],
                block(-stop), rep)

    for k in range(1, REPS):
        await_here(targets.at[on_rep(k)], rep_sem.at[on_rep(k)])
        aim(on_rep(k))
    weigh(1, 4)

    await_here(arrived.at[pl.ds(0, PLANES - 1)], phase_sem.at[1])
    rows = arrived[...].reshape(2 * PLANES, LANES)
    tables = jnp.concatenate(
        [rows] + [pltpu.roll(rows, LANES - 32 * i, 1) for i in range(1, 4)], axis=0
    ).T
    moved = []
    for i in range(4):
        at_row, at_lane = index[i] >> 7, index[i] & 127
        found = [jnp.zeros((16, LANES), F32) for _ in range(3)]
        for t in range(CAP):
            hit = at_row == t
            for c in range(3):
                table = jnp.broadcast_to(tables[c * CAP + t : c * CAP + t + 1], (16, LANES))
                found[c] = jnp.where(hit, pick(table, at_lane), found[c])
        moved.append(found)
    results = [[], []]
    for c in range(3):
        a1, a2, b1, b2 = (found[c][:CAP] for found in moved)
        center = tables[c * CAP : (c + 1) * CAP]
        results[0].append((8.0 * (a1 - b1) - (a2 - b2)) / 12.0)
        results[1].append((16.0 * (a1 + b1) - (a2 + b2) - 30.0 * center) / 12.0)
    values = jnp.concatenate(
        results[0] + results[1] + [jnp.zeros((64 - 6 * CAP, LANES), F32)], axis=0
    )
    values = jnp.concatenate([values, pltpu.roll(values, 64, 1)], axis=0).T
    for i in range(2):
        out2[:, i] = values[32 * i : 32 * i + 32].reshape(PLANES, 2, LANES)

    send_plane(out2, in2, 2)
    in2[plane] = out2[plane]
    weigh(4, 14)
    await_here(in2.at[pl.ds(0, PLANES - 1)], phase_sem.at[2])
    left_half = iota((8, LANES), 1) < 64
    for i in range(2):
        for j in range(2):
            rows = in2[:, i, j, :]
            a, b = rows[:8], rows[8:]
            turned2[2 * i + j] = jnp.where(left_half, a, pltpu.roll(b, 64, 1))
            turned2[4 + 2 * i + j] = jnp.where(left_half, pltpu.roll(a, 64, 1), b)
    send_line(turned2, returned, 3)
    returned[place] = turned2[place]
    weigh(14, 24)
    await_here(returned.at[pl.ds(0, LINE - 1)], phase_sem.at[3])
    rows = returned[...].reshape(64, LANES)
    back = jnp.concatenate([rows, pltpu.roll(rows, 64, 1)], axis=0).T[:64]
    is_owner = member[...]
    spread = sum(dot(part.astype(BF16), is_owner) for part in split(back))
    derived = []
    for q in range(6):
        chosen = jnp.where(iota((CAP, PT), 0) == slot, spread[q * CAP : (q + 1) * CAP], 0.0)
        derived.append(jnp.sum(chosen, axis=0, keepdims=True))

    src_tan[BACK] = jnp.concatenate(derived[0:3] + [jnp.zeros((1, PT), F32)], axis=0)
    for stop in STOP_ORDER[1:]:
        copy_to(src_tan.at[BACK], src_tan.at[stop + BACK], 6, tan_sem.at[stop + BACK],
                block(-stop), rep)
    weigh(24, SOURCES)

    def prepare(stop):
        p, t = rows_of(src_pos[stop], 0, 3), rows_of(src_tan[stop], 0, 3)
        rows = jnp.concatenate(t + cross(t, p) + [jnp.zeros((2, PT), F32)], axis=0)
        h, m, l = split(rows)
        right[stop] = jnp.concatenate([h, m, l, jnp.zeros((8, PT), F32)], axis=0).astype(BF16)
        high = rows.astype(F8).astype(F32)
        right_low[stop] = jnp.concatenate(
            [high, rows - high, jnp.zeros((16, PT), F32)], axis=0
        ).astype(F8)

    def product(other, stop):
        high = dot(right[stop + BACK], weights[other, stop + BACK])
        low = dot(right_low[stop + BACK], weights_low[other, stop + BACK])
        return high + low * (1.0 / LOW_SCALE)

    prepare(BACK)
    for k in range(REPS):
        own_sums[k] = product(k, 0)
    await_sent(out1.at[pl.ds(0, LINE - 1)], 0)
    await_sent(turned1.at[pl.ds(0, PLANES - 1)], 1)
    await_sent(out2.at[pl.ds(0, PLANES - 1)], 2)
    await_sent(turned2.at[pl.ds(0, LINE - 1)], 3)
    await_sent(targets.at[pl.ds(0, REPS - 1)], 4)
    await_sent(src_pos.at[pl.ds(0, STOPS - 1)], 5)
    for stop in STOP_ORDER[1:]:
        await_here(src_tan.at[stop + BACK], tan_sem.at[stop + BACK])

    def finish_sums(i, other, parts):
        parts = parts[0:8] + parts[8:16] + parts[16:24]
        far = cross(rows_of(parts, 0, 3), rows_of(targets[other], 0, 3))
        part_out[i] = jnp.concatenate(
            [far[c] - parts[3 + c : 4 + c] for c in range(3)] + [jnp.zeros((1, PT), F32)], axis=0
        )

    def send_sums(i, other):
        copy_to(part_out.at[i], part_in.at[i], 7, part_sem.at[i], me, other)

    other = (rep + 2) % REPS
    parts = own_sums[other]
    for stop in STOP_ORDER[:0:-1]:
        prepare(stop + BACK)
        parts = parts + product(other, stop)
    finish_sums(0, other, parts)
    send_sums(0, other)

    def sums_of(i, carry):
        other = jnp.where(
            i == 1, REPS - 1 - rep, jnp.where(i == 2, rep + 1 - 2 * (rep % 2), rep)
        )
        parts = own_sums[other]
        for stop in STOP_ORDER[:0:-1]:
            parts = parts + product(other, stop)
        finish_sums(i, other, parts)

        @pl.when(i < REPS - 1)
        def _():
            send_sums(i, other)

        return carry

    lax.fori_loop(1, REPS, sums_of, 0)
    for i in range(REPS - 1):
        await_here(part_in.at[i], part_sem.at[i])
    others = part_out[REPS - 1] + part_in[0] + part_in[1] + part_in[2]
    far = [others[c : c + 1] for c in range(3)]

    tangent, curvature = derived[0:3], derived[3:6]
    speed = jnp.maximum(
        tangent[0] * tangent[0] + tangent[1] * tangent[1] + tangent[2] * tangent[2], SPEED_FLOOR
    )
    per_speed = 1.0 / jnp.sqrt(speed)
    scale = LOCAL_BETA * per_speed / speed
    local = cross(tangent, curvature)
    superfluid = [scale * local[c] + BIOT_SCALE * far[c] for c in range(3)]
    unit = [tangent[c] * per_speed for c in range(3)]
    once = cross(unit, [flow_ref[c : c + 1, :] - superfluid[c] for c in range(3)])
    twice = cross(unit, once)
    for c in range(3):
        out_ref[c : c + 1, :] = (
            superfluid[c] + FRICTION_ALPHA * once[c] - FRICTION_PRIME * twice[c]
        )

    await_sent(src_tan.at[pl.ds(0, STOPS - 1)], 6)
    await_sent(part_out.at[pl.ds(0, REPS - 1)], 7)


def shards(positions, normal_flow, send_owner, send_slot, recv_index, loop_pos, loop_len):
    dma = pltpu.SemaphoreType.DMA
    first = pltpu.VMEM((LINE, PLANES // 4, LANES), F32)
    second = pltpu.VMEM((PLANES, 2, LANES), F32)
    third = pltpu.VMEM((PLANES, 2, 2, LANES), F32)
    fourth = pltpu.VMEM((LINE, 8, LANES), F32)
    points = pltpu.VMEM((3, PT), F32)
    point_index = pltpu.VMEM((1, PT), I32)
    columns = pltpu.VMEM((COLUMN_ROWS, LANES), I32)
    return pl.pallas_call(
        kernel,
        out_shape=jax.ShapeDtypeStruct((3, PT), F32),
        in_specs=[pl.BlockSpec(memory_space=pltpu.HBM)] * 7,
        out_specs=pl.BlockSpec(memory_space=pltpu.VMEM),
        scratch_shapes=[
            points, points, point_index, point_index, columns, columns, columns,
            first, first, second, second, third, third, fourth, fourth,
            pltpu.VMEM((REPS, 4, PT), F32),
            pltpu.VMEM((STOPS, 4, PT), F32),
            pltpu.VMEM((STOPS, 4, PT), F32),
            pltpu.VMEM((REPS, FEATURES, PT), BF16),
            pltpu.VMEM((PT, FEATURES), BF16),
            pltpu.VMEM((REPS, STOPS, PT, PT), BF16),
            pltpu.VMEM((REPS, STOPS, PT, PT), F8),
            pltpu.VMEM((STOPS, 32, PT), BF16),
            pltpu.VMEM((STOPS, 32, PT), F8),
            pltpu.VMEM((REPS, 32, PT), F32),
            pltpu.VMEM((REPS, 4, PT), F32),
            pltpu.VMEM((REPS, 4, PT), F32),
            pltpu.VMEM((4, 16, LANES), I32),
            pltpu.VMEM((BLOCKS, PT), BF16),
            dma((7,)), pltpu.SemaphoreType.REGULAR, dma((8,)), dma((4,)), dma((REPS,)), dma((STOPS,)), dma((STOPS,)),
            dma((REPS,)),
        ],
        compiler_params=pltpu.CompilerParams(
            collective_id=0, has_side_effects=True, vmem_limit_bytes=40 * 1024 * 1024
        ),
        cost_estimate=pl.CostEstimate(
            flops=2 * PT * SOURCES * PT * 128, bytes_accessed=1 << 20,
            transcendentals=PT * SOURCES * PT,
        ),
    )(
        *(
            pltpu.with_memory_space_constraint(operand, pltpu.HBM)
            for operand in (
                positions,
                normal_flow,
                send_owner.reshape(1, PT),
                send_slot.reshape(1, PT),
                recv_index.reshape(CAP, BLOCKS),
                loop_pos.reshape(COLUMN_ROWS, LANES),
                loop_len.reshape(COLUMN_ROWS, LANES),
            )
        )
    )


def solution(mesh):
    both = P(("blk", "rep"))
    wide = P(None, ("blk", "rep"))
    return jax.shard_map(
        shards,
        mesh=mesh,
        in_specs=(wide, wide, both, both, both, both, both),
        out_specs=wide,
        check_vma=False,
    )
```

```python
import functools

import jax
import jax.numpy as jnp
from jax import lax
from jax.experimental import pallas as pl
from jax.experimental.pallas import tpu as pltpu
from jax.sharding import PartitionSpec as P

LOCAL_BETA = 0.3
FRICTION_ALPHA = 0.21
FRICTION_PRIME = 0.06
BIOT_SCALE = 0.01
CORE_SQUARED = 0.25
SPEED_FLOOR = 1.0

BLOCKS = 128
LINE = 8
PLANES = BLOCKS // LINE
REPS = 4
STOPS = 8
BACK = STOPS // 2 - 1
SOURCES = STOPS * REPS
PT = 512
CAP = 10
LANES = 128
COLUMN_ROWS = 10

FEATURES = 64
STOP_ORDER = (0, 4, 3, -3, 2, -2, 1, -1)
LINE_ORDER = (4, 3, 5, 2, 6, 1, 7)
PLANE_ORDER = (10, 9, 11, 6, 14, 7, 13, 2, 8, 5, 15, 3, 1, 4, 12)

MESH = pl.DeviceIdType.MESH
F32 = jnp.float32
BF16 = jnp.bfloat16
I32 = jnp.int32

NT = (((1,), (1,)), ((), ()))
NN = (((1,), (0,)), ((), ()))


def dot(left, right, dims=NN):
    return lax.dot_general(left, right, dims, preferred_element_type=F32)


def rounded(value):
    return value.astype(BF16).astype(F32)


def split(value):
    high = rounded(value)
    rest = value - high
    mid = rounded(rest)
    return high, mid, rest - mid


def iota(shape, dim):
    return lax.broadcasted_iota(I32, shape, dim)


def pick(table, index):
    return jnp.take_along_axis(table, index, axis=1, mode="promise_in_bounds")


def look_up(table, index):
    row, lane = index >> 7, index & 127
    found = jnp.zeros(index.shape, table.dtype)
    for t in range(COLUMN_ROWS):
        piece = jnp.broadcast_to(table[t : t + 1], index.shape)
        found = jnp.where(row == t, pick(piece, lane), found)
    return found


def cross(a, b):
    return [
        a[1] * b[2] - a[2] * b[1],
        a[2] * b[0] - a[0] * b[2],
        a[0] * b[1] - a[1] * b[0],
    ]


def rows_of(value, low, top):
    return [value[c : c + 1] for c in range(low, top)]


def kernel(
    pos_hbm, flow_hbm, owner_hbm, slot_hbm, recv_hbm, order_hbm, count_hbm, out_ref,
    pos_ref, flow_ref, owner_ref, slot_ref, recv_ref, order_ref, count_ref,
    out1, in1, turned1, arrived, out2, in2, turned2, returned,
    targets, src_pos, src_tan, target, features, weights, right, own_sums, part_out, part_in,
    index, member,
    load_sem, ready, send_sem, phase_sem, rep_sem, pos_sem, tan_sem, part_sem,
):
    me = lax.axis_index("blk")
    rep = lax.axis_index("rep")
    plane = me // LINE
    place = me % LINE

    def on_line(k):
        return (place + k) % LINE

    def on_plane(k):
        return (plane + k) % PLANES

    def beside_x(k):
        return (plane + 4 * k) % PLANES

    def beside_y(k):
        return plane // 4 * 4 + (plane + k) % 4

    def on_rep(k):
        return (rep + k) % REPS

    def block(stop):
        return (me + stop + BLOCKS) % BLOCKS

    loads = [
        pltpu.make_async_copy(src, dst, load_sem.at[i])
        for i, (src, dst) in enumerate(
            [
                (pos_hbm, pos_ref), (owner_hbm, owner_ref), (slot_hbm, slot_ref),
                (recv_hbm, recv_ref), (order_hbm, order_ref), (count_hbm, count_ref),
                (flow_hbm, flow_ref),
            ]
        )
    ]

    barrier = pltpu.get_barrier_semaphore()

    def greet(blk, other):
        pl.semaphore_signal(barrier, inc=1, device_id=(blk, other), device_id_type=MESH)

    for k in LINE_ORDER:
        greet(plane * LINE + on_line(k), rep)
    for load in loads[:3]:
        load.start()
    for k in range(1, 4):
        greet(beside_x(k) * LINE + place, rep)
        greet(beside_y(k) * LINE + place, rep)
    for k in range(1, REPS):
        greet(me, on_rep(k))
    for stop in STOP_ORDER[1:]:

        @pl.when((place + stop < 0) | (place + stop >= LINE))
        def _():
            greet(block(stop), rep)

    for load in loads[3:]:
        load.start()
    for load in loads[:3]:
        load.wait()

    pos = pos_ref[...]
    owner = owner_ref[...]
    slot = slot_ref[...]
    owner_place, owner_plane = owner & (LINE - 1), owner >> 3
    member_row = (owner_plane >> 3) * 64 + owner_place * 8 + (owner_plane & 7)
    member[...] = jnp.where(iota((BLOCKS, PT), 0) == member_row, 1.0, 0.0).astype(BF16)
    message_row = owner_place * 4 + (owner_plane >> 2)
    to_row = jnp.where(iota((32, PT), 0) == message_row, 1.0, 0.0).astype(BF16)
    lane = iota((LANES, PT), 0)
    value = lane & 31
    component = jnp.where(value < CAP, 0, jnp.where(value < 2 * CAP, 1, 2))
    here = (lane >> 5) * 16 + value - component * CAP == (owner_plane & 3) * 16 + slot
    slotted = jnp.where(component == 0, pos[0:1], jnp.where(component == 1, pos[1:2], pos[2:3]))
    slotted = jnp.where(here, slotted, 0.0)
    outgoing = sum(dot(to_row, part.astype(BF16), NT) for part in split(slotted))
    out1[...] = outgoing.reshape(LINE, PLANES // 4, LANES)
    square = jnp.sum(pos * pos, axis=0, keepdims=True)
    pos_rows = jnp.concatenate([pos, square], axis=0)
    src_pos[BACK] = pos_rows
    targets[rep] = pos_rows

    def copy_to(src, dst, send, recv, blk, other):
        pltpu.make_async_remote_copy(
            src_ref=src, dst_ref=dst, send_sem=send_sem.at[send], recv_sem=recv,
            device_id=(blk, other), device_id_type=MESH,
        ).start()

    def send_line(src, dst, phase):
        for k in range(1, LINE) if phase == 0 else LINE_ORDER:
            late = jnp.where(LINE - k > place, LINE - k, LINE - 1 - k)
            there = late if phase == 0 else on_line(k)
            copy_to(src.at[there], dst.at[place], phase, phase_sem.at[phase],
                    plane * LINE + there, rep)

    def send_plane(src, dst, phase):
        for k in PLANE_ORDER:
            there = on_plane(k)
            copy_to(src.at[there], dst.at[plane], phase, phase_sem.at[phase],
                    there * LINE + place, rep)

    def await_here(dst, recv):
        pltpu.make_async_remote_copy(
            src_ref=dst, dst_ref=dst, send_sem=send_sem.at[0], recv_sem=recv,
            device_id=(me, rep), device_id_type=MESH,
        ).wait_recv()

    def await_sent(part, send):
        pltpu.make_async_remote_copy(
            src_ref=part, dst_ref=part, send_sem=send_sem.at[send], recv_sem=phase_sem.at[0],
            device_id=(me, rep), device_id_type=MESH,
        ).wait_send()

    ones = jnp.ones((1, PT), F32)
    none = jnp.zeros((3, PT), F32)
    one_row = jnp.concatenate([ones, none], axis=0)

    def aim(other):
        rows = targets[other]
        wanted = jnp.concatenate(
            [-2.0 * rows[0:3], ones, rows[3:4] + CORE_SQUARED, none], axis=0
        )
        th, tm, tl = split(wanted)
        target[other] = jnp.concatenate([th, th, tm, tm, th, tl, tl, tm], axis=0).astype(BF16)

    def describe(stop):
        sh, sm, sl = split(jnp.concatenate([src_pos[stop + BACK], one_row], axis=0))
        rows = jnp.concatenate(
            [sh, sm, sh, sm, sl, sh, sm, sl, jnp.zeros((LANES - FEATURES, PT), F32)], axis=0
        )
        features[...] = rows.T[:, :FEATURES].astype(BF16)

    def weigh(low, top):
        def one(unit, carry):
            i = unit // REPS
            stop = (i % 2) * ((i + 1) // 2) - (1 - i % 2) * (i // 2)
            other = on_rep(unit % REPS)

            @pl.when((unit % REPS == 0) & (i > 0))
            def _():
                await_here(src_pos.at[stop + BACK], pos_sem.at[stop + BACK])

            @pl.when(unit % REPS == 0)
            def _():
                describe(stop)

            for half in range(PT // 256):
                low, top = half * 256, half * 256 + 256
                root = lax.rsqrt(dot(features[...], target[other, :, low:top]))
                weight = root * root * root
                high = weight.astype(BF16)
                weights[other, stop + BACK, :PT, low:top] = high
                weights[other, stop + BACK, PT:, low:top] = (
                    weight - high.astype(F32)
                ).astype(BF16)
            return carry

        lax.fori_loop(low, top, one, 0)

    across = jnp.where(place < STOPS // 2, STOPS // 2 - place, place - STOPS // 2)
    pl.semaphore_wait(barrier, (LINE - 1) + 3 + 3 + (REPS - 1) + across)

    send_line(out1, in1, 0)
    for k in range(1, 4):
        pl.semaphore_signal(
            ready, inc=1, device_id=(beside_x(k) * LINE + place, rep), device_id_type=MESH
        )
    for k in range(1, REPS):
        copy_to(targets.at[rep], targets.at[rep], 4, rep_sem.at[rep], me, on_rep(k))
    in1[place] = out1[place]

    for load in loads[3:]:
        load.wait()
    lane = iota((16, LANES), 1)
    spot = (((lane & 31) >> 1) * LINE + (lane >> 5) * 2 + (lane & 1)) * CAP + iota((16, LANES), 0)
    column = jnp.where(iota((16, LANES), 0) < CAP, look_up(recv_ref[...], spot), -1)
    column_row, column_lane = column >> 7, column & 127
    holder = iota((16, LANES), 1).astype(F32)
    inverse = jnp.zeros((32, LANES), F32)
    for s in range(CAP):
        hit = column_row[s : s + 1] == iota((16, LANES), 0)
        left = jnp.concatenate(
            [jnp.where(hit, holder, 0.0), jnp.where(hit, float(s), 0.0)], axis=0
        ).astype(BF16)
        lane_hit = column_lane[s : s + 1] == iota((LANES, LANES), 0)
        inverse = inverse + dot(left, jnp.where(lane_hit, 1.0, 0.0).astype(BF16), NT)
    inverse = (inverse[16:] * float(LANES) + inverse[:16]).astype(I32)
    at = jnp.maximum(column, 0)
    ring = look_up(order_ref[...] + (count_ref[...] << 11), at)
    order, count = ring & 2047, ring >> 11

    def neighbour(offset):
        moved = order + offset
        moved = jnp.where(moved < 0, moved + count, jnp.where(moved >= count, moved - count, moved))
        there = jnp.clip(at - order + moved, 0, COLUMN_ROWS * LANES - 1)
        return look_up(inverse, there)

    ahead1, ahead2, behind1, behind2 = (neighbour(k) for k in (1, 2, -1, -2))
    for i, table in enumerate((ahead1, ahead2, behind1, behind2)):
        index[i] = table
    aim(rep)
    weigh(0, 1)
    await_here(in1.at[pl.ds(0, LINE - 1)], phase_sem.at[0])
    place_bits, plane_bits = iota((LINE, LANES), 0) >> 1, iota((LINE, LANES), 1) >> 5
    for q in range(PLANES // 4):
        rows = in1[:, q, :]
        down = pltpu.roll(pltpu.roll(rows, LINE - 2, 0), 32, 1)
        up = pltpu.roll(pltpu.roll(rows, 2, 0), LANES - 32, 1)
        rows = jnp.where(
            (place_bits & 1) == (plane_bits & 1), rows, jnp.where((place_bits & 1) == 0, down, up)
        )
        far_rows = pltpu.roll(pltpu.roll(rows, 4, 0), 64, 1)
        rows = jnp.where((place_bits >> 1) == (plane_bits >> 1), rows, far_rows)
        for p in range(4):
            turned1[4 * q + p] = rows[2 * p : 2 * p + 2]
    pl.semaphore_wait(ready, 3)
    send_plane(turned1, arrived, 1)
    arrived[plane] = turned1[plane]
    for stop in STOP_ORDER[1:]:
        copy_to(src_pos.at[BACK], src_pos.at[stop + BACK], 5, pos_sem.at[stop + BACK],
                block(-stop), rep)

    for k in range(1, REPS):
        await_here(targets.at[on_rep(k)], rep_sem.at[on_rep(k)])
        aim(on_rep(k))
    weigh(1, 4)

    await_here(arrived.at[pl.ds(0, PLANES - 1)], phase_sem.at[1])
    rows = arrived[...].reshape(2 * PLANES, LANES)
    tables = jnp.concatenate(
        [rows] + [pltpu.roll(rows, LANES - 32 * i, 1) for i in range(1, 4)], axis=0
    ).T
    moved = []
    for i in range(4):
        at_row, at_lane = index[i] >> 7, index[i] & 127
        found = [jnp.zeros((16, LANES), F32) for _ in range(3)]
        for t in range(CAP):
            hit = at_row == t
            for c in range(3):
                table = jnp.broadcast_to(tables[c * CAP + t : c * CAP + t + 1], (16, LANES))
                found[c] = jnp.where(hit, pick(table, at_lane), found[c])
        moved.append(found)
    results = [[], []]
    for c in range(3):
        a1, a2, b1, b2 = (found[c][:CAP] for found in moved)
        center = tables[c * CAP : (c + 1) * CAP]
        results[0].append((8.0 * (a1 - b1) - (a2 - b2)) / 12.0)
        results[1].append((16.0 * (a1 + b1) - (a2 + b2) - 30.0 * center) / 12.0)
    values = jnp.concatenate(
        results[0] + results[1] + [jnp.zeros((64 - 6 * CAP, LANES), F32)], axis=0
    )
    values = jnp.concatenate([values, pltpu.roll(values, 64, 1)], axis=0).T
    for i in range(2):
        out2[:, i] = values[32 * i : 32 * i + 32].reshape(PLANES, 2, LANES)

    send_plane(out2, in2, 2)
    in2[plane] = out2[plane]
    weigh(4, 16)
    await_here(in2.at[pl.ds(0, PLANES - 1)], phase_sem.at[2])
    left_half = iota((8, LANES), 1) < 64
    for i in range(2):
        for j in range(2):
            rows = in2[:, i, j, :]
            a, b = rows[:8], rows[8:]
            turned2[2 * i + j] = jnp.where(left_half, a, pltpu.roll(b, 64, 1))
            turned2[4 + 2 * i + j] = jnp.where(left_half, pltpu.roll(a, 64, 1), b)
    send_line(turned2, returned, 3)
    returned[place] = turned2[place]
    weigh(16, 28)
    await_here(returned.at[pl.ds(0, LINE - 1)], phase_sem.at[3])
    rows = returned[...].reshape(64, LANES)
    back = jnp.concatenate([rows, pltpu.roll(rows, 64, 1)], axis=0).T[:64]
    is_owner = member[...]
    spread = sum(dot(part.astype(BF16), is_owner) for part in split(back))
    derived = []
    for q in range(6):
        chosen = jnp.where(iota((CAP, PT), 0) == slot, spread[q * CAP : (q + 1) * CAP], 0.0)
        derived.append(jnp.sum(chosen, axis=0, keepdims=True))

    src_tan[BACK] = jnp.concatenate(derived[0:3] + [jnp.zeros((1, PT), F32)], axis=0)
    for stop in STOP_ORDER[1:]:
        copy_to(src_tan.at[BACK], src_tan.at[stop + BACK], 6, tan_sem.at[stop + BACK],
                block(-stop), rep)
    weigh(28, SOURCES)

    def prepare(stop):
        p, t = rows_of(src_pos[stop], 0, 3), rows_of(src_tan[stop], 0, 3)
        h, m, l = split(jnp.concatenate(t + cross(t, p) + [jnp.zeros((2, PT), F32)], axis=0))
        rows = jnp.concatenate([h, m, l, jnp.zeros((8, PT), F32)], axis=0).astype(BF16)
        rows = jnp.concatenate([rows, rows], axis=1)
        right[stop] = rows
        return rows

    prepare(BACK)
    for k in range(REPS):
        own_sums[k] = dot(right[BACK], weights[k, BACK])
    await_sent(out1.at[pl.ds(0, LINE - 1)], 0)
    await_sent(turned1.at[pl.ds(0, PLANES - 1)], 1)
    await_sent(out2.at[pl.ds(0, PLANES - 1)], 2)
    await_sent(turned2.at[pl.ds(0, LINE - 1)], 3)
    await_sent(targets.at[pl.ds(0, REPS - 1)], 4)
    await_sent(src_pos.at[pl.ds(0, STOPS - 1)], 5)
    for stop in STOP_ORDER[1:]:
        await_here(src_tan.at[stop + BACK], tan_sem.at[stop + BACK])

    def finish_sums(i, other, parts):
        parts = parts[0:8] + parts[8:16] + parts[16:24]
        far = cross(rows_of(parts, 0, 3), rows_of(targets[other], 0, 3))
        part_out[i] = jnp.concatenate(
            [far[c] - parts[3 + c : 4 + c] for c in range(3)] + [jnp.zeros((1, PT), F32)], axis=0
        )

    def send_sums(i, other):
        copy_to(part_out.at[i], part_in.at[i], 7, part_sem.at[i], me, other)

    other = (rep + 2) % REPS
    parts = own_sums[other]
    for stop in STOP_ORDER[:0:-1]:
        parts = parts + dot(prepare(stop + BACK), weights[other, stop + BACK])
    finish_sums(0, other, parts)
    send_sums(0, other)

    def sums_of(i, carry):
        other = jnp.where(
            i == 1, REPS - 1 - rep, jnp.where(i == 2, rep + 1 - 2 * (rep % 2), rep)
        )
        parts = own_sums[other]
        for stop in STOP_ORDER[:0:-1]:
            parts = parts + dot(right[stop + BACK], weights[other, stop + BACK])
        finish_sums(i, other, parts)

        @pl.when(i < REPS - 1)
        def _():
            send_sums(i, other)

        return carry

    lax.fori_loop(1, REPS, sums_of, 0)
    for i in range(REPS - 1):
        await_here(part_in.at[i], part_sem.at[i])
    others = part_out[REPS - 1] + part_in[0] + part_in[1] + part_in[2]
    far = [others[c : c + 1] for c in range(3)]

    tangent, curvature = derived[0:3], derived[3:6]
    speed = jnp.maximum(
        tangent[0] * tangent[0] + tangent[1] * tangent[1] + tangent[2] * tangent[2], SPEED_FLOOR
    )
    per_speed = 1.0 / jnp.sqrt(speed)
    scale = LOCAL_BETA * per_speed / speed
    local = cross(tangent, curvature)
    superfluid = [scale * local[c] + BIOT_SCALE * far[c] for c in range(3)]
    unit = [tangent[c] * per_speed for c in range(3)]
    once = cross(unit, [flow_ref[c : c + 1, :] - superfluid[c] for c in range(3)])
    twice = cross(unit, once)
    for c in range(3):
        out_ref[c : c + 1, :] = (
            superfluid[c] + FRICTION_ALPHA * once[c] - FRICTION_PRIME * twice[c]
        )

    await_sent(src_tan.at[pl.ds(0, STOPS - 1)], 6)
    await_sent(part_out.at[pl.ds(0, REPS - 1)], 7)


def shards(positions, normal_flow, send_owner, send_slot, recv_index, loop_pos, loop_len):
    dma = pltpu.SemaphoreType.DMA
    first = pltpu.VMEM((LINE, PLANES // 4, LANES), F32)
    second = pltpu.VMEM((PLANES, 2, LANES), F32)
    third = pltpu.VMEM((PLANES, 2, 2, LANES), F32)
    fourth = pltpu.VMEM((LINE, 8, LANES), F32)
    points = pltpu.VMEM((3, PT), F32)
    point_index = pltpu.VMEM((1, PT), I32)
    columns = pltpu.VMEM((COLUMN_ROWS, LANES), I32)
    return pl.pallas_call(
        kernel,
        out_shape=jax.ShapeDtypeStruct((3, PT), F32),
        in_specs=[pl.BlockSpec(memory_space=pltpu.HBM)] * 7,
        out_specs=pl.BlockSpec(memory_space=pltpu.VMEM),
        scratch_shapes=[
            points, points, point_index, point_index, columns, columns, columns,
            first, first, second, second, third, third, fourth, fourth,
            pltpu.VMEM((REPS, 4, PT), F32),
            pltpu.VMEM((STOPS, 4, PT), F32),
            pltpu.VMEM((STOPS, 4, PT), F32),
            pltpu.VMEM((REPS, FEATURES, PT), BF16),
            pltpu.VMEM((PT, FEATURES), BF16),
            pltpu.VMEM((REPS, STOPS, 2 * PT, PT), BF16),
            pltpu.VMEM((STOPS, 32, 2 * PT), BF16),
            pltpu.VMEM((REPS, 32, PT), F32),
            pltpu.VMEM((REPS, 4, PT), F32),
            pltpu.VMEM((REPS, 4, PT), F32),
            pltpu.VMEM((4, 16, LANES), I32),
            pltpu.VMEM((BLOCKS, PT), BF16),
            dma((7,)), pltpu.SemaphoreType.REGULAR, dma((8,)), dma((4,)), dma((REPS,)), dma((STOPS,)), dma((STOPS,)),
            dma((REPS,)),
        ],
        compiler_params=pltpu.CompilerParams(
            collective_id=0, has_side_effects=True, vmem_limit_bytes=48 * 1024 * 1024
        ),
        cost_estimate=pl.CostEstimate(
            flops=2 * PT * SOURCES * PT * 128, bytes_accessed=1 << 20,
            transcendentals=PT * SOURCES * PT,
        ),
    )(
        *(
            pltpu.with_memory_space_constraint(operand, pltpu.HBM)
            for operand in (
                positions,
                normal_flow,
                send_owner.reshape(1, PT),
                send_slot.reshape(1, PT),
                recv_index.reshape(CAP, BLOCKS),
                loop_pos.reshape(COLUMN_ROWS, LANES),
                loop_len.reshape(COLUMN_ROWS, LANES),
            )
        )
    )


def solution(mesh):
    both = P(("blk", "rep"))
    wide = P(None, ("blk", "rep"))
    return jax.shard_map(
        shards,
        mesh=mesh,
        in_specs=(wide, wide, both, both, both, both, both),
        out_specs=wide,
        check_vma=False,
    )
```

```python
import functools

import jax
import jax.numpy as jnp
from jax import lax
from jax.experimental import pallas as pl
from jax.experimental.pallas import tpu as pltpu
from jax.sharding import PartitionSpec as P

LOCAL_BETA = 0.3
FRICTION_ALPHA = 0.21
FRICTION_PRIME = 0.06
BIOT_SCALE = 0.01
CORE_SQUARED = 0.25
SPEED_FLOOR = 1.0

BLOCKS = 128
LINE = 8
PLANES = BLOCKS // LINE
REPS = 4
STOPS = 8
BACK = STOPS // 2 - 1
SOURCES = STOPS * REPS
PT = 512
CAP = 10
LANES = 128
COLUMN_ROWS = 10

FEATURES = 64
STOP_ORDER = (0, 4, 3, -3, 2, -2, 1, -1)
LINE_ORDER = (4, 3, 5, 2, 6, 1, 7)
PLANE_ORDER = (10, 9, 11, 6, 14, 7, 13, 2, 8, 5, 15, 3, 1, 4, 12)

MESH = pl.DeviceIdType.MESH
F32 = jnp.float32
BF16 = jnp.bfloat16
I32 = jnp.int32

NT = (((1,), (1,)), ((), ()))
NN = (((1,), (0,)), ((), ()))


def dot(left, right, dims=NN):
    return lax.dot_general(left, right, dims, preferred_element_type=F32)


def rounded(value):
    return value.astype(BF16).astype(F32)


def split(value):
    high = rounded(value)
    rest = value - high
    mid = rounded(rest)
    return high, mid, rest - mid


def iota(shape, dim):
    return lax.broadcasted_iota(I32, shape, dim)


def pick(table, index):
    return jnp.take_along_axis(table, index, axis=1, mode="promise_in_bounds")


def look_up(table, index):
    row, lane = index >> 7, index & 127
    found = jnp.zeros(index.shape, table.dtype)
    for t in range(COLUMN_ROWS):
        piece = jnp.broadcast_to(table[t : t + 1], index.shape)
        found = jnp.where(row == t, pick(piece, lane), found)
    return found


def cross(a, b):
    return [
        a[1] * b[2] - a[2] * b[1],
        a[2] * b[0] - a[0] * b[2],
        a[0] * b[1] - a[1] * b[0],
    ]


def rows_of(value, low, top):
    return [value[c : c + 1] for c in range(low, top)]


def kernel(
    pos_hbm, flow_hbm, owner_hbm, slot_hbm, recv_hbm, order_hbm, count_hbm, out_ref,
    pos_ref, flow_ref, owner_ref, slot_ref, recv_ref, order_ref, count_ref,
    out1, in1, turned1, arrived, out2, in2, turned2, returned,
    targets, src_pos, src_tan, target, features, weights, right, own_sums, part_out, part_in,
    index, member,
    load_sem, ready, send_sem, phase_sem, rep_sem, pos_sem, tan_sem, part_sem,
):
    me = lax.axis_index("blk")
    rep = lax.axis_index("rep")
    plane = me // LINE
    place = me % LINE

    def on_line(k):
        return (place + k) % LINE

    def on_plane(k):
        return (plane + k) % PLANES

    def beside_x(k):
        return (plane + 4 * k) % PLANES

    def beside_y(k):
        return plane // 4 * 4 + (plane + k) % 4

    def on_rep(k):
        return (rep + k) % REPS

    def block(stop):
        return (me + stop + BLOCKS) % BLOCKS

    loads = [
        pltpu.make_async_copy(src, dst, load_sem.at[i])
        for i, (src, dst) in enumerate(
            [
                (pos_hbm, pos_ref), (owner_hbm, owner_ref), (slot_hbm, slot_ref),
                (recv_hbm, recv_ref), (order_hbm, order_ref), (count_hbm, count_ref),
                (flow_hbm, flow_ref),
            ]
        )
    ]
    for load in loads[:3]:
        load.start()

    barrier = pltpu.get_barrier_semaphore()

    def greet(blk, other):
        pl.semaphore_signal(barrier, inc=1, device_id=(blk, other), device_id_type=MESH)

    for k in LINE_ORDER:
        greet(plane * LINE + on_line(k), rep)
    for k in range(1, 4):
        greet(beside_x(k) * LINE + place, rep)
        greet(beside_y(k) * LINE + place, rep)
    for k in range(1, REPS):
        greet(me, on_rep(k))
    for stop in STOP_ORDER[1:]:

        @pl.when((place + stop < 0) | (place + stop >= LINE))
        def _():
            greet(block(stop), rep)

    for load in loads[3:]:
        load.start()
    for load in loads[:3]:
        load.wait()

    pos = pos_ref[...]
    owner = owner_ref[...]
    slot = slot_ref[...]
    owner_place, owner_plane = owner & (LINE - 1), owner >> 3
    member_row = (owner_plane >> 3) * 64 + owner_place * 8 + (owner_plane & 7)
    member[...] = jnp.where(iota((BLOCKS, PT), 0) == member_row, 1.0, 0.0).astype(BF16)
    message_row = owner_place * 4 + (owner_plane >> 2)
    to_row = jnp.where(iota((32, PT), 0) == message_row, 1.0, 0.0).astype(BF16)
    lane = iota((LANES, PT), 0)
    value = lane & 31
    component = jnp.where(value < CAP, 0, jnp.where(value < 2 * CAP, 1, 2))
    here = (lane >> 5) * 16 + value - component * CAP == (owner_plane & 3) * 16 + slot
    slotted = jnp.where(component == 0, pos[0:1], jnp.where(component == 1, pos[1:2], pos[2:3]))
    slotted = jnp.where(here, slotted, 0.0)
    outgoing = sum(dot(to_row, part.astype(BF16), NT) for part in split(slotted))
    out1[...] = outgoing.reshape(LINE, PLANES // 4, LANES)
    square = jnp.sum(pos * pos, axis=0, keepdims=True)
    pos_rows = jnp.concatenate([pos, square], axis=0)
    src_pos[BACK] = pos_rows
    targets[rep] = pos_rows

    def copy_to(src, dst, send, recv, blk, other):
        pltpu.make_async_remote_copy(
            src_ref=src, dst_ref=dst, send_sem=send_sem.at[send], recv_sem=recv,
            device_id=(blk, other), device_id_type=MESH,
        ).start()

    def send_line(src, dst, phase):
        for k in LINE_ORDER:
            there = on_line(k)
            copy_to(src.at[there], dst.at[place], phase, phase_sem.at[phase],
                    plane * LINE + there, rep)

    def send_plane(src, dst, phase):
        for k in PLANE_ORDER:
            there = on_plane(k)
            copy_to(src.at[there], dst.at[plane], phase, phase_sem.at[phase],
                    there * LINE + place, rep)

    def await_here(dst, recv):
        pltpu.make_async_remote_copy(
            src_ref=dst, dst_ref=dst, send_sem=send_sem.at[0], recv_sem=recv,
            device_id=(me, rep), device_id_type=MESH,
        ).wait_recv()

    def await_sent(part, send):
        pltpu.make_async_remote_copy(
            src_ref=part, dst_ref=part, send_sem=send_sem.at[send], recv_sem=phase_sem.at[0],
            device_id=(me, rep), device_id_type=MESH,
        ).wait_send()

    ones = jnp.ones((1, PT), F32)
    none = jnp.zeros((3, PT), F32)
    one_row = jnp.concatenate([ones, none], axis=0)

    def aim(other):
        rows = targets[other]
        wanted = jnp.concatenate(
            [-2.0 * rows[0:3], ones, rows[3:4] + CORE_SQUARED, none], axis=0
        )
        th, tm, tl = split(wanted)
        target[other] = jnp.concatenate([th, th, tm, tm, th, tl, tl, tm], axis=0).astype(BF16)

    def describe(stop):
        sh, sm, sl = split(jnp.concatenate([src_pos[stop + BACK], one_row], axis=0))
        rows = jnp.concatenate(
            [sh, sm, sh, sm, sl, sh, sm, sl, jnp.zeros((LANES - FEATURES, PT), F32)], axis=0
        )
        features[...] = rows.T[:, :FEATURES].astype(BF16)

    def weigh(low, top):
        def one(unit, carry):
            i = unit // REPS
            stop = (i % 2) * ((i + 1) // 2) - (1 - i % 2) * (i // 2)
            other = on_rep(unit % REPS)

            @pl.when((unit % REPS == 0) & (i > 0))
            def _():
                await_here(src_pos.at[stop + BACK], pos_sem.at[stop + BACK])

            @pl.when(unit % REPS == 0)
            def _():
                describe(stop)

            for half in range(PT // 256):
                low, top = half * 256, half * 256 + 256
                root = lax.rsqrt(dot(features[...], target[other, :, low:top]))
                weight = root * root * root
                high = weight.astype(BF16)
                weights[other, stop + BACK, :PT, low:top] = high
                weights[other, stop + BACK, PT:, low:top] = (
                    weight - high.astype(F32)
                ).astype(BF16)
            return carry

        lax.fori_loop(low, top, one, 0)

    across = jnp.where(place < STOPS // 2, STOPS // 2 - place, place - STOPS // 2)
    pl.semaphore_wait(barrier, (LINE - 1) + 3 + 3 + (REPS - 1) + across)

    send_line(out1, in1, 0)
    for k in range(1, 4):
        pl.semaphore_signal(
            ready, inc=1, device_id=(beside_x(k) * LINE + place, rep), device_id_type=MESH
        )
    for k in range(1, REPS):
        copy_to(targets.at[rep], targets.at[rep], 4, rep_sem.at[rep], me, on_rep(k))
    in1[place] = out1[place]

    for load in loads[3:]:
        load.wait()
    lane = iota((16, LANES), 1)
    spot = (((lane & 31) >> 1) * LINE + (lane >> 5) * 2 + (lane & 1)) * CAP + iota((16, LANES), 0)
    column = jnp.where(iota((16, LANES), 0) < CAP, look_up(recv_ref[...], spot), -1)
    column_row, column_lane = column >> 7, column & 127
    holder = iota((16, LANES), 1).astype(F32)
    inverse = jnp.zeros((32, LANES), F32)
    for s in range(CAP):
        hit = column_row[s : s + 1] == iota((16, LANES), 0)
        left = jnp.concatenate(
            [jnp.where(hit, holder, 0.0), jnp.where(hit, float(s), 0.0)], axis=0
        ).astype(BF16)
        lane_hit = column_lane[s : s + 1] == iota((LANES, LANES), 0)
        inverse = inverse + dot(left, jnp.where(lane_hit, 1.0, 0.0).astype(BF16), NT)
    inverse = (inverse[16:] * float(LANES) + inverse[:16]).astype(I32)
    at = jnp.maximum(column, 0)
    ring = look_up(order_ref[...] + (count_ref[...] << 11), at)
    order, count = ring & 2047, ring >> 11

    def neighbour(offset):
        moved = order + offset
        moved = jnp.where(moved < 0, moved + count, jnp.where(moved >= count, moved - count, moved))
        there = jnp.clip(at - order + moved, 0, COLUMN_ROWS * LANES - 1)
        return look_up(inverse, there)

    ahead1, ahead2, behind1, behind2 = (neighbour(k) for k in (1, 2, -1, -2))
    for i, table in enumerate((ahead1, ahead2, behind1, behind2)):
        index[i] = table
    aim(rep)
    weigh(0, 1)
    await_here(in1.at[pl.ds(0, LINE - 1)], phase_sem.at[0])
    place_bits, plane_bits = iota((LINE, LANES), 0) >> 1, iota((LINE, LANES), 1) >> 5
    for q in range(PLANES // 4):
        rows = in1[:, q, :]
        down = pltpu.roll(pltpu.roll(rows, LINE - 2, 0), 32, 1)
        up = pltpu.roll(pltpu.roll(rows, 2, 0), LANES - 32, 1)
        rows = jnp.where(
            (place_bits & 1) == (plane_bits & 1), rows, jnp.where((place_bits & 1) == 0, down, up)
        )
        far_rows = pltpu.roll(pltpu.roll(rows, 4, 0), 64, 1)
        rows = jnp.where((place_bits >> 1) == (plane_bits >> 1), rows, far_rows)
        for p in range(4):
            turned1[4 * q + p] = rows[2 * p : 2 * p + 2]
    pl.semaphore_wait(ready, 3)
    send_plane(turned1, arrived, 1)
    arrived[plane] = turned1[plane]
    for stop in STOP_ORDER[1:]:
        copy_to(src_pos.at[BACK], src_pos.at[stop + BACK], 5, pos_sem.at[stop + BACK],
                block(-stop), rep)

    for k in range(1, REPS):
        await_here(targets.at[on_rep(k)], rep_sem.at[on_rep(k)])
        aim(on_rep(k))
    weigh(1, 4)

    await_here(arrived.at[pl.ds(0, PLANES - 1)], phase_sem.at[1])
    rows = arrived[...].reshape(2 * PLANES, LANES)
    tables = jnp.concatenate(
        [rows] + [pltpu.roll(rows, LANES - 32 * i, 1) for i in range(1, 4)], axis=0
    ).T
    moved = []
    for i in range(4):
        at_row, at_lane = index[i] >> 7, index[i] & 127
        found = [jnp.zeros((16, LANES), F32) for _ in range(3)]
        for t in range(CAP):
            hit = at_row == t
            for c in range(3):
                table = jnp.broadcast_to(tables[c * CAP + t : c * CAP + t + 1], (16, LANES))
                found[c] = jnp.where(hit, pick(table, at_lane), found[c])
        moved.append(found)
    results = [[], []]
    for c in range(3):
        a1, a2, b1, b2 = (found[c][:CAP] for found in moved)
        center = tables[c * CAP : (c + 1) * CAP]
        results[0].append((8.0 * (a1 - b1) - (a2 - b2)) / 12.0)
        results[1].append((16.0 * (a1 + b1) - (a2 + b2) - 30.0 * center) / 12.0)
    values = jnp.concatenate(
        results[0] + results[1] + [jnp.zeros((64 - 6 * CAP, LANES), F32)], axis=0
    )
    values = jnp.concatenate([values, pltpu.roll(values, 64, 1)], axis=0).T
    for i in range(2):
        out2[:, i] = values[32 * i : 32 * i + 32].reshape(PLANES, 2, LANES)

    send_plane(out2, in2, 2)
    in2[plane] = out2[plane]
    weigh(4, 10)
    await_here(in2.at[pl.ds(0, PLANES - 1)], phase_sem.at[2])
    left_half = iota((8, LANES), 1) < 64
    for i in range(2):
        for j in range(2):
            rows = in2[:, i, j, :]
            a, b = rows[:8], rows[8:]
            turned2[2 * i + j] = jnp.where(left_half, a, pltpu.roll(b, 64, 1))
            turned2[4 + 2 * i + j] = jnp.where(left_half, pltpu.roll(a, 64, 1), b)
    send_line(turned2, returned, 3)
    returned[place] = turned2[place]
    weigh(10, 16)
    await_here(returned.at[pl.ds(0, LINE - 1)], phase_sem.at[3])
    rows = returned[...].reshape(64, LANES)
    back = jnp.concatenate([rows, pltpu.roll(rows, 64, 1)], axis=0).T[:64]
    is_owner = member[...]
    spread = sum(dot(part.astype(BF16), is_owner) for part in split(back))
    derived = []
    for q in range(6):
        chosen = jnp.where(iota((CAP, PT), 0) == slot, spread[q * CAP : (q + 1) * CAP], 0.0)
        derived.append(jnp.sum(chosen, axis=0, keepdims=True))

    src_tan[BACK] = jnp.concatenate(derived[0:3] + [jnp.zeros((1, PT), F32)], axis=0)
    for stop in STOP_ORDER[1:]:
        copy_to(src_tan.at[BACK], src_tan.at[stop + BACK], 6, tan_sem.at[stop + BACK],
                block(-stop), rep)
    weigh(16, SOURCES)

    def prepare(stop):
        p, t = rows_of(src_pos[stop], 0, 3), rows_of(src_tan[stop], 0, 3)
        h, m, l = split(jnp.concatenate(t + cross(t, p) + [jnp.zeros((2, PT), F32)], axis=0))
        rows = jnp.concatenate([h, m, l, jnp.zeros((8, PT), F32)], axis=0).astype(BF16)
        rows = jnp.concatenate([rows, rows], axis=1)
        right[stop] = rows
        return rows

    prepare(BACK)
    for k in range(REPS):
        own_sums[k] = dot(right[BACK], weights[k, BACK])
    for stop in STOP_ORDER[1:]:
        await_here(src_tan.at[stop + BACK], tan_sem.at[stop + BACK])

    def finish_sums(i, other, parts):
        parts = parts[0:8] + parts[8:16] + parts[16:24]
        far = cross(rows_of(parts, 0, 3), rows_of(targets[other], 0, 3))
        part_out[i] = jnp.concatenate(
            [far[c] - parts[3 + c : 4 + c] for c in range(3)] + [jnp.zeros((1, PT), F32)], axis=0
        )

    def send_sums(i, other):
        copy_to(part_out.at[i], part_in.at[i], 7, part_sem.at[i], me, other)

    other = (rep + 2) % REPS
    parts = own_sums[other]
    for stop in STOP_ORDER[:0:-1]:
        parts = parts + dot(prepare(stop + BACK), weights[other, stop + BACK])
    finish_sums(0, other, parts)
    send_sums(0, other)

    def sums_of(i, carry):
        other = jnp.where(
            i == 1, REPS - 1 - rep, jnp.where(i == 2, rep + 1 - 2 * (rep % 2), rep)
        )
        parts = own_sums[other]
        for stop in STOP_ORDER[:0:-1]:
            parts = parts + dot(right[stop + BACK], weights[other, stop + BACK])
        finish_sums(i, other, parts)

        @pl.when(i < REPS - 1)
        def _():
            send_sums(i, other)

        return carry

    lax.fori_loop(1, REPS, sums_of, 0)
    for i in range(REPS - 1):
        await_here(part_in.at[i], part_sem.at[i])
    others = part_out[REPS - 1] + part_in[0] + part_in[1] + part_in[2]
    far = [others[c : c + 1] for c in range(3)]

    tangent, curvature = derived[0:3], derived[3:6]
    speed = jnp.maximum(
        tangent[0] * tangent[0] + tangent[1] * tangent[1] + tangent[2] * tangent[2], SPEED_FLOOR
    )
    per_speed = 1.0 / jnp.sqrt(speed)
    scale = LOCAL_BETA * per_speed / speed
    local = cross(tangent, curvature)
    superfluid = [scale * local[c] + BIOT_SCALE * far[c] for c in range(3)]
    unit = [tangent[c] * per_speed for c in range(3)]
    once = cross(unit, [flow_ref[c : c + 1, :] - superfluid[c] for c in range(3)])
    twice = cross(unit, once)
    for c in range(3):
        out_ref[c : c + 1, :] = (
            superfluid[c] + FRICTION_ALPHA * once[c] - FRICTION_PRIME * twice[c]
        )

    await_sent(out1.at[pl.ds(0, LINE - 1)], 0)
    await_sent(turned1.at[pl.ds(0, PLANES - 1)], 1)
    await_sent(out2.at[pl.ds(0, PLANES - 1)], 2)
    await_sent(turned2.at[pl.ds(0, LINE - 1)], 3)
    await_sent(targets.at[pl.ds(0, REPS - 1)], 4)
    await_sent(src_pos.at[pl.ds(0, STOPS - 1)], 5)
    await_sent(src_tan.at[pl.ds(0, STOPS - 1)], 6)
    await_sent(part_out.at[pl.ds(0, REPS - 1)], 7)


def shards(positions, normal_flow, send_owner, send_slot, recv_index, loop_pos, loop_len):
    dma = pltpu.SemaphoreType.DMA
    first = pltpu.VMEM((LINE, PLANES // 4, LANES), F32)
    second = pltpu.VMEM((PLANES, 2, LANES), F32)
    third = pltpu.VMEM((PLANES, 2, 2, LANES), F32)
    fourth = pltpu.VMEM((LINE, 8, LANES), F32)
    points = pltpu.VMEM((3, PT), F32)
    point_index = pltpu.VMEM((1, PT), I32)
    columns = pltpu.VMEM((COLUMN_ROWS, LANES), I32)
    return pl.pallas_call(
        kernel,
        out_shape=jax.ShapeDtypeStruct((3, PT), F32),
        in_specs=[pl.BlockSpec(memory_space=pltpu.HBM)] * 7,
        out_specs=pl.BlockSpec(memory_space=pltpu.VMEM),
        scratch_shapes=[
            points, points, point_index, point_index, columns, columns, columns,
            first, first, second, second, third, third, fourth, fourth,
            pltpu.VMEM((REPS, 4, PT), F32),
            pltpu.VMEM((STOPS, 4, PT), F32),
            pltpu.VMEM((STOPS, 4, PT), F32),
            pltpu.VMEM((REPS, FEATURES, PT), BF16),
            pltpu.VMEM((PT, FEATURES), BF16),
            pltpu.VMEM((REPS, STOPS, 2 * PT, PT), BF16),
            pltpu.VMEM((STOPS, 32, 2 * PT), BF16),
            pltpu.VMEM((REPS, 32, PT), F32),
            pltpu.VMEM((REPS, 4, PT), F32),
            pltpu.VMEM((REPS, 4, PT), F32),
            pltpu.VMEM((4, 16, LANES), I32),
            pltpu.VMEM((BLOCKS, PT), BF16),
            dma((7,)), pltpu.SemaphoreType.REGULAR, dma((8,)), dma((4,)), dma((REPS,)), dma((STOPS,)), dma((STOPS,)),
            dma((REPS,)),
        ],
        compiler_params=pltpu.CompilerParams(
            collective_id=0, has_side_effects=True, vmem_limit_bytes=48 * 1024 * 1024
        ),
        cost_estimate=pl.CostEstimate(
            flops=2 * PT * SOURCES * PT * 128, bytes_accessed=1 << 20,
            transcendentals=PT * SOURCES * PT,
        ),
    )(
        *(
            pltpu.with_memory_space_constraint(operand, pltpu.HBM)
            for operand in (
                positions,
                normal_flow,
                send_owner.reshape(1, PT),
                send_slot.reshape(1, PT),
                recv_index.reshape(CAP, BLOCKS),
                loop_pos.reshape(COLUMN_ROWS, LANES),
                loop_len.reshape(COLUMN_ROWS, LANES),
            )
        )
    )


def solution(mesh):
    both = P(("blk", "rep"))
    wide = P(None, ("blk", "rep"))
    return jax.shard_map(
        shards,
        mesh=mesh,
        in_specs=(wide, wide, both, both, both, both, both),
        out_specs=wide,
        check_vma=False,
    )
```
